128 devices in a mesh: leaf: 32 (over z, y, core), tm: 4 (over x).
Axes of the slice: x: 4, y: 4, z: 4, core: 2. Of those that a mesh axis runs over, the one named last changes fastest.
Arguments:
- coords: float32 [4, 524288], P(None, ('leaf', 'tm')), may hold values from -6 to 6
- direction: float32 [8, 524288], P(None, ('leaf', 'tm')), may hold values from -16 to 16
- iterate: float32 [8, 524288], P(None, ('leaf', 'tm')), may hold values from -6 to 6
- residual: float32 [8, 524288], P(None, ('leaf', 'tm')), may hold values from -24 to 24
- order: int32 [524288], P(('leaf', 'tm')), may hold values from 0 to 4095, as said below
- bases: float32 [1024, 64, 512], P(('leaf', 'tm')), may hold values from -0.25 to 0.25
- transfer: float32 [128, 64, 512], P(('leaf', 'tm')), may hold values from -0.25 to 0.25
- near_list: int32 [1024, 8], P(('leaf', 'tm')), may hold values from 0 to 71, as said below
- near_count: int32 [1024], P(('leaf', 'tm')), may hold values from 1 to 8, as said below
- far_list: int32 [1024, 8], P(('leaf', 'tm')), may hold values from 0 to 71, as said below
- device_skel: int32 [128, 64], P(('leaf', 'tm')), may hold values from 0 to 511, as said below
- inv_scale: float32 [4], replicated, may hold values from 0.5 to 2
- noise: float32 [8], replicated, may hold values from 0.5 to 2
Outputs:
- new_iterate: float32 [8, 524288], P(None, ('leaf', 'tm'))
- new_residual: float32 [8, 524288], P(None, ('leaf', 'tm'))
The draws below stay inside these ranges and needn't reach their ends.
Inputs may be any that keep to these rules, and one draw needn't show every extreme that they name: `order`: within each device's block the entries are a permutation of 0 to 4095. `near_list`: window indices name only devices inside the mesh; slot 0 is the leaf itself; the entries of one leaf's near and far lists are all distinct. `near_count`: slot 0 is always live; on every device some leaf has all 8 slots live. `far_list`: window indices name only devices inside the mesh, never the leaf itself nor a leaf of its near list. `device_skel`: the 64 slots of one device are distinct.
All inputs are finite; a program needn't handle non-finite values.
Results may differ from the reference program's by a relative error of at most 0.0003.
Values sent between devices are 32-bit elements; how exact they have to be, the bound alone decides.
No kernel may reach another device: no remote copies, remote signals or barrier semaphores. Data moves between devices by JAX's collectives and lax.ppermute only.
A program may use at most 64 MiB of HBM per device.

```python
import math
import jax
import jax.numpy as jnp
from jax import lax

LEAF_PTS = 512
RANK = 64
NRHS = 8
LEAF_DEV = 8
NEAR = 8
FAR = 8
LEAVES = 1024
NPTS = 524288
N_LEAF = 32
N_TM = 4


def ranked_window(key):
    devices = N_LEAF * N_TM
    leaves = devices * LEAF_DEV
    span = 9 * LEAF_DEV
    leaf_ids = jnp.arange(leaves, dtype=jnp.int32)
    device = leaf_ids // LEAF_DEV
    within = leaf_ids % LEAF_DEV
    grid_a = device // N_TM
    grid_b = device % N_TM
    window = jnp.arange(span, dtype=jnp.int32)
    block = window // LEAF_DEV
    target_a = grid_a[:, None] + block[None, :] // 3 - 1
    target_b = grid_b[:, None] + block[None, :] % 3 - 1
    inside = (target_a >= 0) & (target_a < N_LEAF) & (target_b >= 0) & (target_b < N_TM)
    is_self = window[None, :] == (4 * LEAF_DEV + within)[:, None]
    random_part = jax.random.randint(jax.random.fold_in(key, 101), (leaves, span), 0, 65536)
    score = random_part * 512 + window[None, :]
    score = jnp.where(inside, score, score + 268435456)
    score = jnp.where(is_self, -1, score)
    return jnp.argsort(score, axis=1, stable=True).astype(jnp.int32)


def draw_near_list(key, part):
    ranked = ranked_window(key)
    return ranked[:, :NEAR]


def draw_far_list(key, part):
    ranked = ranked_window(key)
    return ranked[:, NEAR:NEAR + FAR]


def draw_near_count(key, part):
    key = jax.random.fold_in(key, 3)
    devices = N_LEAF * N_TM
    first, second = jax.random.split(key)
    spread = jax.random.randint(first, (devices, 1), 0, NEAR)
    drop = jax.random.randint(second, (devices, LEAF_DEV), 0, spread + 1)
    counts = (NEAR - drop).at[:, 0].set(NEAR)
    return counts.reshape(-1).astype(jnp.int32)


def draw_order(key, part):
    key = jax.random.fold_in(key, 5)
    devices = N_LEAF * N_TM
    keys = jax.random.split(key, devices)
    blocks = jax.vmap(lambda single: jax.random.permutation(single, LEAF_DEV * LEAF_PTS))(keys)
    return blocks.reshape(-1).astype(jnp.int32)


def draw_device_skel(key, part):
    key = jax.random.fold_in(key, 7)
    devices = N_LEAF * N_TM
    keys = jax.random.split(key, devices)
    picks = jax.vmap(lambda single: jax.random.permutation(single, LEAF_DEV * RANK)[:RANK])(keys)
    return picks.astype(jnp.int32)


def shared_field(key):
    count = N_LEAF * N_TM * LEAF_DEV * LEAF_PTS
    first = jax.random.fold_in(key, 0)
    gauss = jnp.clip(jax.random.normal(first, (NRHS, count), jnp.float32), -4.0, 4.0)
    rise = 1.0 + 2.0 * jnp.arange(count, dtype=jnp.float32)[None, :] / count
    return (gauss, rise)


def draw_direction(key, part):
    gauss, rise = shared_field(key)
    values = gauss
    return values * rise


def draw_residual(key, part):
    gauss, rise = shared_field(key)
    key = jax.random.fold_in(key, 13)
    second = jax.random.fold_in(key, 1)
    other = jnp.clip(jax.random.normal(second, gauss.shape, jnp.float32), -4.0, 4.0)
    values = gauss + 0.5 * other
    return values * rise


def levels(own_key, dims, cuts, low, top_value):
    def one(dim, shards_of):
        steps = jax.random.uniform(jax.random.fold_in(jax.random.fold_in(own_key, 6), dim), (shards_of,), jnp.float32, low / len(cuts), top_value / len(cuts))
        return jnp.repeat(jnp.exp(steps), dims[dim] // shards_of).reshape((-1,) + (1,) * (len(dims) - dim - 1))

    loudness = one(*cuts[0])
    for cut in cuts[1:]:
        loudness = loudness * one(*cut)
    return loudness


def scatter_about(own_key, shape, deviation, limit, cuts=(), kind=jnp.bfloat16):
    entries = deviation * jax.random.normal(own_key, shape, jnp.float32)
    if cuts:
        entries = entries * levels(own_key, shape, cuts, -0.22, 0.18)
    return jnp.clip(entries, -limit, limit).astype(kind)


def setup_inputs(seed: int = 0) -> dict:
    streams_of = jax.random.split(jax.random.key(seed), 14)
    return {
        "coords": scatter_about(streams_of[0], (4, NPTS), 1.0, 6.0, ((1, 128),), jnp.float32),
        "direction": draw_direction(jax.random.fold_in(streams_of[13], 71), 0),
        "iterate": scatter_about(streams_of[2], (NRHS, NPTS), 1.0, 6.0, ((1, 128),), jnp.float32),
        "residual": draw_residual(jax.random.fold_in(streams_of[13], 71), 0),
        "order": draw_order(jax.random.fold_in(streams_of[13], 71), 0),
        "bases": scatter_about(streams_of[5], (LEAVES, RANK, LEAF_PTS), LEAF_PTS ** -0.5, 0.25, ((0, 128),), jnp.float32),
        "transfer": scatter_about(streams_of[6], (N_LEAF * N_TM, RANK, LEAF_DEV * RANK), (LEAF_DEV * RANK) ** -0.5, 0.25, ((0, 128),), jnp.float32),
        "near_list": draw_near_list(jax.random.fold_in(streams_of[13], 71), 0),
        "near_count": draw_near_count(jax.random.fold_in(streams_of[13], 71), 0),
        "far_list": draw_far_list(jax.random.fold_in(streams_of[13], 71), 0),
        "device_skel": draw_device_skel(jax.random.fold_in(streams_of[13], 71), 0),
        "inv_scale": jnp.clip(jnp.exp(jax.random.uniform(streams_of[11], (4,), jnp.float32, math.log(0.5), math.log(2.0))), 0.5, 2.0),
        "noise": jnp.clip(jnp.exp(jax.random.uniform(streams_of[12], (NRHS,), jnp.float32, math.log(0.5), math.log(2.0))), 0.5, 2.0),
    }


EXACT = lax.Precision.HIGHEST
ROOT_THREE = 1.7320508075688772

def matern(targets, sources, inv_scale):
    scaled = (targets[..., :, :, None] - sources[..., :, None, :]) * inv_scale[:, None, None]
    distance = jnp.sqrt(lax.optimization_barrier(jnp.sum(scaled * scaled, axis=-3)))
    return (1.0 + ROOT_THREE * distance) * jnp.exp(-ROOT_THREE * distance)

def window_to_global(window, leaf_ids):
    device = leaf_ids // LEAF_DEV
    grid_a = device // N_TM
    grid_b = device % N_TM
    block = window // LEAF_DEV
    within = window % LEAF_DEV
    shift_a = block // 3 - 1
    shift_b = block % 3 - 1
    return (((grid_a[:, None] + shift_a) * N_TM + grid_b[:, None] + shift_b) * LEAF_DEV + within).astype(jnp.int32)

def reference(coords, direction, iterate, residual, order, bases, transfer, near_list, near_count, far_list, device_skel, inv_scale, noise):
    devices = N_LEAF * N_TM
    per_device = LEAF_DEV * LEAF_PTS
    leaves = devices * LEAF_DEV
    offsets = jnp.arange(devices, dtype=jnp.int32) * per_device
    global_order = (order.reshape(devices, per_device) + offsets[:, None]).reshape(-1).astype(jnp.int32)
    leaf_x = coords[:, global_order].reshape(4, leaves, LEAF_PTS).transpose(1, 0, 2)
    leaf_p = direction[:, global_order].reshape(NRHS, leaves, LEAF_PTS).transpose(1, 0, 2)
    skel_coef = jnp.einsum('lrp,lsp->lrs', leaf_p, bases, precision=EXACT)
    skel_x = leaf_x[:, :, :RANK]
    leaf_ids = jnp.arange(leaves, dtype=jnp.int32)
    near_global = window_to_global(near_list, leaf_ids)
    far_global = window_to_global(far_list, leaf_ids)
    live = (jnp.arange(NEAR, dtype=jnp.int32)[None, :] < near_count[:, None]).astype(jnp.float32)

    def near_leaf(item):
        target_x, sources, weights = item
        kernel = matern(target_x, leaf_x[sources], inv_scale)
        return jnp.einsum('smn,srn,s->rm', kernel, leaf_p[sources], weights, precision=EXACT)
    near_field = lax.map(near_leaf, (leaf_x, near_global, live))

    def far_leaf(item):
        own_skel, sources = item
        kernel = matern(own_skel[None], skel_x[sources], inv_scale)
        return jnp.einsum('fmn,frn->rm', kernel, skel_coef[sources], precision=EXACT)
    leaf_far = lax.map(far_leaf, (skel_x, far_global))
    coef_dev = skel_coef.reshape(devices, LEAF_DEV, NRHS, RANK).transpose(0, 2, 1, 3).reshape(devices, NRHS, LEAF_DEV * RANK)
    slots_x = skel_x.reshape(devices, LEAF_DEV, 4, RANK).transpose(0, 2, 1, 3).reshape(devices, 4, LEAF_DEV * RANK)
    device_x = jax.vmap(lambda slots, picks: slots[:, picks])(slots_x, device_skel)
    device_w = jnp.einsum('drl,dsl->drs', coef_dev, transfer, precision=EXACT)
    device_ids = jnp.arange(devices, dtype=jnp.int32)
    grid_a = device_ids // N_TM
    grid_b = device_ids % N_TM

    def far_device(item):
        own_x, own_a, own_b = item
        distant = ((jnp.abs(grid_a - own_a) > 1) | (jnp.abs(grid_b - own_b) > 1)).astype(jnp.float32)
        kernel = matern(own_x, device_x, inv_scale)
        return jnp.einsum('cmn,crn,c->rm', kernel, device_w, distant, precision=EXACT)
    device_far = lax.map(far_device, (device_x, grid_a, grid_b))
    pushed = jnp.einsum('drs,dsl->drl', device_far, transfer, precision=EXACT)
    pushed = pushed.reshape(devices, NRHS, LEAF_DEV, RANK).transpose(0, 2, 1, 3).reshape(leaves, NRHS, RANK)
    incoming = leaf_far + pushed
    leaf_out = near_field + jnp.einsum('lrs,lsp->lrp', incoming, bases, precision=EXACT)
    flat_out = leaf_out.transpose(1, 0, 2).reshape(NRHS, leaves * LEAF_PTS)
    kernel_part = jnp.zeros_like(direction).at[:, global_order].set(flat_out)
    image = kernel_part + noise[:, None] * direction
    along = lax.optimization_barrier(jnp.sum(residual * image, axis=1))
    squares = lax.optimization_barrier(jnp.sum(image * image, axis=1))
    alpha = along / (squares + 1e-06)
    return (iterate + alpha[:, None] * direction, residual - alpha[:, None] * image)
```

```python
import functools
import math

import jax
import jax.numpy as jnp
from jax import lax
from jax.experimental import pallas as pl
from jax.experimental.pallas import tpu as pltpu
from jax.sharding import PartitionSpec as P

F32 = jnp.float32
BF16 = jnp.bfloat16
EXACT = lax.Precision.HIGHEST
LN2 = math.log(2.0)
LOG2E = 1.0 / LN2
UNIT = math.sqrt(3.0) * LOG2E
VMEM = pl.BlockSpec(memory_space=pltpu.VMEM)
SMEM = pl.BlockSpec(memory_space=pltpu.SMEM)
LIMIT = 50 * 2**20


def params(**kw):
    return pltpu.CompilerParams(vmem_limit_bytes=LIMIT, **kw)


def contract(a, b, dims, precision=None):
    return lax.dot_general(
        a, b, ((dims[0], dims[1]), ((), ())), precision=precision, preferred_element_type=F32
    )


def rounded(x):
    return x.astype(BF16).astype(F32)


def row_ids(shape):
    return lax.broadcasted_iota(jnp.int32, shape, 0)


def lane_ids(shape):
    return lax.broadcasted_iota(jnp.int32, shape, 1)


def features(xx, want_source, want_target):
    row = row_ids(xx.shape)
    high = rounded(xx)
    low = rounded(xx - high)
    held = high + low
    square = held * held
    square = square + pltpu.roll(square, 1, 0)
    norm = square + pltpu.roll(square, 2, 0)
    n0 = rounded(norm)
    rest = norm - n0
    n1 = rounded(rest)
    n2 = rest - n1
    zero = jnp.zeros_like(xx)
    out = []
    if want_source:
        parts = jnp.where(row < 4, high, low)
        tail = jnp.where(row == 0, n0, jnp.where(row == 1, n1, jnp.where(row == 2, n2, jnp.where(row < 6, 1.0, 0.0))))
        out.append(jnp.concatenate([parts, parts, tail, zero], axis=0).astype(BF16))
    if want_target:
        tail = jnp.where(row < 3, 1.0, jnp.where(row == 3, n0, jnp.where(row == 4, n1, jnp.where(row == 5, n2, 0.0))))
        out.append(jnp.concatenate([-2.0 * high, -2.0 * low, tail, zero], axis=0).astype(BF16))
    return out


def halves(w):
    high = rounded(w)
    return jnp.concatenate([high, w - high], axis=0).astype(BF16)


def kernel_of(z):
    z = jnp.maximum(z, 1e-30)
    v = z * lax.rsqrt(z)
    return (v + LOG2E) * jnp.exp2(-v)


def split(k):
    high = k.astype(BF16)
    return high, (k - high.astype(F32)).astype(BF16)


def gather_lanes(chunks, ids):
    lane = ids & 127
    chunk = ids >> 7
    picked = [None] * len(chunks)
    for s in range(len(chunks[0])):
        here = chunk == s
        for i, source in enumerate(chunks):
            got = jnp.take_along_axis(source[s](), lane, axis=1, mode="promise_in_bounds")
            picked[i] = got if s == 0 else jnp.where(here, got, picked[i])
    return picked


def upward_body(order_ref, x_ref, p_ref, bases_ref, transfer_ref, skel_ref, halo_ref, node_ref, inv_ref, xx, first, slot, tally):
    leaf_dev, rank, leaf_pts = bases_ref.shape
    points = x_ref.shape[1]
    chunks = points // 128
    per_leaf = leaf_pts // 128
    xx[0:4, :] = x_ref[...]
    xx[4:8, :] = x_ref[...]
    tally[...] = jnp.zeros_like(tally)

    def loads(ref):
        return [lambda s=s: ref[:, s * 128 : (s + 1) * 128] for s in range(chunks)]

    def two_leaves(g, _):
        kept = []
        for h in range(2):
            leaf = 2 * g + h
            for j in range(per_leaf):
                c = leaf * per_leaf + j
                ids = order_ref[pl.ds(c, 1), :]
                got_x, got_p = gather_lanes([loads(xx), loads(p_ref)], jnp.broadcast_to(ids, (8, 128)))
                kept.append(got_x)
                halo_ref[pl.ds(pl.multiple_of(32 + leaf * 8, 8), 8), j * 128 : (j + 1) * 128] = got_p
                low = jnp.where(row_ids((128, 128)) == (ids & 127), 1.0, 0.0).astype(BF16)
                row = row_ids((chunks, 128)) == (ids >> 7)
                lane = lane_ids((chunks, 128))
                digit1 = jnp.where(row, (2 * c + (lane >> 6)).astype(F32), 0.0)
                digit0 = jnp.where(row, (lane & 63).astype(F32), 0.0)
                digits = jnp.concatenate([digit1, digit0], axis=0).astype(BF16)
                tally[...] += contract(digits, low, ((1,), (1,)))
            first[leaf] = kept[h * per_leaf]
        for j in range(per_leaf):
            both = jnp.where(row_ids((8, 128)) < 4, kept[j], kept[per_leaf + j])
            halo_ref[pl.ds(pl.multiple_of(g * 8, 8), 8), j * 128 : (j + 1) * 128] = both
        return 0

    lax.fori_loop(0, leaf_dev // 2, two_leaves, 0)
    inv_ref[...] = (64.0 * tally[0:chunks, :] + tally[chunks : 2 * chunks, :] + 0.5).astype(jnp.int32)
    for leaf in range(leaf_dev):
        coef = contract(halo_ref[32 + leaf * 8 : 40 + leaf * 8, :], bases_ref[leaf], ((1,), (1,)), EXACT)
        halo_ref[96:104, leaf * rank : (leaf + 1) * rank] = coef
        slot[:, leaf * rank : (leaf + 1) * rank] = first[leaf][:, :rank]
    weights = contract(halo_ref[96:104, :], transfer_ref[...], ((1,), (1,)), EXACT)
    slots = [lambda s=s: slot[:, s * 128 : (s + 1) * 128] for s in range(leaf_dev * rank // 128)]
    (node_x,) = gather_lanes([slots], jnp.broadcast_to(skel_ref[...], (8, 128)))
    tile = jnp.concatenate([weights, node_x[:, :rank]], axis=1)
    node_ref[...] = jnp.broadcast_to(tile[None], node_ref.shape)


def near_body(near_ref, count_ref, far_ref, scale_ref, up_ref, mid_ref, down_ref, out_ref, far_out_ref, src, tgt, wgt, coef, k_high, k_low):
    leaf_dev = out_ref.shape[0]
    rank = far_out_ref.shape[2]
    leaf_pts = out_ref.shape[2]
    slots = near_ref.shape[1]
    row = row_ids((8, leaf_pts))
    scale = jnp.where((row & 3) == 0, scale_ref[0], jnp.where((row & 3) == 1, scale_ref[1], jnp.where((row & 3) == 2, scale_ref[2], scale_ref[3]))) * UNIT

    def prepare(ref, k, base, middle):
        def one(g, _):
            both = ref[k, pl.ds(pl.multiple_of(g * 8, 8), 8), :] * scale
            turned = pltpu.roll(both, 4, 0)
            for h in range(2):
                leaf = 2 * g + h
                xx = jnp.where(row < 4, both, turned) if h == 0 else jnp.where(row < 4, turned, both)
                made = features(xx, True, middle)
                src[base + leaf] = made[0]
                if middle:
                    tgt[leaf] = made[1]
                wgt[base + leaf] = halves(ref[k, pl.ds(pl.multiple_of(32 + leaf * 8, 8), 8), :] * LN2)
            return 0

        lax.fori_loop(0, leaf_dev // 2, one, 0)
        for leaf in range(leaf_dev):
            coef[base + leaf] = halves(ref[k, 96:104, leaf * rank : (leaf + 1) * rank] * LN2)

    for k in range(3):
        prepare(up_ref, k, k * leaf_dev, False)
        prepare(mid_ref, k, (3 + k) * leaf_dev, k == 1)
        prepare(down_ref, k, (6 + k) * leaf_dev, False)

    def leaf_step(leaf, _):
        target = tgt[leaf]
        total = jnp.zeros((16, leaf_pts), F32)
        for j in range(slots):
            w = near_ref[leaf, j]
            live = jnp.where(j < count_ref[leaf], 1.0, 0.0).astype(BF16)
            for q in range(0, leaf_pts, 128):
                z = contract(src[w, :, q : q + 128], target, ((0,), (0,)))
                high, low = split(kernel_of(z))
                k_high[j, q : q + 128, :] = high
                k_low[j, q : q + 128, :] = low
            weight = wgt[w] * live
            total = total + jnp.dot(weight, k_high[j], preferred_element_type=F32)
            total = total + jnp.dot(weight, k_low[j], preferred_element_type=F32)
        out_ref[leaf] = total[:8] + total[8:]
        far = jnp.zeros((16, rank), F32)
        for j in range(far_ref.shape[1]):
            w = far_ref[leaf, j]
            z = contract(src[w, :, 0:rank], tgt[leaf, :, 0:rank], ((0,), (0,)))
            high, low = split(kernel_of(z))
            far = far + jnp.dot(coef[w], high, preferred_element_type=F32)
            far = far + jnp.dot(coef[w], low, preferred_element_type=F32)
        far_out_ref[leaf] = far[:8] + far[8:]
        return 0

    lax.fori_loop(0, leaf_dev, leaf_step, 0)


def downward_body(place_ref, scale_ref, noise_ref, node_ref, own_ref, transfer_ref, bases_ref, near_ref, far_ref, inv_ref, p_ref, res_ref, image_ref, sums_ref, src, wgt, flat):
    devices = node_ref.shape[0]
    leaf_dev, rank, leaf_pts = bases_ref.shape
    tm_size = place_ref[2]
    row = row_ids((8, 128))
    lane = lane_ids((8, 128))
    scale = jnp.where((row & 3) == 0, scale_ref[0], jnp.where((row & 3) == 1, scale_ref[1], jnp.where((row & 3) == 2, scale_ref[2], scale_ref[3]))) * UNIT

    def distant(e):
        far_a = jnp.abs(e // tm_size - place_ref[0]) > 1
        far_b = jnp.abs(e % tm_size - place_ref[1]) > 1
        return jnp.where(far_a | far_b, LN2, 0.0)

    def unpack(g, _):
        one, two = node_ref[2 * g], node_ref[2 * g + 1]
        xx = jnp.where(lane < 64, pltpu.roll(one, 64, 1), two) * scale
        w = jnp.where(lane < 64, one * distant(2 * g), pltpu.roll(two, 64, 1) * distant(2 * g + 1))
        at = pl.ds(pl.multiple_of(g * 128, 128), 128)
        src[:, at] = features(xx, True, False)[0]
        wgt[:, at] = halves(w)
        return 0

    lax.fori_loop(0, devices // 2, unpack, 0)
    own = own_ref[...]
    own_xx = pltpu.roll(own, 64, 1) * scale
    target = features(own_xx, False, True)[0][:, :rank]
    total = jnp.zeros((16, rank), F32)
    step = 512
    for q in range(0, devices * rank, step):
        z = contract(target, src[:, q : q + step], ((0,), (0,)))
        high, low = split(kernel_of(z))
        weight = wgt[:, q : q + step]
        total = total + contract(weight, high, ((1,), (1,)))
        total = total + contract(weight, low, ((1,), (1,)))
    device_far = total[:8] + total[8:]
    pushed = jnp.dot(device_far, transfer_ref[...], precision=EXACT, preferred_element_type=F32)
    for leaf in range(leaf_dev):
        incoming = far_ref[leaf] + pushed[:, leaf * rank : (leaf + 1) * rank]
        out = near_ref[leaf] + jnp.dot(incoming, bases_ref[leaf], precision=EXACT, preferred_element_type=F32)
        flat[:, leaf * leaf_pts : (leaf + 1) * leaf_pts] = out
    chunks = flat.shape[1] // 128
    source = [lambda s=s: flat[:, s * 128 : (s + 1) * 128] for s in range(chunks)]
    noise = jnp.zeros((8, 128), F32)
    for r in range(8):
        noise = jnp.where(row == r, noise_ref[r], noise)

    def place(c, sums):
        at = pl.ds(pl.multiple_of(c * 128, 128), 128)
        ids = jnp.broadcast_to(inv_ref[pl.ds(c, 1), :], (8, 128))
        (part,) = gather_lanes([source], ids)
        image = part + noise * p_ref[:, at]
        image_ref[:, at] = image
        return sums[0] + res_ref[:, at] * image, sums[1] + image * image

    zero = jnp.zeros((8, 128), F32)
    along, squares = lax.fori_loop(0, chunks, place, (zero, zero))
    along = jnp.sum(along, axis=1, keepdims=True)
    squares = jnp.sum(squares, axis=1, keepdims=True)
    both = jnp.where(lane == row, along, 0.0) + jnp.where(lane == row + 8, squares, 0.0)
    sums_ref[...] = jnp.broadcast_to(jnp.sum(both, axis=0, keepdims=True), sums_ref.shape)


def update_body(sums_ref, it_ref, p_ref, res_ref, image_ref, new_it_ref, new_res_ref):
    total = jnp.sum(sums_ref[...], axis=0, keepdims=True)
    row = row_ids((8, 128))
    lane = lane_ids((8, 128))
    along = jnp.sum(jnp.where(lane == row, total, 0.0), axis=1, keepdims=True)
    squares = jnp.sum(jnp.where(lane == row + 8, total, 0.0), axis=1, keepdims=True)
    alpha = along / (squares + 1e-06)
    new_it_ref[...] = it_ref[...] + alpha * p_ref[...]
    new_res_ref[...] = res_ref[...] - alpha * image_ref[...]


def shifted(x, axis, by):
    n = lax.axis_size(axis)
    return lax.ppermute(x, axis, [(i, i + by) for i in range(n) if 0 <= i + by < n])


def shards(coords, direction, iterate, residual, order, bases, transfer, near_list, near_count, far_list, device_skel, inv_scale, noise):
    leaf_dev, rank, leaf_pts = bases.shape
    rhs, points = direction.shape
    axes = ("leaf", "tm")
    devices = lax.axis_size("leaf") * lax.axis_size("tm")
    chunks = points // 128
    shape = jax.ShapeDtypeStruct
    skel = jnp.pad(device_skel, ((0, 0), (0, 128 - rank)))
    halo, node, inverse = pl.pallas_call(
        upward_body,
        in_specs=[VMEM] * 6,
        out_specs=[VMEM] * 3,
        out_shape=[shape((104, leaf_pts), F32), shape((devices, 8, 128), F32), shape((chunks, 128), jnp.int32)],
        scratch_shapes=[
            pltpu.VMEM((8, points), F32),
            pltpu.VMEM((leaf_dev, 8, 128), F32),
            pltpu.VMEM((8, leaf_dev * rank), F32),
            pltpu.VMEM((2 * chunks, 128), F32),
        ],
        compiler_params=params(),
        name="upward",
    )(order.reshape(chunks, 128), coords, direction, bases, transfer[0], skel)
    before = shifted(halo, "tm", 1)
    after = shifted(halo, "tm", -1)
    nodes = lax.all_to_all(node, axes, 0, 0)
    mid = jnp.stack([before, halo, after])
    up = shifted(mid, "leaf", 1)
    down = shifted(mid, "leaf", -1)
    near, far = pl.pallas_call(
        near_body,
        in_specs=[SMEM] * 4 + [VMEM] * 3,
        out_specs=[VMEM] * 2,
        out_shape=[shape((leaf_dev, rhs, leaf_pts), F32), shape((leaf_dev, rhs, rank), F32)],
        scratch_shapes=[
            pltpu.VMEM((9 * leaf_dev, 32, leaf_pts), BF16),
            pltpu.VMEM((leaf_dev, 32, leaf_pts), BF16),
            pltpu.VMEM((9 * leaf_dev, 16, leaf_pts), BF16),
            pltpu.VMEM((9 * leaf_dev, 16, rank), BF16),
            pltpu.VMEM((near_list.shape[1], leaf_pts, leaf_pts), BF16),
            pltpu.VMEM((near_list.shape[1], leaf_pts, leaf_pts), BF16),
        ],
        compiler_params=params(),
        name="near",
    )(near_list, near_count, far_list, inv_scale, up, mid, down)
    place = jnp.stack([lax.axis_index("leaf"), lax.axis_index("tm"), lax.axis_size("tm")]).astype(jnp.int32)
    image, sums = pl.pallas_call(
        downward_body,
        in_specs=[SMEM] * 3 + [VMEM] * 9,
        out_specs=[VMEM] * 2,
        out_shape=[shape((rhs, points), F32), shape((devices, 128), F32)],
        scratch_shapes=[
            pltpu.VMEM((32, devices * rank), BF16),
            pltpu.VMEM((16, devices * rank), BF16),
            pltpu.VMEM((rhs, points), F32),
        ],
        compiler_params=params(),
        name="downward",
    )(place, inv_scale, noise, nodes, node[0], transfer[0], bases, near, far, inverse, direction, residual)
    all_sums = lax.all_to_all(sums, axes, 0, 0, tiled=True)
    return pl.pallas_call(
        update_body,
        in_specs=[VMEM] * 5,
        out_specs=[VMEM] * 2,
        out_shape=[shape((rhs, points), F32)] * 2,
        compiler_params=params(),
        name="update",
    )(all_sums, iterate, direction, residual, image)


def solution(mesh):
    whole = P(None, ("leaf", "tm"))
    first = P(("leaf", "tm"))
    return jax.shard_map(
        shards,
        mesh=mesh,
        in_specs=(whole,) * 4 + (first,) * 7 + (P(), P()),
        out_specs=(whole, whole),
        check_vma=False,
    )
```

```python
import math

import jax
import jax.numpy as jnp
from jax import lax
from jax.experimental import pallas as pl
from jax.experimental.pallas import tpu as pltpu
from jax.sharding import PartitionSpec as P

F32 = jnp.float32
BF16 = jnp.bfloat16
EXACT = lax.Precision.HIGHEST
LN2 = math.log(2.0)
LOG2E = 1.0 / LN2
UNIT = math.sqrt(3.0) * LOG2E
VMEM = pl.BlockSpec(memory_space=pltpu.VMEM)
SMEM = pl.BlockSpec(memory_space=pltpu.SMEM)
HBM = pl.BlockSpec(memory_space=pltpu.HBM)
PART = 256


def params(mib, **kw):
    return pltpu.CompilerParams(vmem_limit_bytes=mib * 2**20, **kw)


def contract(a, b, dims, precision=None):
    return lax.dot_general(
        a, b, ((dims[0], dims[1]), ((), ())), precision=precision, preferred_element_type=F32
    )


def rounded(x):
    return x.astype(BF16).astype(F32)


def row_ids(shape):
    return lax.broadcasted_iota(jnp.int32, shape, 0)


def lane_ids(shape):
    return lax.broadcasted_iota(jnp.int32, shape, 1)


def features(xx, want_source, want_target):
    row = row_ids(xx.shape)
    high = rounded(xx)
    low = rounded(xx - high)
    held = high + low
    square = held * held
    square = square + pltpu.roll(square, 1, 0)
    norm = square + pltpu.roll(square, 2, 0)
    n0 = rounded(norm)
    rest = norm - n0
    n1 = rounded(rest)
    n2 = rest - n1
    zero = jnp.zeros_like(xx)
    out = []
    if want_source:
        parts = jnp.where(row < 4, high, low)
        tail = jnp.where(row == 0, n0, jnp.where(row == 1, n1, jnp.where(row == 2, n2, jnp.where(row < 6, 1.0, 0.0))))
        out.append(jnp.concatenate([parts, parts, tail, zero], axis=0).astype(BF16))
    if want_target:
        tail = jnp.where(row < 3, 1.0, jnp.where(row == 3, n0, jnp.where(row == 4, n1, jnp.where(row == 5, n2, 0.0))))
        out.append(jnp.concatenate([-2.0 * high, -2.0 * low, tail, zero], axis=0).astype(BF16))
    return out


def halves(w):
    high = rounded(w)
    return jnp.concatenate([high, w - high], axis=0).astype(BF16)


def kernel_of(z):
    z = jnp.maximum(z, 1e-30)
    v = z * lax.rsqrt(z)
    return (v + LOG2E) * jnp.exp2(-v)


def split(k):
    high = k.astype(BF16)
    return high, (k - high.astype(F32)).astype(BF16)


def gather_lanes(chunks, ids):
    lane = ids & 127
    chunk = ids >> 7
    picked = [None] * len(chunks)
    for s in range(len(chunks[0])):
        here = chunk == s
        for i, source in enumerate(chunks):
            got = jnp.take_along_axis(source[s](), lane, axis=1, mode="promise_in_bounds")
            picked[i] = got if s == 0 else jnp.where(here, got, picked[i])
    return picked


def upward_body(order_hbm, x_hbm, p_hbm, bases_hbm, transfer_hbm, skel_hbm, halo_ref, node_ref, own_ref, inv_ref, order_ref, xx, p_ref, bases_ref, transfer_ref, skel_ref, first, slot, tally, sems):
    leaf_dev, rank, leaf_pts = bases_ref.shape
    points = p_ref.shape[1]
    chunks = points // 128
    per_leaf = leaf_pts // 128
    moves = [
        pltpu.make_async_copy(source, target, sems.at[i])
        for i, (source, target) in enumerate(
            [
                (order_hbm, order_ref),
                (x_hbm, xx.at[0:4, :]),
                (x_hbm, xx.at[4:8, :]),
                (p_hbm, p_ref),
                (bases_hbm, bases_ref),
                (transfer_hbm, transfer_ref),
                (skel_hbm, skel_ref),
            ]
        )
    ]
    for move in moves:
        move.start()
    tally[...] = jnp.zeros_like(tally)
    for move in moves[:4]:
        move.wait()

    def loads(ref):
        return [lambda s=s: ref[:, s * 128 : (s + 1) * 128] for s in range(chunks)]

    def two_leaves(g, _):
        kept = []
        for h in range(2):
            leaf = 2 * g + h
            for j in range(per_leaf):
                c = leaf * per_leaf + j
                ids = order_ref[pl.ds(c, 1), :]
                got_x, got_p = gather_lanes([loads(xx), loads(p_ref)], jnp.broadcast_to(ids, (8, 128)))
                kept.append(got_x)
                halo_ref[pl.ds(pl.multiple_of(32 + leaf * 8, 8), 8), j * 128 : (j + 1) * 128] = got_p
                low = jnp.where(row_ids((128, 128)) == (ids & 127), 1.0, 0.0).astype(BF16)
                row = row_ids((chunks, 128)) == (ids >> 7)
                lane = lane_ids((chunks, 128))
                digit1 = jnp.where(row, (2 * c + (lane >> 6)).astype(F32), 0.0)
                digit0 = jnp.where(row, (lane & 63).astype(F32), 0.0)
                digits = jnp.concatenate([digit1, digit0], axis=0).astype(BF16)
                tally[...] += contract(digits, low, ((1,), (1,)))
            first[leaf] = kept[h * per_leaf]
        for j in range(per_leaf):
            both = jnp.where(row_ids((8, 128)) < 4, kept[j], kept[per_leaf + j])
            halo_ref[pl.ds(pl.multiple_of(g * 8, 8), 8), j * 128 : (j + 1) * 128] = both
        return 0

    lax.fori_loop(0, leaf_dev // 2, two_leaves, 0)
    inv_ref[...] = (64.0 * tally[0:chunks, :] + tally[chunks : 2 * chunks, :] + 0.5).astype(jnp.int32)
    for move in moves[4:]:
        move.wait()
    for leaf in range(leaf_dev):
        coef = contract(halo_ref[32 + leaf * 8 : 40 + leaf * 8, :], bases_ref[leaf], ((1,), (1,)), EXACT)
        halo_ref[96:104, leaf * rank : (leaf + 1) * rank] = coef
        slot[:, leaf * rank : (leaf + 1) * rank] = first[leaf][:, :rank]
    weights = contract(halo_ref[96:104, :], transfer_ref[...], ((1,), (1,)), EXACT)
    slots = [lambda s=s: slot[:, s * 128 : (s + 1) * 128] for s in range(leaf_dev * rank // 128)]
    ids = jnp.concatenate([skel_ref[...], skel_ref[...]], axis=1)
    (node_x,) = gather_lanes([slots], jnp.broadcast_to(ids, (8, 128)))
    tile = jnp.concatenate([weights, node_x[:, :rank]], axis=1)
    own_ref[...] = tile
    node_ref[...] = jnp.broadcast_to(tile[None], node_ref.shape)


def scale_rows(scale_ref, shape):
    row = row_ids(shape) & 3
    picked = jnp.where(row == 0, scale_ref[0], jnp.where(row == 1, scale_ref[1], jnp.where(row == 2, scale_ref[2], scale_ref[3])))
    return picked * UNIT


def prepare(ref, scale, base, src, wgt=None, tgt=None, coef=None):
    leaf_dev = ref.shape[0] // 13
    width = scale.shape[1]
    row = row_ids(scale.shape)
    for g in range(leaf_dev // 2):
        both = ref[g * 8 : g * 8 + 8, 0:width] * scale
        turned = pltpu.roll(both, 4, 0)
        for h in range(2):
            leaf = 2 * g + h
            xx = jnp.where(row < 4, both, turned) if h == 0 else jnp.where(row < 4, turned, both)
            made = features(xx, True, tgt is not None)
            src[base + leaf, :, 0:width] = made[0]
            if tgt is not None:
                tgt[leaf, :, 0:width] = made[1]
            if wgt is not None:
                wgt[base + leaf] = halves(ref[32 + leaf * 8 : 40 + leaf * 8, :] * LN2)
            if coef is not None:
                rank = coef.shape[2]
                coef[base + leaf] = halves(ref[96:104, leaf * rank : (leaf + 1) * rank] * LN2)


def list_pairs(near_ref, count_ref, keep, slot_of, idle, pairs):
    leaf_dev, slots = near_ref.shape

    def leaf_step(leaf, n):
        def entry(j, n):
            w = near_ref[leaf, j]
            pairs[n] = leaf * 128 + slot_of(w)
            return n + jnp.where(keep(w // leaf_dev), 1, 0)

        return lax.fori_loop(0, count_ref[leaf], entry, n)

    n = lax.fori_loop(0, leaf_dev, leaf_step, 0)
    for extra in range(3):
        pairs[n + extra] = idle
    return n


def near_pairs(pairs, n, src, tgt, wgt, out, z, high, low):
    parts = wgt.shape[2] // PART

    def where(p):
        return pairs[p] >> 7, pairs[p] & 127

    def distances(p, c, b):
        leaf, w = where(p)
        z[b] = contract(src[w, :, c * PART : (c + 1) * PART], tgt[leaf], ((0,), (0,)))

    def values(b):
        high[b], low[b] = split(kernel_of(z[b]))

    def product(p, c, b):
        _, w = where(p)
        weight = wgt[w, :, c * PART : (c + 1) * PART]
        got = jnp.dot(weight, high[b], preferred_element_type=F32)
        return got + jnp.dot(weight, low[b], preferred_element_type=F32)

    distances(0, 0, 0)
    distances(0, 1, 1)
    values(0)

    def two_pairs(g, _):
        for h in range(2):
            p = 2 * g + h
            got = None
            for c in range(parts):
                b = c % 2
                values(1 - b)
                mine = product(p, c, b)
                got = mine if got is None else got + mine
                distances(p + (c + 2) // parts, (c + 2) % parts, b)
            leaf, _ = where(p)
            out[leaf] += got[:8] + got[8:]
        return 0

    lax.fori_loop(0, (n + 1) // 2, two_pairs, 0)


def blank(src, wgt):
    src[src.shape[0] - 1] = jnp.zeros(src.shape[1:], BF16)
    wgt[wgt.shape[0] - 1] = jnp.zeros(wgt.shape[1:], BF16)


def close_body(near_ref, count_ref, place_ref, scale_ref, left_ref, mid_ref, right_ref, node_ref, own_ref, transfer_ref, out_ref, pushed_ref, pairs, src, tgt, wgt, z, high, low, node_src, node_wgt):
    leaf_dev, rhs, leaf_pts = out_ref.shape
    devices, _, _ = node_ref.shape
    rank = own_ref.shape[1] // 2
    scale = scale_rows(scale_ref, (8, leaf_pts))
    n = list_pairs(near_ref, count_ref, lambda k: (k >= 3) & (k < 6), lambda w: w - 3 * leaf_dev, 3 * leaf_dev, pairs)
    blank(src, wgt)
    prepare(left_ref, scale, 0, src, wgt)
    prepare(mid_ref, scale, leaf_dev, src, wgt, tgt)
    prepare(right_ref, scale, 2 * leaf_dev, src, wgt)
    out_ref[...] = jnp.zeros_like(out_ref)
    near_pairs(pairs, n, src, tgt, wgt, out_ref, z, high, low)

    tm_size = place_ref[2]
    lane = lane_ids((8, 128))

    def distant(e):
        far_a = jnp.abs(e // tm_size - place_ref[0]) > 1
        far_b = jnp.abs(e % tm_size - place_ref[1]) > 1
        return jnp.where(far_a | far_b, LN2, 0.0)

    def unpack(g, _):
        xs, ws = [], []
        for k in range(4):
            e = 8 * g + 2 * k
            one, two = node_ref[e], node_ref[e + 1]
            xs.append(jnp.where(lane < rank, pltpu.roll(one, rank, 1), two))
            ws.append(jnp.where(lane < rank, one * distant(e), pltpu.roll(two, rank, 1) * distant(e + 1)))
        at = pl.ds(pl.multiple_of(g * 512, 512), 512)
        node_src[:, at] = features(jnp.concatenate(xs, axis=1) * scale, True, False)[0]
        node_wgt[:, at] = halves(jnp.concatenate(ws, axis=1))
        return 0

    lax.fori_loop(0, devices // 8, unpack, 0, unroll=4)
    own_xx = pltpu.roll(own_ref[...], rank, 1) * scale[:, 0 : 2 * rank]
    target = features(own_xx, False, True)[0][:, :rank]
    total = jnp.zeros((16, rank), F32)
    step = 512
    for q in range(0, devices * rank, step):
        z_far = contract(target, node_src[:, q : q + step], ((0,), (0,)))
        k_high, k_low = split(kernel_of(z_far))
        weight = node_wgt[:, q : q + step]
        total = total + contract(weight, k_high, ((1,), (1,)))
        total = total + contract(weight, k_low, ((1,), (1,)))
    device_far = total[:8] + total[8:]
    pushed_ref[...] = jnp.dot(device_far, transfer_ref[...], precision=EXACT, preferred_element_type=F32)


def rest_body(near_ref, count_ref, far_ref, scale_ref, noise_ref, left_ref, mid_ref, right_ref, up_ref, down_ref, close_ref, pushed_ref, bases_ref, inv_ref, p_ref, res_ref, image_ref, sums_ref, pairs, src, tgt, wgt, coef, z, high, low, out, flat):
    leaf_dev, rank, leaf_pts = bases_ref.shape
    scale = scale_rows(scale_ref, (8, leaf_pts))
    n = list_pairs(near_ref, count_ref, lambda k: (k < 3) | (k >= 6), lambda w: w, 9 * leaf_dev, pairs)
    blank(src, wgt)
    for k in range(3):
        prepare(up_ref.at[k], scale, k * leaf_dev, src, wgt, None, coef)
        prepare(down_ref.at[k], scale, (6 + k) * leaf_dev, src, wgt, None, coef)
    prepare(left_ref, scale[:, :128], 3 * leaf_dev, src, None, None, coef)
    prepare(mid_ref, scale, 4 * leaf_dev, src, None, tgt, coef)
    prepare(right_ref, scale[:, :128], 5 * leaf_dev, src, None, None, coef)
    out[...] = close_ref[...]
    near_pairs(pairs, n, src, tgt, wgt, out, z, high, low)

    for leaf in range(leaf_dev):
        far = jnp.zeros((16, rank), F32)
        for j in range(far_ref.shape[1]):
            w = far_ref[leaf, j]
            z_far = contract(src[w, :, 0:rank], tgt[leaf, :, 0:rank], ((0,), (0,)))
            k_high, k_low = split(kernel_of(z_far))
            far = far + jnp.dot(coef[w], k_high, preferred_element_type=F32)
            far = far + jnp.dot(coef[w], k_low, preferred_element_type=F32)
        incoming = halves(far[:8] + far[8:] + pushed_ref[:, leaf * rank : (leaf + 1) * rank])
        base_high, base_low = split(bases_ref[leaf])
        got = jnp.dot(incoming, base_high, preferred_element_type=F32)
        got = got + jnp.dot(incoming, base_low, preferred_element_type=F32)
        flat[:, leaf * leaf_pts : (leaf + 1) * leaf_pts] = out[leaf] + got[:8] + got[8:]

    chunks = flat.shape[1] // 128
    row = row_ids((8, 128))
    lane = lane_ids((8, 128))
    source = [lambda s=s: flat[:, s * 128 : (s + 1) * 128] for s in range(chunks)]
    noise = jnp.zeros((8, 128), F32)
    for r in range(8):
        noise = jnp.where(row == r, noise_ref[r], noise)

    def place(g, sums):
        along, squares = sums
        for h in range(4):
            c = 4 * g + h
            at = pl.ds(pl.multiple_of(c * 128, 128), 128)
            ids = jnp.broadcast_to(inv_ref[pl.ds(c, 1), :], (8, 128))
            (part,) = gather_lanes([source], ids)
            image = part + noise * p_ref[:, at]
            image_ref[:, at] = image
            along, squares = along + res_ref[:, at] * image, squares + image * image
        return along, squares

    zero = jnp.zeros((8, 128), F32)
    along, squares = lax.fori_loop(0, chunks // 4, place, (zero, zero))
    along = jnp.sum(along, axis=1, keepdims=True)
    squares = jnp.sum(squares, axis=1, keepdims=True)
    both = jnp.where(lane == row, along, 0.0) + jnp.where(lane == row + 8, squares, 0.0)
    sums_ref[...] = jnp.broadcast_to(jnp.sum(both, axis=0, keepdims=True), sums_ref.shape)


def update_body(sums_ref, it_ref, p_ref, res_ref, image_ref, new_it_ref, new_res_ref):
    total = jnp.sum(sums_ref[...], axis=0, keepdims=True)
    row = row_ids((8, 128))
    lane = lane_ids((8, 128))
    along = jnp.sum(jnp.where(lane == row, total, 0.0), axis=1, keepdims=True)
    squares = jnp.sum(jnp.where(lane == row + 8, total, 0.0), axis=1, keepdims=True)
    alpha = along / (squares + 1e-06)
    new_it_ref[...] = it_ref[...] + alpha * p_ref[...]
    new_res_ref[...] = res_ref[...] - alpha * image_ref[...]


def shifted(x, axis, by):
    n = lax.axis_size(axis)
    return lax.ppermute(x, axis, [(i, i + by) for i in range(n) if 0 <= i + by < n])


def shards(coords, direction, iterate, residual, order, bases, transfer, near_list, near_count, far_list, device_skel, inv_scale, noise):
    leaf_dev, rank, leaf_pts = bases.shape
    rhs, points = direction.shape
    axes = ("leaf", "tm")
    devices = lax.axis_size("leaf") * lax.axis_size("tm")
    chunks = points // 128
    shape = jax.ShapeDtypeStruct
    halo, node, own, inverse = pl.pallas_call(
        upward_body,
        in_specs=[HBM] * 6,
        out_specs=[VMEM] * 4,
        out_shape=[
            shape((13 * leaf_dev, leaf_pts), F32),
            shape((devices, 8, 128), F32),
            shape((8, 128), F32),
            shape((chunks, 128), jnp.int32),
        ],
        scratch_shapes=[
            pltpu.VMEM((chunks, 128), jnp.int32),
            pltpu.VMEM((8, points), F32),
            pltpu.VMEM((rhs, points), F32),
            pltpu.VMEM(bases.shape, F32),
            pltpu.VMEM(transfer.shape[1:], F32),
            pltpu.VMEM(device_skel.shape, jnp.int32),
            pltpu.VMEM((leaf_dev, 8, 128), F32),
            pltpu.VMEM((8, leaf_dev * rank), F32),
            pltpu.VMEM((2 * chunks, 128), F32),
            pltpu.SemaphoreType.DMA((7,)),
        ],
        compiler_params=params(24),
        name="upward",
    )(order.reshape(chunks, 128), coords, direction, bases, transfer[0], device_skel)
    left = shifted(halo, "tm", 1)
    right = shifted(halo, "tm", -1)
    nodes = lax.all_to_all(node, axes, 0, 0)
    left, right, nodes = lax.optimization_barrier((left, right, nodes))
    row = jnp.stack([left, halo, right])
    up = shifted(row, "leaf", 1)
    down = shifted(row, "leaf", -1)
    place = jnp.stack([lax.axis_index("leaf"), lax.axis_index("tm"), lax.axis_size("tm")]).astype(jnp.int32)

    def pipeline(sources):
        return [
            pltpu.VMEM((sources + 1, 32, leaf_pts), BF16),
            pltpu.VMEM((leaf_dev, 32, leaf_pts), BF16),
            pltpu.VMEM((sources + 1, 16, leaf_pts), BF16),
        ]

    buffers = [
        pltpu.VMEM((2, PART, leaf_pts), F32),
        pltpu.VMEM((2, PART, leaf_pts), BF16),
        pltpu.VMEM((2, PART, leaf_pts), BF16),
    ]
    listed = pltpu.SMEM((near_list.size + 4,), jnp.int32)
    close, pushed = pl.pallas_call(
        close_body,
        in_specs=[SMEM] * 4 + [VMEM] * 6,
        out_specs=[VMEM] * 2,
        out_shape=[shape((leaf_dev, rhs, leaf_pts), F32), shape((rhs, leaf_dev * rank), F32)],
        scratch_shapes=[listed]
        + pipeline(3 * leaf_dev)
        + buffers
        + [pltpu.VMEM((32, devices * rank), BF16), pltpu.VMEM((16, devices * rank), BF16)],
        compiler_params=params(24),
        cost_estimate=pl.CostEstimate(flops=10**10, bytes_accessed=2**21, transcendentals=10**7),
        name="close",
    )(near_list, near_count, place, inv_scale, left, halo, right, nodes, own, transfer[0])
    image, sums = pl.pallas_call(
        rest_body,
        in_specs=[SMEM] * 5 + [VMEM] * 11,
        out_specs=[VMEM] * 2,
        out_shape=[shape((rhs, points), F32), shape((devices, 128), F32)],
        scratch_shapes=[listed]
        + pipeline(9 * leaf_dev)
        + [pltpu.VMEM((9 * leaf_dev, 16, rank), BF16)]
        + buffers
        + [pltpu.VMEM((leaf_dev, rhs, leaf_pts), F32), pltpu.VMEM((rhs, points), F32)],
        compiler_params=params(24),
        name="rest",
    )(near_list, near_count, far_list, inv_scale, noise, left, halo, right, up, down, close, pushed, bases, inverse, direction, residual)
    all_sums = lax.all_to_all(sums, axes, 0, 0, tiled=True)
    return pl.pallas_call(
        update_body,
        in_specs=[VMEM] * 5,
        out_specs=[VMEM] * 2,
        out_shape=[shape((rhs, points), F32)] * 2,
        compiler_params=params(24),
        name="update",
    )(all_sums, iterate, direction, residual, image)


def solution(mesh):
    whole = P(None, ("leaf", "tm"))
    first = P(("leaf", "tm"))
    return jax.shard_map(
        shards,
        mesh=mesh,
        in_specs=(whole,) * 4 + (first,) * 7 + (P(), P()),
        out_specs=(whole, whole),
        check_vma=False,
    )
```

```python
import functools
import math

import jax
import jax.numpy as jnp
from jax import lax
from jax.experimental import pallas as pl
from jax.experimental.pallas import tpu as pltpu
from jax.sharding import PartitionSpec as P

F32 = jnp.float32
BF16 = jnp.bfloat16
EXACT = lax.Precision.HIGHEST
LN2 = math.log(2.0)
LOG2E = 1.0 / LN2
UNIT = math.sqrt(3.0) * LOG2E
FACTOR = -LN2 * math.e
VMEM = pl.BlockSpec(memory_space=pltpu.VMEM)
SMEM = pl.BlockSpec(memory_space=pltpu.SMEM)
ANY = pl.BlockSpec(memory_space=pl.ANY)
PART = 256


def params(mib, **kw):
    return pltpu.CompilerParams(vmem_limit_bytes=mib * 2**20, **kw)


def contract(a, b, dims, precision=None):
    return lax.dot_general(
        a, b, ((dims[0], dims[1]), ((), ())), precision=precision, preferred_element_type=F32
    )


def rounded(x):
    return x.astype(BF16).astype(F32)


def row_ids(shape):
    return lax.broadcasted_iota(jnp.int32, shape, 0)


def lane_ids(shape):
    return lax.broadcasted_iota(jnp.int32, shape, 1)


def features(xx, want_source, want_target):
    row = row_ids(xx.shape)
    high = rounded(xx)
    low = rounded(xx - high)
    held = high + low
    square = held * held
    square = square + pltpu.roll(square, 1, 0)
    norm = square + pltpu.roll(square, 2, 0)
    n0 = rounded(norm)
    rest = norm - n0
    n1 = rounded(rest)
    n2 = rest - n1
    zero = jnp.zeros_like(xx)
    out = []
    if want_source:
        parts = jnp.where(row < 4, high, low)
        tail = jnp.where(row == 0, n0, jnp.where(row == 1, n1, jnp.where(row == 2, n2, jnp.where(row < 6, 1.0, 0.0))))
        out.append(jnp.concatenate([parts, parts, tail, zero], axis=0).astype(BF16))
    if want_target:
        tail = jnp.where(row < 3, 1.0, jnp.where(row == 3, n0, jnp.where(row == 4, n1, jnp.where(row == 5, n2, 0.0))))
        out.append(jnp.concatenate([-2.0 * high, -2.0 * low, tail, zero], axis=0).astype(BF16))
    return out


def halves(w):
    high = rounded(w)
    return jnp.concatenate([high, w - high], axis=0).astype(BF16)


def kernel_of(z):
    z = jnp.maximum(z, 1e-30)
    q = -LOG2E - z * lax.rsqrt(z)
    return q * jnp.exp2(q)


def split(k):
    high = k.astype(BF16)
    return high, (k - high.astype(F32)).astype(BF16)


def gather_lanes(chunks, ids):
    lane = ids & 127
    chunk = ids >> 7
    picked = [None] * len(chunks)
    for s in range(len(chunks[0])):
        here = chunk == s
        for i, source in enumerate(chunks):
            got = jnp.take_along_axis(source[s](), lane, axis=1, mode="promise_in_bounds")
            picked[i] = got if s == 0 else jnp.where(here, got, picked[i])
    return picked


def gather_body(order_hbm, x_hbm, p_hbm, bases_hbm, halo_ref, first_ref, order_ref, xx, p_ref, bases_ref, sems):
    leaf_dev, rank, leaf_pts = bases_ref.shape
    points = p_ref.shape[1]
    chunks = points // 128
    per_leaf = leaf_pts // 128
    moves = [
        pltpu.make_async_copy(source, target, sems.at[i])
        for i, (source, target) in enumerate(
            [
                (order_hbm, order_ref),
                (x_hbm, xx.at[0:4, :]),
                (x_hbm, xx.at[4:8, :]),
                (p_hbm, p_ref),
                (bases_hbm, bases_ref),
            ]
        )
    ]
    for move in moves:
        move.start()
    for move in moves[:4]:
        move.wait()

    def loads(ref):
        return [lambda s=s: ref[:, s * 128 : (s + 1) * 128] for s in range(chunks)]

    def two_leaves(g, _):
        kept = []
        for h in range(2):
            leaf = 2 * g + h
            for j in range(per_leaf):
                ids = order_ref[pl.ds(leaf * per_leaf + j, 1), :]
                got_x, got_p = gather_lanes([loads(xx), loads(p_ref)], jnp.broadcast_to(ids, (8, 128)))
                kept.append(got_x)
                halo_ref[pl.ds(pl.multiple_of(32 + leaf * 8, 8), 8), j * 128 : (j + 1) * 128] = got_p
            first_ref[leaf] = kept[h * per_leaf]
        for j in range(per_leaf):
            both = jnp.where(row_ids((8, 128)) < 4, kept[j], kept[per_leaf + j])
            halo_ref[pl.ds(pl.multiple_of(g * 8, 8), 8), j * 128 : (j + 1) * 128] = both
        return 0

    lax.fori_loop(0, leaf_dev // 2, two_leaves, 0)
    moves[4].wait()
    for leaf in range(leaf_dev):
        coef = contract(halo_ref[32 + leaf * 8 : 40 + leaf * 8, :], bases_ref[leaf], ((1,), (1,)), EXACT)
        halo_ref[96:104, leaf * rank : (leaf + 1) * rank] = coef


def node_body(order_ref, halo_ref, first_ref, transfer_ref, skel_ref, node_ref, own_ref, inv_ref, slot):
    chunks = order_ref.shape[0]
    rank = transfer_ref.shape[0]
    leaf_dev = first_ref.shape[0]
    for leaf in range(leaf_dev):
        slot[:, leaf * rank : (leaf + 1) * rank] = first_ref[leaf][:, :rank]
    weights = contract(halo_ref[96:104, :], transfer_ref[...], ((1,), (1,)), EXACT)
    slots = [lambda s=s: slot[:, s * 128 : (s + 1) * 128] for s in range(leaf_dev * rank // 128)]
    ids = jnp.concatenate([skel_ref[...], skel_ref[...]], axis=1)
    (node_x,) = gather_lanes([slots], jnp.broadcast_to(ids, (8, 128)))
    tile = jnp.concatenate([weights, node_x[:, :rank]], axis=1)
    own_ref[...] = tile
    node_ref[...] = jnp.broadcast_to(tile[None], node_ref.shape)
    tally = jnp.zeros((2 * chunks, 128), F32)
    for c in range(chunks):
        ids = order_ref[c : c + 1, :]
        low = jnp.where(row_ids((128, 128)) == (ids & 127), 1.0, 0.0).astype(BF16)
        row = row_ids((chunks, 128)) == (ids >> 7)
        lane = lane_ids((chunks, 128))
        digit1 = jnp.where(row, (2 * c + (lane >> 6)).astype(F32), 0.0)
        digit0 = jnp.where(row, (lane & 63).astype(F32), 0.0)
        digits = jnp.concatenate([digit1, digit0], axis=0).astype(BF16)
        tally = tally + contract(digits, low, ((1,), (1,)))
    inv_ref[...] = (64.0 * tally[0:chunks] + tally[chunks : 2 * chunks] + 0.5).astype(jnp.int32)


def scale_rows(scale_ref, shape):
    row = row_ids(shape) & 3
    picked = jnp.where(row == 0, scale_ref[0], jnp.where(row == 1, scale_ref[1], jnp.where(row == 2, scale_ref[2], scale_ref[3])))
    return picked * UNIT


def prepare(ref, scale, base, src, wgt=None, tgt=None, coef=None):
    leaf_dev = ref.shape[0] // 13
    width = scale.shape[1]
    row = row_ids(scale.shape)
    for g in range(leaf_dev // 2):
        both = ref[g * 8 : g * 8 + 8, 0:width] * scale
        turned = pltpu.roll(both, 4, 0)
        for h in range(2):
            leaf = 2 * g + h
            xx = jnp.where(row < 4, both, turned) if h == 0 else jnp.where(row < 4, turned, both)
            made = features(xx, True, tgt is not None)
            src[base + leaf, :, 0:width] = made[0]
            if tgt is not None:
                tgt[leaf, :, 0:width] = made[1]
            if wgt is not None:
                wgt[base + leaf] = halves(ref[32 + leaf * 8 : 40 + leaf * 8, :] * FACTOR)
            if coef is not None:
                rank = coef.shape[2]
                coef[base + leaf] = halves(ref[96:104, leaf * rank : (leaf + 1) * rank] * FACTOR)


def list_pairs(near_ref, count_ref, keep, slot_of, idle, pairs):
    leaf_dev, slots = near_ref.shape

    def leaf_step(leaf, n):
        def entry(j, n):
            w = near_ref[leaf, j]
            pairs[n] = leaf * 128 + slot_of(w)
            return n + jnp.where(keep(w // leaf_dev), 1, 0)

        return lax.fori_loop(0, count_ref[leaf], entry, n)

    n = lax.fori_loop(0, leaf_dev, leaf_step, 0)
    for extra in range(3):
        pairs[n + extra] = idle
    return n


def near_pairs(pairs, n, src, tgt, wgt, out, z, high, low):
    parts = wgt.shape[2] // PART

    def where(p):
        return pairs[p] >> 7, pairs[p] & 127

    def distances(p, c, b):
        leaf, w = where(p)
        z[b] = contract(src[w, :, c * PART : (c + 1) * PART], tgt[leaf], ((0,), (0,)))

    def values(b):
        high[b], low[b] = split(kernel_of(z[b]))

    def product(p, c, b):
        _, w = where(p)
        weight = wgt[w, :, c * PART : (c + 1) * PART]
        got = jnp.dot(weight, high[b], preferred_element_type=F32)
        return got + jnp.dot(weight, low[b], preferred_element_type=F32)

    distances(0, 0, 0)
    distances(0, 1, 1)
    values(0)

    def two_pairs(g, _):
        for h in range(2):
            p = 2 * g + h
            got = None
            for c in range(parts):
                b = c % 2
                values(1 - b)
                mine = product(p, c, b)
                got = mine if got is None else got + mine
                distances(p + (c + 2) // parts, (c + 2) % parts, b)
            leaf, _ = where(p)
            out[leaf] += got[:8] + got[8:]
        return 0

    lax.fori_loop(0, (n + 1) // 2, two_pairs, 0)


def blank(src, wgt):
    src[src.shape[0] - 1] = jnp.zeros(src.shape[1:], BF16)
    wgt[wgt.shape[0] - 1] = jnp.zeros(wgt.shape[1:], BF16)


def close_body(tm_size, near_ref, count_ref, place_ref, scale_ref, left_ref, mid_ref, right_ref, node_ref, own_ref, transfer_ref, out_ref, pushed_ref, pairs, src, tgt, wgt, z, high, low, node_src, node_wgt):
    leaf_dev, rhs, leaf_pts = out_ref.shape
    devices, _, _ = node_ref.shape
    rank = own_ref.shape[1] // 2
    scale = scale_rows(scale_ref, (8, leaf_pts))
    n = list_pairs(near_ref, count_ref, lambda k: (k >= 3) & (k < 6), lambda w: w - 3 * leaf_dev, 3 * leaf_dev, pairs)
    blank(src, wgt)
    prepare(left_ref, scale, 0, src, wgt)
    prepare(mid_ref, scale, leaf_dev, src, wgt, tgt)
    prepare(right_ref, scale, 2 * leaf_dev, src, wgt)
    out_ref[...] = jnp.zeros_like(out_ref)
    near_pairs(pairs, n, src, tgt, wgt, out_ref, z, high, low)

    lane = lane_ids((8, 128))

    def distant(e):
        far_a = jnp.abs(e // tm_size - place_ref[0]) > 1
        far_b = jnp.abs(e % tm_size - place_ref[1]) > 1
        return jnp.where(far_a | far_b, FACTOR, 0.0)

    def unpack(g, _):
        xs, ws = [], []
        for k in range(4):
            e = 8 * g + 2 * k
            one, two = node_ref[e], node_ref[e + 1]
            xs.append(jnp.where(lane < rank, pltpu.roll(one, rank, 1), two))
            ws.append(jnp.where(lane < rank, one * distant(e), pltpu.roll(two, rank, 1) * distant(e + 1)))
        at = pl.ds(pl.multiple_of(g * 512, 512), 512)
        node_src[:, at] = features(jnp.concatenate(xs, axis=1) * scale, True, False)[0]
        node_wgt[:, at] = halves(jnp.concatenate(ws, axis=1))
        return 0

    lax.fori_loop(0, devices // 8, unpack, 0, unroll=4)
    own_xx = pltpu.roll(own_ref[...], rank, 1) * scale[:, 0 : 2 * rank]
    target = features(own_xx, False, True)[0][:, :rank]
    total = jnp.zeros((16, rank), F32)
    step = 512
    for q in range(0, devices * rank, step):
        z_far = contract(target, node_src[:, q : q + step], ((0,), (0,)))
        k_high, k_low = split(kernel_of(z_far))
        weight = node_wgt[:, q : q + step]
        total = total + contract(weight, k_high, ((1,), (1,)))
        total = total + contract(weight, k_low, ((1,), (1,)))
    device_far = total[:8] + total[8:]
    pushed_ref[...] = jnp.dot(device_far, transfer_ref[...], precision=EXACT, preferred_element_type=F32)


def rest_body(near_ref, count_ref, far_ref, scale_ref, noise_ref, left_ref, mid_ref, right_ref, up_ref, down_ref, close_ref, pushed_ref, bases_ref, inv_ref, p_ref, res_ref, image_ref, sums_ref, pairs, src, tgt, wgt, coef, z, high, low, out, flat, far_src, far_wgt):
    leaf_dev, rank, leaf_pts = bases_ref.shape
    scale = scale_rows(scale_ref, (8, leaf_pts))
    n = list_pairs(near_ref, count_ref, lambda k: (k < 3) | (k >= 6), lambda w: w, 9 * leaf_dev, pairs)
    blank(src, wgt)
    for k in range(3):
        prepare(up_ref.at[k], scale, k * leaf_dev, src, wgt, None, coef)
        prepare(down_ref.at[k], scale, (6 + k) * leaf_dev, src, wgt, None, coef)
    prepare(left_ref, scale[:, :128], 3 * leaf_dev, src, None, None, coef)
    prepare(mid_ref, scale, 4 * leaf_dev, src, None, tgt, coef)
    prepare(right_ref, scale[:, :128], 5 * leaf_dev, src, None, None, coef)
    out[...] = close_ref[...]
    near_pairs(pairs, n, src, tgt, wgt, out, z, high, low)

    for leaf in range(leaf_dev):
        for j in range(far_ref.shape[1]):
            w = far_ref[leaf, j]
            at = slice(j * rank, (j + 1) * rank)
            far_src[leaf, :, at] = src[w, :, 0:rank]
            far_wgt[leaf, :, at] = coef[w]
    for leaf in range(leaf_dev):
        k_high, k_low = split(kernel_of(contract(tgt[leaf, :, 0:rank], far_src[leaf], ((0,), (0,)))))
        far = contract(far_wgt[leaf], k_high, ((1,), (1,))) + contract(far_wgt[leaf], k_low, ((1,), (1,)))
        incoming = halves(far[:8] + far[8:] + pushed_ref[:, leaf * rank : (leaf + 1) * rank])
        base_high, base_low = split(bases_ref[leaf])
        got = jnp.dot(incoming, base_high, preferred_element_type=F32)
        got = got + jnp.dot(incoming, base_low, preferred_element_type=F32)
        flat[:, leaf * leaf_pts : (leaf + 1) * leaf_pts] = out[leaf] + got[:8] + got[8:]

    chunks = flat.shape[1] // 128
    row = row_ids((8, 128))
    lane = lane_ids((8, 128))
    source = [lambda s=s: flat[:, s * 128 : (s + 1) * 128] for s in range(chunks)]
    noise = jnp.zeros((8, 128), F32)
    for r in range(8):
        noise = jnp.where(row == r, noise_ref[r], noise)

    def place(g, sums):
        along, squares = sums
        for h in range(4):
            c = 4 * g + h
            at = pl.ds(pl.multiple_of(c * 128, 128), 128)
            ids = jnp.broadcast_to(inv_ref[pl.ds(c, 1), :], (8, 128))
            (part,) = gather_lanes([source], ids)
            image = part + noise * p_ref[:, at]
            image_ref[:, at] = image
            along, squares = along + res_ref[:, at] * image, squares + image * image
        return along, squares

    zero = jnp.zeros((8, 128), F32)
    along, squares = lax.fori_loop(0, chunks // 4, place, (zero, zero))
    along = jnp.sum(along, axis=1, keepdims=True)
    squares = jnp.sum(squares, axis=1, keepdims=True)
    both = jnp.where(lane == row, along, 0.0) + jnp.where(lane == row + 8, squares, 0.0)
    sums_ref[...] = jnp.broadcast_to(jnp.sum(both, axis=0, keepdims=True), sums_ref.shape)


def update_body(sums_ref, it_ref, p_ref, res_ref, image_ref, new_it_ref, new_res_ref):
    total = jnp.sum(sums_ref[...], axis=0, keepdims=True)
    row = row_ids((8, 128))
    lane = lane_ids((8, 128))
    along = jnp.sum(jnp.where(lane == row, total, 0.0), axis=1, keepdims=True)
    squares = jnp.sum(jnp.where(lane == row + 8, total, 0.0), axis=1, keepdims=True)
    alpha = along / (squares + 1e-06)
    new_it_ref[...] = it_ref[...] + alpha * p_ref[...]
    new_res_ref[...] = res_ref[...] - alpha * image_ref[...]


def shifted(x, axis, by):
    n = lax.axis_size(axis)
    return lax.ppermute(x, axis, [(i, i + by) for i in range(n) if 0 <= i + by < n])


def shards(coords, direction, iterate, residual, order, bases, transfer, near_list, near_count, far_list, device_skel, inv_scale, noise):
    leaf_dev, rank, leaf_pts = bases.shape
    rhs, points = direction.shape
    axes = ("leaf", "tm")
    devices = lax.axis_size("leaf") * lax.axis_size("tm")
    chunks = points // 128
    shape = jax.ShapeDtypeStruct
    by_row = order.reshape(chunks, 128)
    halo, first = pl.pallas_call(
        gather_body,
        in_specs=[ANY] * 4,
        out_specs=[VMEM] * 2,
        out_shape=[shape((13 * leaf_dev, leaf_pts), F32), shape((leaf_dev, 8, 128), F32)],
        scratch_shapes=[
            pltpu.VMEM((chunks, 128), jnp.int32),
            pltpu.VMEM((8, points), F32),
            pltpu.VMEM((rhs, points), F32),
            pltpu.VMEM(bases.shape, F32),
            pltpu.SemaphoreType.DMA((5,)),
        ],
        compiler_params=params(60),
        name="gather",
    )(by_row, coords, direction, bases)
    node, own, inverse = pl.pallas_call(
        node_body,
        in_specs=[VMEM] * 5,
        out_specs=[VMEM] * 3,
        out_shape=[shape((devices, 8, 128), F32), shape((8, 128), F32), shape((chunks, 128), jnp.int32)],
        scratch_shapes=[pltpu.VMEM((8, leaf_dev * rank), F32)],
        compiler_params=params(24),
        cost_estimate=pl.CostEstimate(flops=10**9, bytes_accessed=2**20, transcendentals=0),
        name="node",
    )(by_row, halo, first, transfer[0], device_skel)
    left = shifted(halo, "tm", 1)
    right = shifted(halo, "tm", -1)
    nodes = lax.all_to_all(node, axes, 0, 0)
    left, right, nodes = lax.optimization_barrier((left, right, nodes))
    row = jnp.stack([left, halo, right])
    up = shifted(row, "leaf", 1)
    down = shifted(row, "leaf", -1)
    place = jnp.stack([lax.axis_index("leaf"), lax.axis_index("tm")]).astype(jnp.int32)

    def pipeline(sources):
        return [
            pltpu.VMEM((sources + 1, 32, leaf_pts), BF16),
            pltpu.VMEM((leaf_dev, 32, leaf_pts), BF16),
            pltpu.VMEM((sources + 1, 16, leaf_pts), BF16),
        ]

    buffers = [
        pltpu.VMEM((2, PART, leaf_pts), F32),
        pltpu.VMEM((2, PART, leaf_pts), BF16),
        pltpu.VMEM((2, PART, leaf_pts), BF16),
    ]
    listed = pltpu.SMEM((near_list.size + 4,), jnp.int32)
    close, pushed = pl.pallas_call(
        functools.partial(close_body, lax.axis_size("tm")),
        in_specs=[SMEM] * 4 + [VMEM] * 6,
        out_specs=[VMEM] * 2,
        out_shape=[shape((leaf_dev, rhs, leaf_pts), F32), shape((rhs, leaf_dev * rank), F32)],
        scratch_shapes=[listed]
        + pipeline(3 * leaf_dev)
        + buffers
        + [pltpu.VMEM((32, devices * rank), BF16), pltpu.VMEM((16, devices * rank), BF16)],
        compiler_params=params(24),
        cost_estimate=pl.CostEstimate(flops=10**10, bytes_accessed=2**21, transcendentals=10**7),
        name="close",
    )(near_list, near_count, place, inv_scale, left, halo, right, nodes, own, transfer[0])
    image, sums = pl.pallas_call(
        rest_body,
        in_specs=[SMEM] * 5 + [VMEM] * 11,
        out_specs=[VMEM] * 2,
        out_shape=[shape((rhs, points), F32), shape((devices, 128), F32)],
        scratch_shapes=[listed]
        + pipeline(9 * leaf_dev)
        + [pltpu.VMEM((9 * leaf_dev, 16, rank), BF16)]
        + buffers
        + [
            pltpu.VMEM((leaf_dev, rhs, leaf_pts), F32),
            pltpu.VMEM((rhs, points), F32),
            pltpu.VMEM((leaf_dev, 32, far_list.shape[1] * rank), BF16),
            pltpu.VMEM((leaf_dev, 16, far_list.shape[1] * rank), BF16),
        ],
        compiler_params=params(24),
        name="rest",
    )(near_list, near_count, far_list, inv_scale, noise, left, halo, right, up, down, close, pushed, bases, inverse, direction, residual)
    all_sums = lax.all_to_all(sums, axes, 0, 0, tiled=True)
    return pl.pallas_call(
        update_body,
        in_specs=[VMEM] * 5,
        out_specs=[VMEM] * 2,
        out_shape=[shape((rhs, points), F32)] * 2,
        compiler_params=params(24),
        name="update",
    )(all_sums, iterate, direction, residual, image)


def solution(mesh):
    whole = P(None, ("leaf", "tm"))
    first = P(("leaf", "tm"))
    return jax.shard_map(
        shards,
        mesh=mesh,
        in_specs=(whole,) * 4 + (first,) * 7 + (P(), P()),
        out_specs=(whole, whole),
        check_vma=False,
    )
```

```python
import functools
import math

import jax
import jax.numpy as jnp
from jax import lax
from jax.experimental import pallas as pl
from jax.experimental.pallas import tpu as pltpu
from jax.sharding import PartitionSpec as P

F32 = jnp.float32
BF16 = jnp.bfloat16
EXACT = lax.Precision.HIGHEST
LN2 = math.log(2.0)
LOG2E = 1.0 / LN2
UNIT = math.sqrt(3.0) * LOG2E
FACTOR = -LN2 * math.e
VMEM = pl.BlockSpec(memory_space=pltpu.VMEM)
SMEM = pl.BlockSpec(memory_space=pltpu.SMEM)
ANY = pl.BlockSpec(memory_space=pl.ANY)
PART = 256


def params(mib, **kw):
    return pltpu.CompilerParams(vmem_limit_bytes=mib * 2**20, **kw)


def contract(a, b, dims, precision=None):
    return lax.dot_general(
        a, b, ((dims[0], dims[1]), ((), ())), precision=precision, preferred_element_type=F32
    )


def rounded(x):
    return x.astype(BF16).astype(F32)


def row_ids(shape):
    return lax.broadcasted_iota(jnp.int32, shape, 0)


def lane_ids(shape):
    return lax.broadcasted_iota(jnp.int32, shape, 1)


def features(xx, want_source, want_target):
    row = row_ids(xx.shape)
    high = rounded(xx)
    low = rounded(xx - high)
    held = high + low
    square = held * held
    square = square + pltpu.roll(square, 1, 0)
    norm = square + pltpu.roll(square, 2, 0)
    n0 = rounded(norm)
    rest = norm - n0
    n1 = rounded(rest)
    n2 = rest - n1
    zero = jnp.zeros_like(xx)
    out = []
    if want_source:
        parts = jnp.where(row < 4, high, low)
        tail = jnp.where(row == 0, n0, jnp.where(row == 1, n1, jnp.where(row == 2, n2, jnp.where(row < 6, 1.0, 0.0))))
        out.append(jnp.concatenate([parts, parts, tail, zero], axis=0).astype(BF16))
    if want_target:
        tail = jnp.where(row < 3, 1.0, jnp.where(row == 3, n0, jnp.where(row == 4, n1, jnp.where(row == 5, n2, 0.0))))
        out.append(jnp.concatenate([-2.0 * high, -2.0 * low, tail, zero], axis=0).astype(BF16))
    return out


def halves(w):
    high = rounded(w)
    return jnp.concatenate([high, w - high], axis=0).astype(BF16)


def kernel_of(z):
    z = jnp.maximum(z, 1e-30)
    q = -LOG2E - z * lax.rsqrt(z)
    return q * jnp.exp2(q)


def split(k):
    high = k.astype(BF16)
    return high, (k - high.astype(F32)).astype(BF16)


def gather_lanes(chunks, ids):
    lane = ids & 127
    chunk = ids >> 7
    picked = [None] * len(chunks)
    for s in range(len(chunks[0])):
        here = chunk == s
        for i, source in enumerate(chunks):
            got = jnp.take_along_axis(source[s](), lane, axis=1, mode="promise_in_bounds")
            picked[i] = got if s == 0 else jnp.where(here, got, picked[i])
    return picked


def gather_body(order_hbm, x_hbm, p_hbm, bases_hbm, halo_ref, first_ref, order_ref, xx, p_ref, bases_ref, sems):
    leaf_dev, rank, leaf_pts = bases_ref.shape
    points = p_ref.shape[1]
    chunks = points // 128
    per_leaf = leaf_pts // 128
    moves = [
        pltpu.make_async_copy(source, target, sems.at[i])
        for i, (source, target) in enumerate(
            [
                (order_hbm, order_ref),
                (x_hbm, xx.at[0:4, :]),
                (x_hbm, xx.at[4:8, :]),
                (p_hbm, p_ref),
                (bases_hbm, bases_ref),
            ]
        )
    ]
    for move in moves:
        move.start()
    for move in moves[:4]:
        move.wait()

    def loads(ref):
        return [lambda s=s: ref[:, s * 128 : (s + 1) * 128] for s in range(chunks)]

    def two_leaves(g, _):
        kept = []
        for h in range(2):
            leaf = 2 * g + h
            for j in range(per_leaf):
                ids = order_ref[pl.ds(leaf * per_leaf + j, 1), :]
                got_x, got_p = gather_lanes([loads(xx), loads(p_ref)], jnp.broadcast_to(ids, (8, 128)))
                kept.append(got_x)
                halo_ref[pl.ds(pl.multiple_of(32 + leaf * 8, 8), 8), j * 128 : (j + 1) * 128] = got_p
            first_ref[leaf] = kept[h * per_leaf]
        for j in range(per_leaf):
            both = jnp.where(row_ids((8, 128)) < 4, kept[j], kept[per_leaf + j])
            halo_ref[pl.ds(pl.multiple_of(g * 8, 8), 8), j * 128 : (j + 1) * 128] = both
        return 0

    lax.fori_loop(0, leaf_dev // 2, two_leaves, 0)
    moves[4].wait()
    for leaf in range(leaf_dev):
        coef = contract(halo_ref[32 + leaf * 8 : 40 + leaf * 8, :], bases_ref[leaf], ((1,), (1,)), EXACT)
        halo_ref[96:104, leaf * rank : (leaf + 1) * rank] = coef


def node_body(order_ref, halo_ref, first_ref, transfer_ref, skel_ref, node_ref, own_ref, inv_ref, slot):
    chunks = order_ref.shape[0]
    rank = transfer_ref.shape[0]
    leaf_dev = first_ref.shape[0]
    for leaf in range(leaf_dev):
        slot[:, leaf * rank : (leaf + 1) * rank] = first_ref[leaf][:, :rank]
    weights = contract(halo_ref[96:104, :], transfer_ref[...], ((1,), (1,)), EXACT)
    slots = [lambda s=s: slot[:, s * 128 : (s + 1) * 128] for s in range(leaf_dev * rank // 128)]
    ids = jnp.concatenate([skel_ref[...], skel_ref[...]], axis=1)
    (node_x,) = gather_lanes([slots], jnp.broadcast_to(ids, (8, 128)))
    tile = jnp.concatenate([weights, node_x[:, :rank]], axis=1)
    own_ref[...] = tile
    node_ref[...] = jnp.broadcast_to(tile[None], node_ref.shape)
    tally = jnp.zeros((2 * chunks, 128), F32)
    for c in range(chunks):
        ids = order_ref[c : c + 1, :]
        low = jnp.where(row_ids((128, 128)) == (ids & 127), 1.0, 0.0).astype(BF16)
        row = row_ids((chunks, 128)) == (ids >> 7)
        lane = lane_ids((chunks, 128))
        digit1 = jnp.where(row, (2 * c + (lane >> 6)).astype(F32), 0.0)
        digit0 = jnp.where(row, (lane & 63).astype(F32), 0.0)
        digits = jnp.concatenate([digit1, digit0], axis=0).astype(BF16)
        tally = tally + contract(digits, low, ((1,), (1,)))
    inv_ref[...] = (64.0 * tally[0:chunks] + tally[chunks : 2 * chunks] + 0.5).astype(jnp.int32)


def scale_rows(scale_ref, shape):
    row = row_ids(shape) & 3
    picked = jnp.where(row == 0, scale_ref[0], jnp.where(row == 1, scale_ref[1], jnp.where(row == 2, scale_ref[2], scale_ref[3])))
    return picked * UNIT


def prepare(ref, scale, base, src, wgt=None, tgt=None, coef=None):
    leaf_dev = ref.shape[0] // 13
    width = scale.shape[1]
    row = row_ids(scale.shape)
    for g in range(leaf_dev // 2):
        both = ref[g * 8 : g * 8 + 8, 0:width] * scale
        turned = pltpu.roll(both, 4, 0)
        for h in range(2):
            leaf = 2 * g + h
            xx = jnp.where(row < 4, both, turned) if h == 0 else jnp.where(row < 4, turned, both)
            made = features(xx, True, tgt is not None)
            src[base + leaf, :, 0:width] = made[0]
            if tgt is not None:
                tgt[leaf, :, 0:width] = made[1]
            if wgt is not None:
                wgt[base + leaf] = halves(ref[32 + leaf * 8 : 40 + leaf * 8, :] * FACTOR)
            if coef is not None:
                rank = coef.shape[2]
                coef[base + leaf] = halves(ref[96:104, leaf * rank : (leaf + 1) * rank] * FACTOR)


def list_pairs(near_ref, count_ref, inside, outside, sizes):
    leaf_dev, slots = near_ref.shape

    def leaf_step(leaf, sums):
        def entry(j, sums):
            w = near_ref[leaf, j]
            here = jnp.where(w // leaf_dev == 4, 1, 0)
            code = leaf * 128 + w
            inside[sums[0]] = code
            outside[sums[1]] = code
            return sums[0] + here, sums[1] + 1 - here

        return lax.fori_loop(0, count_ref[leaf], entry, sums)

    sums = lax.fori_loop(0, leaf_dev, leaf_step, (0, 0))
    idle = 9 * leaf_dev
    for extra in range(3):
        inside[sums[0] + extra] = idle
        outside[sums[1] + extra] = idle
    sizes[0], sizes[1] = sums
    return sums[0]


def near_pairs(pairs, n, first, src, tgt, wgt, out, z, high, low):
    parts = wgt.shape[2] // PART

    def where(p):
        return pairs[p] >> 7, (pairs[p] & 127) - first

    def distances(p, c, b):
        leaf, w = where(p)
        z[b] = contract(src[w, :, c * PART : (c + 1) * PART], tgt[leaf], ((0,), (0,)))

    def values(b):
        high[b], low[b] = split(kernel_of(z[b]))

    def product(p, c, b):
        _, w = where(p)
        weight = wgt[w, :, c * PART : (c + 1) * PART]
        got = jnp.dot(weight, high[b], preferred_element_type=F32)
        return got + jnp.dot(weight, low[b], preferred_element_type=F32)

    distances(0, 0, 0)
    distances(0, 1, 1)
    values(0)

    def two_pairs(g, _):
        for h in range(2):
            p = 2 * g + h
            got = None
            for c in range(parts):
                b = c % 2
                values(1 - b)
                mine = product(p, c, b)
                got = mine if got is None else got + mine
                distances(p + (c + 2) // parts, (c + 2) % parts, b)
            leaf, _ = where(p)
            out[leaf] += got[:8] + got[8:]
        return 0

    lax.fori_loop(0, (n + 1) // 2, two_pairs, 0)


def inside_body(near_ref, count_ref, scale_ref, halo_ref, out_ref, pairs_ref, sizes_ref, pairs, src, tgt, wgt, z, high, low):
    leaf_dev, rhs, leaf_pts = out_ref.shape
    n = list_pairs(near_ref, count_ref, pairs, pairs_ref, sizes_ref)
    for extra in range(3):
        pairs[n + extra] = 5 * leaf_dev
    prepare(halo_ref, scale_rows(scale_ref, (8, leaf_pts)), 0, src, wgt, tgt)
    src[leaf_dev] = jnp.zeros(src.shape[1:], BF16)
    wgt[leaf_dev] = jnp.zeros(wgt.shape[1:], BF16)
    out_ref[...] = jnp.zeros_like(out_ref)
    near_pairs(pairs, n, 4 * leaf_dev, src, tgt, wgt, out_ref, z, high, low)


def node_field(tm_size, place_ref, scale, node_ref, own_ref, transfer_ref, node_src, node_wgt):
    devices = node_ref.shape[0]
    rank = own_ref.shape[1] // 2
    lane = lane_ids((8, 128))

    def distant(e):
        far_a = jnp.abs(e // tm_size - place_ref[0]) > 1
        far_b = jnp.abs(e % tm_size - place_ref[1]) > 1
        return jnp.where(far_a | far_b, FACTOR, 0.0)

    def unpack(g, _):
        xs, ws = [], []
        for k in range(4):
            e = 8 * g + 2 * k
            one, two = node_ref[e], node_ref[e + 1]
            xs.append(jnp.where(lane < rank, pltpu.roll(one, rank, 1), two))
            ws.append(jnp.where(lane < rank, one * distant(e), pltpu.roll(two, rank, 1) * distant(e + 1)))
        at = pl.ds(pl.multiple_of(g * 512, 512), 512)
        node_src[:, at] = features(jnp.concatenate(xs, axis=1) * scale, True, False)[0]
        node_wgt[:, at] = halves(jnp.concatenate(ws, axis=1))
        return 0

    lax.fori_loop(0, devices // 8, unpack, 0, unroll=4)
    own_xx = pltpu.roll(own_ref[...], rank, 1) * scale[:, 0 : 2 * rank]
    target = features(own_xx, False, True)[0][:, :rank]
    total = jnp.zeros((16, rank), F32)
    step = 512
    for q in range(0, devices * rank, step):
        z_far = contract(target, node_src[:, q : q + step], ((0,), (0,)))
        k_high, k_low = split(kernel_of(z_far))
        weight = node_wgt[:, q : q + step]
        total = total + contract(weight, k_high, ((1,), (1,)))
        total = total + contract(weight, k_low, ((1,), (1,)))
    return jnp.dot(total[:8] + total[8:], transfer_ref[...], precision=EXACT, preferred_element_type=F32)


def rest_body(tm_size, pairs_ref, sizes_ref, far_ref, place_ref, scale_ref, noise_ref, left_ref, mid_ref, right_ref, up_ref, down_ref, inside_ref, node_ref, own_ref, transfer_ref, bases_ref, inv_ref, p_ref, res_ref, image_ref, sums_ref, src, tgt, wgt, coef, z, high, low, out, flat, far_src, far_wgt, node_src, node_wgt):
    leaf_dev, rank, leaf_pts = bases_ref.shape
    scale = scale_rows(scale_ref, (8, leaf_pts))
    pushed = node_field(tm_size, place_ref, scale, node_ref, own_ref, transfer_ref, node_src, node_wgt)
    idle = 9 * leaf_dev
    src[idle] = jnp.zeros(src.shape[1:], BF16)
    wgt[idle] = jnp.zeros(wgt.shape[1:], BF16)
    for k in range(3):
        prepare(up_ref.at[k], scale, k * leaf_dev, src, wgt, None, coef)
        prepare(down_ref.at[k], scale, (6 + k) * leaf_dev, src, wgt, None, coef)
    prepare(left_ref, scale, 3 * leaf_dev, src, wgt, None, coef)
    prepare(mid_ref, scale, 4 * leaf_dev, src, None, tgt, coef)
    prepare(right_ref, scale, 5 * leaf_dev, src, wgt, None, coef)
    out[...] = inside_ref[...]
    near_pairs(pairs_ref, sizes_ref[1], 0, src, tgt, wgt, out, z, high, low)

    for leaf in range(leaf_dev):
        for j in range(far_ref.shape[1]):
            w = far_ref[leaf, j]
            at = slice(j * rank, (j + 1) * rank)
            far_src[leaf, :, at] = src[w, :, 0:rank]
            far_wgt[leaf, :, at] = coef[w]
    for leaf in range(leaf_dev):
        k_high, k_low = split(kernel_of(contract(tgt[leaf, :, 0:rank], far_src[leaf], ((0,), (0,)))))
        far = contract(far_wgt[leaf], k_high, ((1,), (1,))) + contract(far_wgt[leaf], k_low, ((1,), (1,)))
        incoming = halves(far[:8] + far[8:] + pushed[:, leaf * rank : (leaf + 1) * rank])
        base_high, base_low = split(bases_ref[leaf])
        got = jnp.dot(incoming, base_high, preferred_element_type=F32)
        got = got + jnp.dot(incoming, base_low, preferred_element_type=F32)
        flat[:, leaf * leaf_pts : (leaf + 1) * leaf_pts] = out[leaf] + got[:8] + got[8:]

    chunks = flat.shape[1] // 128
    row = row_ids((8, 128))
    lane = lane_ids((8, 128))
    source = [lambda s=s: flat[:, s * 128 : (s + 1) * 128] for s in range(chunks)]
    noise = jnp.zeros((8, 128), F32)
    for r in range(8):
        noise = jnp.where(row == r, noise_ref[r], noise)

    def place(g, sums):
        along, squares = sums
        for h in range(4):
            c = 4 * g + h
            at = pl.ds(pl.multiple_of(c * 128, 128), 128)
            ids = jnp.broadcast_to(inv_ref[pl.ds(c, 1), :], (8, 128))
            (part,) = gather_lanes([source], ids)
            image = part + noise * p_ref[:, at]
            image_ref[:, at] = image
            along, squares = along + res_ref[:, at] * image, squares + image * image
        return along, squares

    zero = jnp.zeros((8, 128), F32)
    along, squares = lax.fori_loop(0, chunks // 4, place, (zero, zero))
    along = jnp.sum(along, axis=1, keepdims=True)
    squares = jnp.sum(squares, axis=1, keepdims=True)
    both = jnp.where(lane == row, along, 0.0) + jnp.where(lane == row + 8, squares, 0.0)
    sums_ref[...] = jnp.broadcast_to(jnp.sum(both, axis=0, keepdims=True), sums_ref.shape)


def update_body(sums_ref, it_ref, p_ref, res_ref, image_ref, new_it_ref, new_res_ref):
    total = jnp.sum(sums_ref[...], axis=0, keepdims=True)
    row = row_ids((8, 128))
    lane = lane_ids((8, 128))
    along = jnp.sum(jnp.where(lane == row, total, 0.0), axis=1, keepdims=True)
    squares = jnp.sum(jnp.where(lane == row + 8, total, 0.0), axis=1, keepdims=True)
    alpha = along / (squares + 1e-06)
    new_it_ref[...] = it_ref[...] + alpha * p_ref[...]
    new_res_ref[...] = res_ref[...] - alpha * image_ref[...]


def shifted(x, axis, by):
    n = lax.axis_size(axis)
    return lax.ppermute(x, axis, [(i, i + by) for i in range(n) if 0 <= i + by < n])


def shards(coords, direction, iterate, residual, order, bases, transfer, near_list, near_count, far_list, device_skel, inv_scale, noise):
    leaf_dev, rank, leaf_pts = bases.shape
    rhs, points = direction.shape
    axes = ("leaf", "tm")
    devices = lax.axis_size("leaf") * lax.axis_size("tm")
    chunks = points // 128
    shape = jax.ShapeDtypeStruct
    by_row = order.reshape(chunks, 128)
    halo, first = pl.pallas_call(
        gather_body,
        in_specs=[ANY] * 4,
        out_specs=[VMEM] * 2,
        out_shape=[shape((13 * leaf_dev, leaf_pts), F32), shape((leaf_dev, 8, 128), F32)],
        scratch_shapes=[
            pltpu.VMEM((chunks, 128), jnp.int32),
            pltpu.VMEM((8, points), F32),
            pltpu.VMEM((rhs, points), F32),
            pltpu.VMEM(bases.shape, F32),
            pltpu.SemaphoreType.DMA((5,)),
        ],
        compiler_params=params(60),
        name="gather",
    )(by_row, coords, direction, bases)
    node, own, inverse = pl.pallas_call(
        node_body,
        in_specs=[VMEM] * 5,
        out_specs=[VMEM] * 3,
        out_shape=[shape((devices, 8, 128), F32), shape((8, 128), F32), shape((chunks, 128), jnp.int32)],
        scratch_shapes=[pltpu.VMEM((8, leaf_dev * rank), F32)],
        compiler_params=params(24),
        cost_estimate=pl.CostEstimate(flops=10**9, bytes_accessed=2**20, transcendentals=0),
        name="node",
    )(by_row, halo, first, transfer[0], device_skel)
    left = shifted(halo, "tm", 1)
    right = shifted(halo, "tm", -1)

    def pipeline(sources):
        return [
            pltpu.VMEM((sources + 1, 32, leaf_pts), BF16),
            pltpu.VMEM((leaf_dev, 32, leaf_pts), BF16),
            pltpu.VMEM((sources + 1, 16, leaf_pts), BF16),
        ]

    buffers = [
        pltpu.VMEM((2, PART, leaf_pts), F32),
        pltpu.VMEM((2, PART, leaf_pts), BF16),
        pltpu.VMEM((2, PART, leaf_pts), BF16),
    ]
    entries = near_list.size + 4
    inside, pairs, sizes = pl.pallas_call(
        inside_body,
        in_specs=[SMEM] * 3 + [VMEM],
        out_specs=[VMEM, SMEM, SMEM],
        out_shape=[shape((leaf_dev, rhs, leaf_pts), F32), shape((entries,), jnp.int32), shape((2,), jnp.int32)],
        scratch_shapes=[pltpu.SMEM((entries,), jnp.int32)] + pipeline(leaf_dev) + buffers,
        compiler_params=params(24),
        cost_estimate=pl.CostEstimate(flops=10**10, bytes_accessed=2**21, transcendentals=10**7),
        name="inside",
    )(near_list, near_count, inv_scale, halo)
    left, right, inside, node = lax.optimization_barrier((left, right, inside, node))
    nodes = lax.all_to_all(node, axes, 0, 0)
    row = jnp.stack([left, halo, right])
    up = shifted(row, "leaf", 1)
    down = shifted(row, "leaf", -1)
    place = jnp.stack([lax.axis_index("leaf"), lax.axis_index("tm")]).astype(jnp.int32)

    image, sums = pl.pallas_call(
        functools.partial(rest_body, lax.axis_size("tm")),
        in_specs=[SMEM] * 6 + [VMEM] * 13,
        out_specs=[VMEM] * 2,
        out_shape=[shape((rhs, points), F32), shape((devices, 128), F32)],
        scratch_shapes=pipeline(9 * leaf_dev)
        + [pltpu.VMEM((9 * leaf_dev, 16, rank), BF16)]
        + buffers
        + [
            pltpu.VMEM((leaf_dev, rhs, leaf_pts), F32),
            pltpu.VMEM((rhs, points), F32),
            pltpu.VMEM((leaf_dev, 32, far_list.shape[1] * rank), BF16),
            pltpu.VMEM((leaf_dev, 16, far_list.shape[1] * rank), BF16),
            pltpu.VMEM((32, devices * rank), BF16),
            pltpu.VMEM((16, devices * rank), BF16),
        ],
        compiler_params=params(24),
        name="rest",
    )(pairs, sizes, far_list, place, inv_scale, noise, left, halo, right, up, down, inside, nodes, own, transfer[0], bases, inverse, direction, residual)
    all_sums = lax.all_to_all(sums, axes, 0, 0, tiled=True)
    return pl.pallas_call(
        update_body,
        in_specs=[VMEM] * 5,
        out_specs=[VMEM] * 2,
        out_shape=[shape((rhs, points), F32)] * 2,
        compiler_params=params(24),
        name="update",
    )(all_sums, iterate, direction, residual, image)


def solution(mesh):
    whole = P(None, ("leaf", "tm"))
    first = P(("leaf", "tm"))
    return jax.shard_map(
        shards,
        mesh=mesh,
        in_specs=(whole,) * 4 + (first,) * 7 + (P(), P()),
        out_specs=(whole, whole),
        check_vma=False,
    )
```

```python
import functools
import math

import jax
import jax.numpy as jnp
from jax import lax
from jax.experimental import pallas as pl
from jax.experimental.pallas import tpu as pltpu
from jax.sharding import PartitionSpec as P

F32 = jnp.float32
BF16 = jnp.bfloat16
EXACT = lax.Precision.HIGHEST
LN2 = math.log(2.0)
LOG2E = 1.0 / LN2
UNIT = math.sqrt(3.0) * LOG2E
FACTOR = -LN2 * math.e
VMEM = pl.BlockSpec(memory_space=pltpu.VMEM)
SMEM = pl.BlockSpec(memory_space=pltpu.SMEM)
ANY = pl.BlockSpec(memory_space=pl.ANY)
PART = 256


def params(mib, **kw):
    return pltpu.CompilerParams(vmem_limit_bytes=mib * 2**20, **kw)


def contract(a, b, dims, precision=None):
    return lax.dot_general(
        a, b, ((dims[0], dims[1]), ((), ())), precision=precision, preferred_element_type=F32
    )


def rounded(x):
    return x.astype(BF16).astype(F32)


def row_ids(shape):
    return lax.broadcasted_iota(jnp.int32, shape, 0)


def lane_ids(shape):
    return lax.broadcasted_iota(jnp.int32, shape, 1)


def features(xx, want_source, want_target):
    row = row_ids(xx.shape)
    high = rounded(xx)
    low = rounded(xx - high)
    held = high + low
    square = held * held
    square = square + pltpu.roll(square, 1, 0)
    norm = square + pltpu.roll(square, 2, 0)
    n0 = rounded(norm)
    rest = norm - n0
    n1 = rounded(rest)
    n2 = rest - n1
    zero = jnp.zeros_like(xx)
    out = []
    if want_source:
        parts = jnp.where(row < 4, high, low)
        tail = jnp.where(row == 0, n0, jnp.where(row == 1, n1, jnp.where(row == 2, n2, jnp.where(row < 6, 1.0, 0.0))))
        out.append(jnp.concatenate([parts, parts, tail, zero], axis=0).astype(BF16))
    if want_target:
        tail = jnp.where(row < 3, 1.0, jnp.where(row == 3, n0, jnp.where(row == 4, n1, jnp.where(row == 5, n2, 0.0))))
        out.append(jnp.concatenate([-2.0 * high, -2.0 * low, tail, zero], axis=0).astype(BF16))
    return out


def halves(w):
    high = rounded(w)
    return jnp.concatenate([high, w - high], axis=0).astype(BF16)


def kernel_of(z):
    z = jnp.maximum(z, 1e-30)
    q = -LOG2E - z * lax.rsqrt(z)
    return q * jnp.exp2(q)


def split(k):
    high = k.astype(BF16)
    return high, (k - high.astype(F32)).astype(BF16)


def gather_lanes(chunks, ids):
    lane = ids & 127
    chunk = ids >> 7
    picked = [None] * len(chunks)
    for s in range(len(chunks[0])):
        here = chunk == s
        for i, source in enumerate(chunks):
            got = jnp.take_along_axis(source[s](), lane, axis=1, mode="promise_in_bounds")
            picked[i] = got if s == 0 else jnp.where(here, got, picked[i])
    return picked


def gather_body(order_hbm, x_hbm, p_hbm, bases_hbm, halo_ref, first_ref, order_ref, xx, p_ref, bases_ref, sems):
    leaf_dev, rank, leaf_pts = bases_ref.shape
    points = p_ref.shape[1]
    chunks = points // 128
    per_leaf = leaf_pts // 128
    moves = [
        pltpu.make_async_copy(source, target, sems.at[i])
        for i, (source, target) in enumerate(
            [
                (order_hbm, order_ref),
                (x_hbm, xx.at[0:4, :]),
                (x_hbm, xx.at[4:8, :]),
                (p_hbm, p_ref),
                (bases_hbm, bases_ref),
            ]
        )
    ]
    for move in moves:
        move.start()
    for move in moves[:4]:
        move.wait()

    def loads(ref):
        return [lambda s=s: ref[:, s * 128 : (s + 1) * 128] for s in range(chunks)]

    def two_leaves(g, _):
        kept = []
        for h in range(2):
            leaf = 2 * g + h
            for j in range(per_leaf):
                ids = order_ref[pl.ds(leaf * per_leaf + j, 1), :]
                got_x, got_p = gather_lanes([loads(xx), loads(p_ref)], jnp.broadcast_to(ids, (8, 128)))
                kept.append(got_x)
                halo_ref[pl.ds(pl.multiple_of(32 + leaf * 8, 8), 8), j * 128 : (j + 1) * 128] = got_p
            first_ref[leaf] = kept[h * per_leaf]
        for j in range(per_leaf):
            both = jnp.where(row_ids((8, 128)) < 4, kept[j], kept[per_leaf + j])
            halo_ref[pl.ds(pl.multiple_of(g * 8, 8), 8), j * 128 : (j + 1) * 128] = both
        return 0

    lax.fori_loop(0, leaf_dev // 2, two_leaves, 0)
    moves[4].wait()
    for leaf in range(leaf_dev):
        coef = contract(halo_ref[32 + leaf * 8 : 40 + leaf * 8, :], bases_ref[leaf], ((1,), (1,)), EXACT)
        halo_ref[96:104, leaf * rank : (leaf + 1) * rank] = coef


def node_work(order_ref, halo_ref, first_ref, transfer_ref, skel_ref, node_ref, own_ref, inv_ref, slot):
    chunks = order_ref.shape[0]
    rank = transfer_ref.shape[0]
    leaf_dev = first_ref.shape[0]
    for leaf in range(leaf_dev):
        slot[:, leaf * rank : (leaf + 1) * rank] = first_ref[leaf][:, :rank]
    weights = contract(halo_ref[96:104, :], transfer_ref[...], ((1,), (1,)), EXACT)
    slots = [lambda s=s: slot[:, s * 128 : (s + 1) * 128] for s in range(leaf_dev * rank // 128)]
    ids = jnp.concatenate([skel_ref[...], skel_ref[...]], axis=1)
    (node_x,) = gather_lanes([slots], jnp.broadcast_to(ids, (8, 128)))
    tile = jnp.concatenate([weights, node_x[:, :rank]], axis=1)
    own_ref[...] = tile
    node_ref[...] = jnp.broadcast_to(tile[None], node_ref.shape)
    tally = jnp.zeros((2 * chunks, 128), F32)
    for c in range(chunks):
        ids = order_ref[c : c + 1, :]
        low = jnp.where(row_ids((128, 128)) == (ids & 127), 1.0, 0.0).astype(BF16)
        row = row_ids((chunks, 128)) == (ids >> 7)
        lane = lane_ids((chunks, 128))
        digit1 = jnp.where(row, (2 * c + (lane >> 6)).astype(F32), 0.0)
        digit0 = jnp.where(row, (lane & 63).astype(F32), 0.0)
        digits = jnp.concatenate([digit1, digit0], axis=0).astype(BF16)
        tally = tally + contract(digits, low, ((1,), (1,)))
    inv_ref[...] = (64.0 * tally[0:chunks] + tally[chunks : 2 * chunks] + 0.5).astype(jnp.int32)


def scale_rows(scale_ref, shape):
    row = row_ids(shape) & 3
    picked = jnp.where(row == 0, scale_ref[0], jnp.where(row == 1, scale_ref[1], jnp.where(row == 2, scale_ref[2], scale_ref[3])))
    return picked * UNIT


def prepare(ref, scale, base, src, wgt=None, tgt=None, coef=None):
    leaf_dev = ref.shape[0] // 13
    width = scale.shape[1]
    row = row_ids(scale.shape)
    for g in range(leaf_dev // 2):
        both = ref[g * 8 : g * 8 + 8, 0:width] * scale
        turned = pltpu.roll(both, 4, 0)
        for h in range(2):
            leaf = 2 * g + h
            xx = jnp.where(row < 4, both, turned) if h == 0 else jnp.where(row < 4, turned, both)
            made = features(xx, True, tgt is not None)
            src[base + leaf, :, 0:width] = made[0]
            if tgt is not None:
                tgt[leaf, :, 0:width] = made[1]
            if wgt is not None:
                wgt[base + leaf] = halves(ref[32 + leaf * 8 : 40 + leaf * 8, :] * FACTOR)
            if coef is not None:
                rank = coef.shape[2]
                coef[base + leaf] = halves(ref[96:104, leaf * rank : (leaf + 1) * rank] * FACTOR)


def list_pairs(near_ref, count_ref, inside, outside, sizes):
    leaf_dev, slots = near_ref.shape

    def leaf_step(leaf, sums):
        def entry(j, sums):
            w = near_ref[leaf, j]
            here = jnp.where(w // leaf_dev == 4, 1, 0)
            code = leaf * 128 + w
            inside[sums[0]] = code
            outside[sums[1]] = code
            return sums[0] + here, sums[1] + 1 - here

        return lax.fori_loop(0, count_ref[leaf], entry, sums)

    sums = lax.fori_loop(0, leaf_dev, leaf_step, (0, 0))
    idle = 9 * leaf_dev
    for extra in range(3):
        inside[sums[0] + extra] = idle
        outside[sums[1] + extra] = idle
    sizes[0], sizes[1] = sums
    return sums[0]


def near_pairs(pairs, n, first, src, tgt, wgt, out, z, high, low):
    parts = wgt.shape[2] // PART

    def where(p):
        return pairs[p] >> 7, (pairs[p] & 127) - first

    def distances(p, c, b):
        leaf, w = where(p)
        z[b] = contract(src[w, :, c * PART : (c + 1) * PART], tgt[leaf], ((0,), (0,)))

    def values(b):
        high[b], low[b] = split(kernel_of(z[b]))

    def product(p, c, b):
        _, w = where(p)
        weight = wgt[w, :, c * PART : (c + 1) * PART]
        got = jnp.dot(weight, high[b], preferred_element_type=F32)
        return got + jnp.dot(weight, low[b], preferred_element_type=F32)

    distances(0, 0, 0)
    distances(0, 1, 1)
    values(0)

    def two_pairs(g, _):
        for h in range(2):
            p = 2 * g + h
            got = None
            for c in range(parts):
                b = c % 2
                values(1 - b)
                mine = product(p, c, b)
                got = mine if got is None else got + mine
                distances(p + (c + 2) // parts, (c + 2) % parts, b)
            leaf, _ = where(p)
            out[leaf] += got[:8] + got[8:]
        return 0

    lax.fori_loop(0, (n + 1) // 2, two_pairs, 0)


def inside_body(near_ref, count_ref, scale_ref, halo_hbm, first_ref, order_ref, transfer_ref, skel_ref, out_ref, node_ref, own_ref, inv_ref, pairs_ref, sizes_ref, pairs, halo_ref, slot, src, tgt, wgt, z, high, low, sem):
    leaf_dev, rhs, leaf_pts = out_ref.shape
    move = pltpu.make_async_copy(halo_hbm, halo_ref, sem)
    move.start()
    n = list_pairs(near_ref, count_ref, pairs, pairs_ref, sizes_ref)
    for extra in range(3):
        pairs[n + extra] = 5 * leaf_dev
    src[leaf_dev] = jnp.zeros(src.shape[1:], BF16)
    wgt[leaf_dev] = jnp.zeros(wgt.shape[1:], BF16)
    out_ref[...] = jnp.zeros_like(out_ref)
    move.wait()
    node_work(order_ref, halo_ref, first_ref, transfer_ref, skel_ref, node_ref, own_ref, inv_ref, slot)
    prepare(halo_ref, scale_rows(scale_ref, (8, leaf_pts)), 0, src, wgt, tgt)
    near_pairs(pairs, n, 4 * leaf_dev, src, tgt, wgt, out_ref, z, high, low)


def node_field(tm_size, place_ref, scale, node_ref, own_ref, transfer_ref, node_src, node_wgt):
    devices = node_ref.shape[0]
    rank = own_ref.shape[1] // 2
    lane = lane_ids((8, 128))

    def distant(e):
        far_a = jnp.abs(e // tm_size - place_ref[0]) > 1
        far_b = jnp.abs(e % tm_size - place_ref[1]) > 1
        return jnp.where(far_a | far_b, FACTOR, 0.0)

    def unpack(g, _):
        xs, ws = [], []
        for k in range(4):
            e = 8 * g + 2 * k
            one, two = node_ref[e], node_ref[e + 1]
            xs.append(jnp.where(lane < rank, pltpu.roll(one, rank, 1), two))
            ws.append(jnp.where(lane < rank, one * distant(e), pltpu.roll(two, rank, 1) * distant(e + 1)))
        at = pl.ds(pl.multiple_of(g * 512, 512), 512)
        node_src[:, at] = features(jnp.concatenate(xs, axis=1) * scale, True, False)[0]
        node_wgt[:, at] = halves(jnp.concatenate(ws, axis=1))
        return 0

    lax.fori_loop(0, devices // 8, unpack, 0, unroll=4)
    own_xx = pltpu.roll(own_ref[...], rank, 1) * scale[:, 0 : 2 * rank]
    target = features(own_xx, False, True)[0][:, :rank]
    total = jnp.zeros((16, rank), F32)
    step = 512
    for q in range(0, devices * rank, step):
        z_far = contract(target, node_src[:, q : q + step], ((0,), (0,)))
        k_high, k_low = split(kernel_of(z_far))
        weight = node_wgt[:, q : q + step]
        total = total + contract(weight, k_high, ((1,), (1,)))
        total = total + contract(weight, k_low, ((1,), (1,)))
    return jnp.dot(total[:8] + total[8:], transfer_ref[...], precision=EXACT, preferred_element_type=F32)


def outside_body(pairs_ref, sizes_ref, scale_ref, left_ref, mid_ref, right_ref, up_ref, down_ref, inside_ref, out_ref, src, tgt, wgt, z, high, low):
    leaf_dev, rhs, leaf_pts = out_ref.shape
    scale = scale_rows(scale_ref, (8, leaf_pts))
    idle = 9 * leaf_dev
    src[idle] = jnp.zeros(src.shape[1:], BF16)
    wgt[idle] = jnp.zeros(wgt.shape[1:], BF16)
    for k in range(3):
        prepare(up_ref.at[k], scale, k * leaf_dev, src, wgt)
        prepare(down_ref.at[k], scale, (6 + k) * leaf_dev, src, wgt)
    prepare(left_ref, scale, 3 * leaf_dev, src, wgt)
    prepare(mid_ref, scale, 4 * leaf_dev, src, None, tgt)
    prepare(right_ref, scale, 5 * leaf_dev, src, wgt)
    out_ref[...] = inside_ref[...]
    near_pairs(pairs_ref, sizes_ref[1], 0, src, tgt, wgt, out_ref, z, high, low)


def tail_body(tm_size, far_ref, place_ref, scale_ref, noise_ref, left_ref, mid_ref, right_ref, up_ref, down_ref, near_ref, node_ref, own_ref, transfer_ref, bases_ref, inv_ref, p_ref, res_ref, image_ref, sums_ref, src, tgt, coef, flat, far_src, far_wgt, node_src, node_wgt):
    leaf_dev, rank, leaf_pts = bases_ref.shape
    scale = scale_rows(scale_ref, (8, 4 * 128))
    pushed = node_field(tm_size, place_ref, scale, node_ref, own_ref, transfer_ref, node_src, node_wgt)
    brief = scale[:, :128]
    for k in range(3):
        prepare(up_ref.at[k], brief, k * leaf_dev, src, None, None, coef)
        prepare(down_ref.at[k], brief, (6 + k) * leaf_dev, src, None, None, coef)
    prepare(left_ref, brief, 3 * leaf_dev, src, None, None, coef)
    prepare(mid_ref, brief, 4 * leaf_dev, src, None, tgt, coef)
    prepare(right_ref, brief, 5 * leaf_dev, src, None, None, coef)
    for leaf in range(leaf_dev):
        for j in range(far_ref.shape[1]):
            w = far_ref[leaf, j]
            at = slice(j * rank, (j + 1) * rank)
            far_src[leaf, :, at] = src[w, :, 0:rank]
            far_wgt[leaf, :, at] = coef[w]
    for leaf in range(leaf_dev):
        k_high, k_low = split(kernel_of(contract(tgt[leaf, :, 0:rank], far_src[leaf], ((0,), (0,)))))
        far = contract(far_wgt[leaf], k_high, ((1,), (1,))) + contract(far_wgt[leaf], k_low, ((1,), (1,)))
        incoming = halves(far[:8] + far[8:] + pushed[:, leaf * rank : (leaf + 1) * rank])
        base_high, base_low = split(bases_ref[leaf])
        got = jnp.dot(incoming, base_high, preferred_element_type=F32)
        got = got + jnp.dot(incoming, base_low, preferred_element_type=F32)
        flat[:, leaf * leaf_pts : (leaf + 1) * leaf_pts] = near_ref[leaf] + got[:8] + got[8:]

    chunks = flat.shape[1] // 128
    row = row_ids((8, 128))
    lane = lane_ids((8, 128))
    source = [lambda s=s: flat[:, s * 128 : (s + 1) * 128] for s in range(chunks)]
    noise = jnp.zeros((8, 128), F32)
    for r in range(8):
        noise = jnp.where(row == r, noise_ref[r], noise)

    def place(g, sums):
        along, squares = sums
        for h in range(4):
            c = 4 * g + h
            at = pl.ds(pl.multiple_of(c * 128, 128), 128)
            ids = jnp.broadcast_to(inv_ref[pl.ds(c, 1), :], (8, 128))
            (part,) = gather_lanes([source], ids)
            image = part + noise * p_ref[:, at]
            image_ref[:, at] = image
            along, squares = along + res_ref[:, at] * image, squares + image * image
        return along, squares

    zero = jnp.zeros((8, 128), F32)
    along, squares = lax.fori_loop(0, chunks // 4, place, (zero, zero))
    along = jnp.sum(along, axis=1, keepdims=True)
    squares = jnp.sum(squares, axis=1, keepdims=True)
    both = jnp.where(lane == row, along, 0.0) + jnp.where(lane == row + 8, squares, 0.0)
    sums_ref[...] = jnp.broadcast_to(jnp.sum(both, axis=0, keepdims=True), sums_ref.shape)


def update_body(sums_ref, it_ref, p_ref, res_ref, image_ref, new_it_ref, new_res_ref):
    total = jnp.sum(sums_ref[...], axis=0, keepdims=True)
    row = row_ids((8, 128))
    lane = lane_ids((8, 128))
    along = jnp.sum(jnp.where(lane == row, total, 0.0), axis=1, keepdims=True)
    squares = jnp.sum(jnp.where(lane == row + 8, total, 0.0), axis=1, keepdims=True)
    alpha = along / (squares + 1e-06)
    new_it_ref[...] = it_ref[...] + alpha * p_ref[...]
    new_res_ref[...] = res_ref[...] - alpha * image_ref[...]


def shifted(x, axis, by):
    n = lax.axis_size(axis)
    return lax.ppermute(x, axis, [(i, i + by) for i in range(n) if 0 <= i + by < n])


def shards(coords, direction, iterate, residual, order, bases, transfer, near_list, near_count, far_list, device_skel, inv_scale, noise):
    leaf_dev, rank, leaf_pts = bases.shape
    rhs, points = direction.shape
    axes = ("leaf", "tm")
    devices = lax.axis_size("leaf") * lax.axis_size("tm")
    chunks = points // 128
    shape = jax.ShapeDtypeStruct
    by_row = order.reshape(chunks, 128)
    halo, first = pl.pallas_call(
        gather_body,
        in_specs=[ANY] * 4,
        out_specs=[VMEM] * 2,
        out_shape=[shape((13 * leaf_dev, leaf_pts), F32), shape((leaf_dev, 8, 128), F32)],
        scratch_shapes=[
            pltpu.VMEM((chunks, 128), jnp.int32),
            pltpu.VMEM((8, points), F32),
            pltpu.VMEM((rhs, points), F32),
            pltpu.VMEM(bases.shape, F32),
            pltpu.SemaphoreType.DMA((5,)),
        ],
        compiler_params=params(60),
        name="gather",
    )(by_row, coords, direction, bases)
    left = shifted(halo, "tm", 1)
    right = shifted(halo, "tm", -1)

    def pipeline(sources):
        return [
            pltpu.VMEM((sources + 1, 32, leaf_pts), BF16),
            pltpu.VMEM((leaf_dev, 32, leaf_pts), BF16),
            pltpu.VMEM((sources + 1, 16, leaf_pts), BF16),
        ]

    buffers = [
        pltpu.VMEM((2, PART, leaf_pts), F32),
        pltpu.VMEM((2, PART, leaf_pts), BF16),
        pltpu.VMEM((2, PART, leaf_pts), BF16),
    ]
    entries = near_list.size + 4
    inside, node, own, inverse, pairs, sizes = pl.pallas_call(
        inside_body,
        in_specs=[SMEM] * 3 + [ANY] + [VMEM] * 4,
        out_specs=[VMEM] * 4 + [SMEM] * 2,
        out_shape=[
            shape((leaf_dev, rhs, leaf_pts), F32),
            shape((devices, 8, 128), F32),
            shape((8, 128), F32),
            shape((chunks, 128), jnp.int32),
            shape((entries,), jnp.int32),
            shape((2,), jnp.int32),
        ],
        scratch_shapes=[
            pltpu.SMEM((entries,), jnp.int32),
            pltpu.VMEM(halo.shape, F32),
            pltpu.VMEM((8, leaf_dev * rank), F32),
        ]
        + pipeline(leaf_dev)
        + buffers
        + [pltpu.SemaphoreType.DMA(())],
        compiler_params=params(24),
        cost_estimate=pl.CostEstimate(flops=10**10, bytes_accessed=2**21, transcendentals=10**7),
        name="inside",
    )(near_list, near_count, inv_scale, halo, first, by_row, transfer[0], device_skel)
    left, right, inside, node = lax.optimization_barrier((left, right, inside, node))
    nodes = lax.all_to_all(node, axes, 0, 0)
    row = jnp.stack([left, halo, right])
    up = shifted(row, "leaf", 1)
    down = shifted(row, "leaf", -1)
    place = jnp.stack([lax.axis_index("leaf"), lax.axis_index("tm")]).astype(jnp.int32)

    near = pl.pallas_call(
        outside_body,
        in_specs=[SMEM] * 3 + [VMEM] * 6,
        out_specs=VMEM,
        out_shape=shape((leaf_dev, rhs, leaf_pts), F32),
        scratch_shapes=pipeline(9 * leaf_dev) + buffers,
        compiler_params=params(24),
        cost_estimate=pl.CostEstimate(flops=3 * 10**10, bytes_accessed=2**21, transcendentals=3 * 10**7),
        name="outside",
    )(pairs, sizes, inv_scale, left, halo, right, up, down, inside)
    image, sums = pl.pallas_call(
        functools.partial(tail_body, lax.axis_size("tm")),
        in_specs=[SMEM] * 4 + [VMEM] * 13,
        out_specs=[VMEM] * 2,
        out_shape=[shape((rhs, points), F32), shape((devices, 128), F32)],
        scratch_shapes=[
            pltpu.VMEM((9 * leaf_dev, 32, 128), BF16),
            pltpu.VMEM((leaf_dev, 32, 128), BF16),
            pltpu.VMEM((9 * leaf_dev, 16, rank), BF16),
            pltpu.VMEM((rhs, points), F32),
            pltpu.VMEM((leaf_dev, 32, far_list.shape[1] * rank), BF16),
            pltpu.VMEM((leaf_dev, 16, far_list.shape[1] * rank), BF16),
            pltpu.VMEM((32, devices * rank), BF16),
            pltpu.VMEM((16, devices * rank), BF16),
        ],
        compiler_params=params(24),
        name="tail",
    )(far_list, place, inv_scale, noise, left, halo, right, up, down, near, nodes, own, transfer[0], bases, inverse, direction, residual)
    all_sums = lax.all_to_all(sums, axes, 0, 0, tiled=True)
    return pl.pallas_call(
        update_body,
        in_specs=[VMEM] * 5,
        out_specs=[VMEM] * 2,
        out_shape=[shape((rhs, points), F32)] * 2,
        compiler_params=params(24),
        name="update",
    )(all_sums, iterate, direction, residual, image)


def solution(mesh):
    whole = P(None, ("leaf", "tm"))
    first = P(("leaf", "tm"))
    return jax.shard_map(
        shards,
        mesh=mesh,
        in_specs=(whole,) * 4 + (first,) * 7 + (P(), P()),
        out_specs=(whole, whole),
        check_vma=False,
    )
```

```python
import functools
import math

import jax
import jax.numpy as jnp
from jax import lax
from jax.experimental import pallas as pl
from jax.experimental.pallas import tpu as pltpu
from jax.sharding import PartitionSpec as P

F32 = jnp.float32
BF16 = jnp.bfloat16
EXACT = lax.Precision.HIGHEST
LN2 = math.log(2.0)
LOG2E = 1.0 / LN2
UNIT = math.sqrt(3.0) * LOG2E
FACTOR = -LN2 * math.e
VMEM = pl.BlockSpec(memory_space=pltpu.VMEM)
SMEM = pl.BlockSpec(memory_space=pltpu.SMEM)
ANY = pl.BlockSpec(memory_space=pl.ANY)
PART = 256
FIRST_PAIRS = 10


def params(mib, **kw):
    return pltpu.CompilerParams(vmem_limit_bytes=mib * 2**20, **kw)


def contract(a, b, dims, precision=None):
    return lax.dot_general(
        a, b, ((dims[0], dims[1]), ((), ())), precision=precision, preferred_element_type=F32
    )


def rounded(x):
    return x.astype(BF16).astype(F32)


def row_ids(shape):
    return lax.broadcasted_iota(jnp.int32, shape, 0)


def lane_ids(shape):
    return lax.broadcasted_iota(jnp.int32, shape, 1)


def features(xx, want_source, want_target):
    row = row_ids(xx.shape)
    high = rounded(xx)
    low = rounded(xx - high)
    held = high + low
    square = held * held
    square = square + pltpu.roll(square, 1, 0)
    norm = square + pltpu.roll(square, 2, 0)
    n0 = rounded(norm)
    rest = norm - n0
    n1 = rounded(rest)
    n2 = rest - n1
    zero = jnp.zeros_like(xx)
    out = []
    if want_source:
        parts = jnp.where(row < 4, high, low)
        tail = jnp.where(row == 0, n0, jnp.where(row == 1, n1, jnp.where(row == 2, n2, jnp.where(row < 6, 1.0, 0.0))))
        out.append(jnp.concatenate([parts, parts, tail, zero], axis=0).astype(BF16))
    if want_target:
        tail = jnp.where(row < 3, 1.0, jnp.where(row == 3, n0, jnp.where(row == 4, n1, jnp.where(row == 5, n2, 0.0))))
        out.append(jnp.concatenate([-2.0 * high, -2.0 * low, tail, zero], axis=0).astype(BF16))
    return out


def halves(w):
    high = rounded(w)
    return jnp.concatenate([high, w - high], axis=0).astype(BF16)


def kernel_of(z):
    z = jnp.maximum(z, 1e-30)
    q = -LOG2E - z * lax.rsqrt(z)
    return q * jnp.exp2(q)


def split(k):
    high = k.astype(BF16)
    return high, (k - high.astype(F32)).astype(BF16)


def gather_lanes(chunks, ids):
    lane = ids & 127
    chunk = ids >> 7
    picked = [None] * len(chunks)
    for s in range(len(chunks[0])):
        here = chunk == s
        for i, source in enumerate(chunks):
            got = jnp.take_along_axis(source[s](), lane, axis=1, mode="promise_in_bounds")
            picked[i] = got if s == 0 else jnp.where(here, got, picked[i])
    return picked


def gather_body(order_hbm, x_hbm, p_hbm, bases_hbm, halo_ref, order_ref, xx, p_ref, bases_ref, sems):
    leaf_dev, rank, leaf_pts = bases_ref.shape
    points = p_ref.shape[1]
    chunks = points // 128
    per_leaf = leaf_pts // 128
    moves = [
        pltpu.make_async_copy(source, target, sems.at[i])
        for i, (source, target) in enumerate(
            [
                (order_hbm, order_ref),
                (x_hbm, xx.at[0:4, :]),
                (x_hbm, xx.at[4:8, :]),
                (p_hbm, p_ref),
                (bases_hbm, bases_ref),
            ]
        )
    ]
    for move in moves:
        move.start()
    for move in moves[:4]:
        move.wait()

    def loads(ref):
        return [lambda s=s: ref[:, s * 128 : (s + 1) * 128] for s in range(chunks)]

    def two_leaves(g, _):
        kept = []
        for h in range(2):
            leaf = 2 * g + h
            for j in range(per_leaf):
                ids = order_ref[pl.ds(leaf * per_leaf + j, 1), :]
                got_x, got_p = gather_lanes([loads(xx), loads(p_ref)], jnp.broadcast_to(ids, (8, 128)))
                kept.append(got_x)
                halo_ref[pl.ds(pl.multiple_of(32 + leaf * 8, 8), 8), j * 128 : (j + 1) * 128] = got_p
        for j in range(per_leaf):
            both = jnp.where(row_ids((8, 128)) < 4, kept[j], kept[per_leaf + j])
            halo_ref[pl.ds(pl.multiple_of(g * 8, 8), 8), j * 128 : (j + 1) * 128] = both
        return 0

    lax.fori_loop(0, leaf_dev // 2, two_leaves, 0)
    moves[4].wait()
    for leaf in range(leaf_dev):
        coef = contract(halo_ref[32 + leaf * 8 : 40 + leaf * 8, :], bases_ref[leaf], ((1,), (1,)), EXACT)
        halo_ref[96:104, leaf * rank : (leaf + 1) * rank] = coef


def node_work(order_ref, halo_ref, transfer_ref, skel_ref, node_ref, own_ref, inv_ref, slot):
    chunks = order_ref.shape[0]
    rank = transfer_ref.shape[0]
    leaf_dev = halo_ref.shape[0] // 13
    upper = row_ids((8, 128)) < 4
    for g in range(leaf_dev // 2):
        both = halo_ref[g * 8 : g * 8 + 8, 0:128]
        turned = pltpu.roll(both, 4, 0)
        slot[:, 2 * g * rank : (2 * g + 1) * rank] = jnp.where(upper, both, turned)[:, :rank]
        slot[:, (2 * g + 1) * rank : (2 * g + 2) * rank] = jnp.where(upper, turned, both)[:, :rank]
    weights = contract(halo_ref[96:104, :], transfer_ref[...], ((1,), (1,)), EXACT)
    slots = [lambda s=s: slot[:, s * 128 : (s + 1) * 128] for s in range(leaf_dev * rank // 128)]
    ids = jnp.concatenate([skel_ref[...], skel_ref[...]], axis=1)
    (node_x,) = gather_lanes([slots], jnp.broadcast_to(ids, (8, 128)))
    tile = jnp.concatenate([weights, node_x[:, :rank]], axis=1)
    own_ref[...] = tile
    node_ref[...] = jnp.broadcast_to(tile[None], node_ref.shape)
    tally = jnp.zeros((2 * chunks, 128), F32)
    for c in range(chunks):
        ids = order_ref[c : c + 1, :]
        low = jnp.where(row_ids((128, 128)) == (ids & 127), 1.0, 0.0).astype(BF16)
        row = row_ids((chunks, 128)) == (ids >> 7)
        lane = lane_ids((chunks, 128))
        digit1 = jnp.where(row, (2 * c + (lane >> 6)).astype(F32), 0.0)
        digit0 = jnp.where(row, (lane & 63).astype(F32), 0.0)
        digits = jnp.concatenate([digit1, digit0], axis=0).astype(BF16)
        tally = tally + contract(digits, low, ((1,), (1,)))
    inv_ref[...] = (64.0 * tally[0:chunks] + tally[chunks : 2 * chunks] + 0.5).astype(jnp.int32)


def scale_rows(scale_ref, shape):
    row = row_ids(shape) & 3
    picked = jnp.where(row == 0, scale_ref[0], jnp.where(row == 1, scale_ref[1], jnp.where(row == 2, scale_ref[2], scale_ref[3])))
    return picked * UNIT


def prepare(ref, scale, base, src, wgt=None, tgt=None, coef=None):
    leaf_dev = ref.shape[0] // 13
    width = scale.shape[1]
    row = row_ids(scale.shape)
    for g in range(leaf_dev // 2):
        both = ref[g * 8 : g * 8 + 8, 0:width] * scale
        turned = pltpu.roll(both, 4, 0)
        for h in range(2):
            leaf = 2 * g + h
            xx = jnp.where(row < 4, both, turned) if h == 0 else jnp.where(row < 4, turned, both)
            made = features(xx, True, tgt is not None)
            src[base + leaf, :, 0:width] = made[0]
            if tgt is not None:
                tgt[leaf, :, 0:width] = made[1]
            if wgt is not None:
                wgt[base + leaf] = halves(ref[32 + leaf * 8 : 40 + leaf * 8, :] * FACTOR)
            if coef is not None:
                rank = coef.shape[2]
                coef[base + leaf] = halves(ref[96:104, leaf * rank : (leaf + 1) * rank] * FACTOR)


def list_pairs(near_ref, count_ref, inside, outside, sizes):
    leaf_dev, slots = near_ref.shape

    def leaf_step(leaf, sums):
        def entry(j, sums):
            w = near_ref[leaf, j]
            here = jnp.where((w // leaf_dev == 4) & (sums[0] < FIRST_PAIRS), 1, 0)
            code = leaf * 128 + w
            inside[sums[0]] = code
            outside[sums[1]] = code
            return sums[0] + here, sums[1] + 1 - here

        return lax.fori_loop(0, count_ref[leaf], entry, sums)

    sums = lax.fori_loop(0, leaf_dev, leaf_step, (0, 0))
    idle = 9 * leaf_dev
    for extra in range(3):
        inside[sums[0] + extra] = idle
        outside[sums[1] + extra] = idle
    sizes[0], sizes[1] = sums
    return sums[0]


def near_pairs(pairs, n, first, src, tgt, wgt, out, z, high, low):
    parts = wgt.shape[2] // PART

    def where(p):
        return pairs[p] >> 7, (pairs[p] & 127) - first

    def distances(p, c, b):
        leaf, w = where(p)
        z[b] = contract(src[w, :, c * PART : (c + 1) * PART], tgt[leaf], ((0,), (0,)))

    def values(b):
        high[b], low[b] = split(kernel_of(z[b]))

    def product(p, c, b):
        _, w = where(p)
        weight = wgt[w, :, c * PART : (c + 1) * PART]
        got = jnp.dot(weight, high[b], preferred_element_type=F32)
        return got + jnp.dot(weight, low[b], preferred_element_type=F32)

    distances(0, 0, 0)
    distances(0, 1, 1)
    values(0)

    def two_pairs(g, _):
        for h in range(2):
            p = 2 * g + h
            got = None
            for c in range(parts):
                b = c % 2
                values(1 - b)
                mine = product(p, c, b)
                got = mine if got is None else got + mine
                distances(p + (c + 2) // parts, (c + 2) % parts, b)
            leaf, _ = where(p)
            out[leaf] += got[:8] + got[8:]
        return 0

    lax.fori_loop(0, (n + 1) // 2, two_pairs, 0)


def inside_body(near_ref, count_ref, scale_ref, halo_hbm, order_ref, transfer_ref, skel_ref, out_ref, node_ref, own_ref, inv_ref, pairs_ref, sizes_ref, pairs, halo_ref, slot, src, tgt, wgt, z, high, low, sem):
    leaf_dev, rhs, leaf_pts = out_ref.shape
    move = pltpu.make_async_copy(halo_hbm, halo_ref, sem)
    move.start()
    n = list_pairs(near_ref, count_ref, pairs, pairs_ref, sizes_ref)
    for extra in range(3):
        pairs[n + extra] = 5 * leaf_dev
    src[leaf_dev] = jnp.zeros(src.shape[1:], BF16)
    wgt[leaf_dev] = jnp.zeros(wgt.shape[1:], BF16)
    out_ref[...] = jnp.zeros_like(out_ref)
    move.wait()
    node_work(order_ref, halo_ref, transfer_ref, skel_ref, node_ref, own_ref, inv_ref, slot)
    prepare(halo_ref, scale_rows(scale_ref, (8, leaf_pts)), 0, src, wgt, tgt)
    near_pairs(pairs, n, 4 * leaf_dev, src, tgt, wgt, out_ref, z, high, low)


def node_field(tm_size, place_ref, scale, node_ref, own_ref, transfer_ref, node_src, node_wgt):
    devices = node_ref.shape[0]
    rank = own_ref.shape[1] // 2
    lane = lane_ids((8, 128))

    def distant(e):
        far_a = jnp.abs(e // tm_size - place_ref[0]) > 1
        far_b = jnp.abs(e % tm_size - place_ref[1]) > 1
        return jnp.where(far_a | far_b, FACTOR, 0.0)

    def unpack(g, _):
        xs, ws = [], []
        for k in range(4):
            e = 8 * g + 2 * k
            one, two = node_ref[e], node_ref[e + 1]
            xs.append(jnp.where(lane < rank, pltpu.roll(one, rank, 1), two))
            ws.append(jnp.where(lane < rank, one * distant(e), pltpu.roll(two, rank, 1) * distant(e + 1)))
        at = pl.ds(pl.multiple_of(g * 512, 512), 512)
        node_src[:, at] = features(jnp.concatenate(xs, axis=1) * scale, True, False)[0]
        node_wgt[:, at] = halves(jnp.concatenate(ws, axis=1))
        return 0

    lax.fori_loop(0, devices // 8, unpack, 0, unroll=4)
    own_xx = pltpu.roll(own_ref[...], rank, 1) * scale[:, 0 : 2 * rank]
    target = features(own_xx, False, True)[0][:, :rank]
    total = jnp.zeros((16, rank), F32)
    step = 512
    for q in range(0, devices * rank, step):
        z_far = contract(target, node_src[:, q : q + step], ((0,), (0,)))
        k_high, k_low = split(kernel_of(z_far))
        weight = node_wgt[:, q : q + step]
        total = total + contract(weight, k_high, ((1,), (1,)))
        total = total + contract(weight, k_low, ((1,), (1,)))
    return jnp.dot(total[:8] + total[8:], transfer_ref[...], precision=EXACT, preferred_element_type=F32)


def outside_body(pairs_ref, sizes_ref, scale_ref, left_ref, mid_ref, right_ref, up_ref, down_ref, inside_ref, out_ref, src, tgt, wgt, z, high, low):
    leaf_dev, rhs, leaf_pts = out_ref.shape
    scale = scale_rows(scale_ref, (8, leaf_pts))
    idle = 9 * leaf_dev
    src[idle] = jnp.zeros(src.shape[1:], BF16)
    wgt[idle] = jnp.zeros(wgt.shape[1:], BF16)
    for k in range(3):
        prepare(up_ref.at[k], scale, k * leaf_dev, src, wgt)
        prepare(down_ref.at[k], scale, (6 + k) * leaf_dev, src, wgt)
    prepare(left_ref, scale, 3 * leaf_dev, src, wgt)
    prepare(mid_ref, scale, 4 * leaf_dev, src, wgt, tgt)
    prepare(right_ref, scale, 5 * leaf_dev, src, wgt)
    out_ref[...] = inside_ref[...]
    near_pairs(pairs_ref, sizes_ref[1], 0, src, tgt, wgt, out_ref, z, high, low)


def tail_body(tm_size, far_ref, place_ref, scale_ref, noise_ref, left_ref, mid_ref, right_ref, up_ref, down_ref, near_ref, node_ref, own_ref, transfer_ref, bases_ref, inv_ref, p_ref, res_ref, image_ref, sums_ref, src, tgt, coef, flat, far_src, far_wgt, node_src, node_wgt):
    leaf_dev, rank, leaf_pts = bases_ref.shape
    scale = scale_rows(scale_ref, (8, 4 * 128))
    pushed = node_field(tm_size, place_ref, scale, node_ref, own_ref, transfer_ref, node_src, node_wgt)
    brief = scale[:, :128]
    for k in range(3):
        prepare(up_ref.at[k], brief, k * leaf_dev, src, None, None, coef)
        prepare(down_ref.at[k], brief, (6 + k) * leaf_dev, src, None, None, coef)
    prepare(left_ref, brief, 3 * leaf_dev, src, None, None, coef)
    prepare(mid_ref, brief, 4 * leaf_dev, src, None, tgt, coef)
    prepare(right_ref, brief, 5 * leaf_dev, src, None, None, coef)
    for leaf in range(leaf_dev):
        for j in range(far_ref.shape[1]):
            w = far_ref[leaf, j]
            at = slice(j * rank, (j + 1) * rank)
            far_src[leaf, :, at] = src[w, :, 0:rank]
            far_wgt[leaf, :, at] = coef[w]
    for leaf in range(leaf_dev):
        k_high, k_low = split(kernel_of(contract(tgt[leaf, :, 0:rank], far_src[leaf], ((0,), (0,)))))
        far = contract(far_wgt[leaf], k_high, ((1,), (1,))) + contract(far_wgt[leaf], k_low, ((1,), (1,)))
        incoming = halves(far[:8] + far[8:] + pushed[:, leaf * rank : (leaf + 1) * rank])
        base_high, base_low = split(bases_ref[leaf])
        got = jnp.dot(incoming, base_high, preferred_element_type=F32)
        got = got + jnp.dot(incoming, base_low, preferred_element_type=F32)
        flat[:, leaf * leaf_pts : (leaf + 1) * leaf_pts] = near_ref[leaf] + got[:8] + got[8:]

    chunks = flat.shape[1] // 128
    row = row_ids((8, 128))
    lane = lane_ids((8, 128))
    source = [lambda s=s: flat[:, s * 128 : (s + 1) * 128] for s in range(chunks)]
    noise = jnp.zeros((8, 128), F32)
    for r in range(8):
        noise = jnp.where(row == r, noise_ref[r], noise)

    def place(g, sums):
        along, squares = sums
        for h in range(4):
            c = 4 * g + h
            at = pl.ds(pl.multiple_of(c * 128, 128), 128)
            ids = jnp.broadcast_to(inv_ref[pl.ds(c, 1), :], (8, 128))
            (part,) = gather_lanes([source], ids)
            image = part + noise * p_ref[:, at]
            image_ref[:, at] = image
            along, squares = along + res_ref[:, at] * image, squares + image * image
        return along, squares

    zero = jnp.zeros((8, 128), F32)
    along, squares = lax.fori_loop(0, chunks // 4, place, (zero, zero))
    along = jnp.sum(along, axis=1, keepdims=True)
    squares = jnp.sum(squares, axis=1, keepdims=True)
    both = jnp.where(lane == row, along, 0.0) + jnp.where(lane == row + 8, squares, 0.0)
    sums_ref[...] = jnp.broadcast_to(jnp.sum(both, axis=0, keepdims=True), sums_ref.shape)


def update_body(sums_ref, it_ref, p_ref, res_ref, image_ref, new_it_ref, new_res_ref):
    total = jnp.sum(sums_ref[...], axis=0, keepdims=True)
    row = row_ids((8, 128))
    lane = lane_ids((8, 128))
    along = jnp.sum(jnp.where(lane == row, total, 0.0), axis=1, keepdims=True)
    squares = jnp.sum(jnp.where(lane == row + 8, total, 0.0), axis=1, keepdims=True)
    alpha = along / (squares + 1e-06)
    new_it_ref[...] = it_ref[...] + alpha * p_ref[...]
    new_res_ref[...] = res_ref[...] - alpha * image_ref[...]


def shifted(x, axis, by):
    n = lax.axis_size(axis)
    return lax.ppermute(x, axis, [(i, i + by) for i in range(n) if 0 <= i + by < n])


def shards(coords, direction, iterate, residual, order, bases, transfer, near_list, near_count, far_list, device_skel, inv_scale, noise):
    leaf_dev, rank, leaf_pts = bases.shape
    rhs, points = direction.shape
    axes = ("leaf", "tm")
    devices = lax.axis_size("leaf") * lax.axis_size("tm")
    chunks = points // 128
    shape = jax.ShapeDtypeStruct
    by_row = order.reshape(chunks, 128)
    halo = pl.pallas_call(
        gather_body,
        in_specs=[ANY] * 4,
        out_specs=VMEM,
        out_shape=shape((13 * leaf_dev, leaf_pts), F32),
        scratch_shapes=[
            pltpu.VMEM((chunks, 128), jnp.int32),
            pltpu.VMEM((8, points), F32),
            pltpu.VMEM((rhs, points), F32),
            pltpu.VMEM(bases.shape, F32),
            pltpu.SemaphoreType.DMA((5,)),
        ],
        compiler_params=params(60),
        name="gather",
    )(by_row, coords, direction, bases)
    left = shifted(halo, "tm", 1)
    right = shifted(halo, "tm", -1)

    def pipeline(sources):
        return [
            pltpu.VMEM((sources + 1, 32, leaf_pts), BF16),
            pltpu.VMEM((leaf_dev, 32, leaf_pts), BF16),
            pltpu.VMEM((sources + 1, 16, leaf_pts), BF16),
        ]

    buffers = [
        pltpu.VMEM((2, PART, leaf_pts), F32),
        pltpu.VMEM((2, PART, leaf_pts), BF16),
        pltpu.VMEM((2, PART, leaf_pts), BF16),
    ]
    entries = near_list.size + 4
    inside, node, own, inverse, pairs, sizes = pl.pallas_call(
        inside_body,
        in_specs=[SMEM] * 3 + [ANY] + [VMEM] * 3,
        out_specs=[VMEM] * 4 + [SMEM] * 2,
        out_shape=[
            shape((leaf_dev, rhs, leaf_pts), F32),
            shape((devices, 8, 128), F32),
            shape((8, 128), F32),
            shape((chunks, 128), jnp.int32),
            shape((entries,), jnp.int32),
            shape((2,), jnp.int32),
        ],
        scratch_shapes=[
            pltpu.SMEM((entries,), jnp.int32),
            pltpu.VMEM(halo.shape, F32),
            pltpu.VMEM((8, leaf_dev * rank), F32),
        ]
        + pipeline(leaf_dev)
        + buffers
        + [pltpu.SemaphoreType.DMA(())],
        compiler_params=params(58),
        cost_estimate=pl.CostEstimate(flops=10**10, bytes_accessed=2**21, transcendentals=10**7),
        name="inside",
    )(near_list, near_count, inv_scale, halo, by_row, transfer[0], device_skel)
    left, right, inside, node = lax.optimization_barrier((left, right, inside, node))
    nodes = lax.all_to_all(node, axes, 0, 0)
    row = jnp.stack([left, halo, right])
    up = shifted(row, "leaf", 1)
    down = shifted(row, "leaf", -1)
    place = jnp.stack([lax.axis_index("leaf"), lax.axis_index("tm")]).astype(jnp.int32)

    near = pl.pallas_call(
        outside_body,
        in_specs=[SMEM] * 3 + [VMEM] * 6,
        out_specs=VMEM,
        out_shape=shape((leaf_dev, rhs, leaf_pts), F32),
        scratch_shapes=pipeline(9 * leaf_dev) + buffers,
        compiler_params=params(14),
        cost_estimate=pl.CostEstimate(flops=3 * 10**10, bytes_accessed=2**21, transcendentals=3 * 10**7),
        name="outside",
    )(pairs, sizes, inv_scale, left, halo, right, up, down, inside)
    image, sums = pl.pallas_call(
        functools.partial(tail_body, lax.axis_size("tm")),
        in_specs=[SMEM] * 4 + [VMEM] * 13,
        out_specs=[VMEM] * 2,
        out_shape=[shape((rhs, points), F32), shape((devices, 128), F32)],
        scratch_shapes=[
            pltpu.VMEM((9 * leaf_dev, 32, 128), BF16),
            pltpu.VMEM((leaf_dev, 32, 128), BF16),
            pltpu.VMEM((9 * leaf_dev, 16, rank), BF16),
            pltpu.VMEM((rhs, points), F32),
            pltpu.VMEM((leaf_dev, 32, far_list.shape[1] * rank), BF16),
            pltpu.VMEM((leaf_dev, 16, far_list.shape[1] * rank), BF16),
            pltpu.VMEM((32, devices * rank), BF16),
            pltpu.VMEM((16, devices * rank), BF16),
        ],
        compiler_params=params(14),
        name="tail",
    )(far_list, place, inv_scale, noise, left, halo, right, up, down, near, nodes, own, transfer[0], bases, inverse, direction, residual)
    all_sums = lax.all_to_all(sums, axes, 0, 0, tiled=True)
    return pl.pallas_call(
        update_body,
        in_specs=[VMEM] * 5,
        out_specs=[VMEM] * 2,
        out_shape=[shape((rhs, points), F32)] * 2,
        compiler_params=params(8),
        name="update",
    )(all_sums, iterate, direction, residual, image)


def solution(mesh):
    whole = P(None, ("leaf", "tm"))
    first = P(("leaf", "tm"))
    return jax.shard_map(
        shards,
        mesh=mesh,
        in_specs=(whole,) * 4 + (first,) * 7 + (P(), P()),
        out_specs=(whole, whole),
        check_vma=False,
    )
```

```python
import functools
import math

import jax
import jax.numpy as jnp
from jax import lax
from jax.experimental import pallas as pl
from jax.experimental.pallas import tpu as pltpu
from jax.sharding import PartitionSpec as P

F32 = jnp.float32
BF16 = jnp.bfloat16
EXACT = lax.Precision.HIGHEST
LN2 = math.log(2.0)
LOG2E = 1.0 / LN2
UNIT = math.sqrt(3.0) * LOG2E
FACTOR = -LN2 * math.e
VMEM = pl.BlockSpec(memory_space=pltpu.VMEM)
SMEM = pl.BlockSpec(memory_space=pltpu.SMEM)
ANY = pl.BlockSpec(memory_space=pl.ANY)
PART = 256
FIRST_PAIRS = 10


def params(mib, **kw):
    return pltpu.CompilerParams(vmem_limit_bytes=mib * 2**20, **kw)


def contract(a, b, dims, precision=None):
    return lax.dot_general(
        a, b, ((dims[0], dims[1]), ((), ())), precision=precision, preferred_element_type=F32
    )


def rounded(x):
    return x.astype(BF16).astype(F32)


def row_ids(shape):
    return lax.broadcasted_iota(jnp.int32, shape, 0)


def lane_ids(shape):
    return lax.broadcasted_iota(jnp.int32, shape, 1)


def features(xx, want_source, want_target):
    row = row_ids(xx.shape)
    high = rounded(xx)
    low = rounded(xx - high)
    held = high + low
    square = held * held
    square = square + pltpu.roll(square, 1, 0)
    norm = square + pltpu.roll(square, 2, 0)
    n0 = rounded(norm)
    rest = norm - n0
    n1 = rounded(rest)
    n2 = rest - n1
    zero = jnp.zeros_like(xx)
    out = []
    if want_source:
        parts = jnp.where(row < 4, high, low)
        tail = jnp.where(row == 0, n0, jnp.where(row == 1, n1, jnp.where(row == 2, n2, jnp.where(row < 6, 1.0, 0.0))))
        out.append(jnp.concatenate([parts, parts, tail, zero], axis=0).astype(BF16))
    if want_target:
        tail = jnp.where(row < 3, 1.0, jnp.where(row == 3, n0, jnp.where(row == 4, n1, jnp.where(row == 5, n2, 0.0))))
        out.append(jnp.concatenate([-2.0 * high, -2.0 * low, tail, zero], axis=0).astype(BF16))
    return out


def halves(w):
    high = rounded(w)
    return jnp.concatenate([high, w - high], axis=0).astype(BF16)


def kernel_of(z):
    z = jnp.maximum(z, 1e-30)
    q = -LOG2E - z * lax.rsqrt(z)
    return q * jnp.exp2(q)


def split(k):
    high = k.astype(BF16)
    return high, (k - high.astype(F32)).astype(BF16)


def gather_lanes(chunks, ids):
    lane = ids & 127
    chunk = ids >> 7
    picked = [None] * len(chunks)
    for s in range(len(chunks[0])):
        here = chunk == s
        for i, source in enumerate(chunks):
            got = jnp.take_along_axis(source[s](), lane, axis=1, mode="promise_in_bounds")
            picked[i] = got if s == 0 else jnp.where(here, got, picked[i])
    return picked


def gather_body(order_hbm, x_hbm, p_hbm, bases_hbm, halo_ref, order_ref, xx, p_ref, bases_ref, sems):
    leaf_dev, rank, leaf_pts = bases_ref.shape
    points = p_ref.shape[1]
    chunks = points // 128
    per_leaf = leaf_pts // 128
    moves = [
        pltpu.make_async_copy(source, target, sems.at[i])
        for i, (source, target) in enumerate(
            [
                (order_hbm, order_ref),
                (x_hbm, xx.at[0:4, :]),
                (x_hbm, xx.at[4:8, :]),
                (p_hbm, p_ref),
                (bases_hbm, bases_ref),
            ]
        )
    ]
    for move in moves:
        move.start()
    for move in moves[:4]:
        move.wait()

    def loads(ref):
        return [lambda s=s: ref[:, s * 128 : (s + 1) * 128] for s in range(chunks)]

    def two_leaves(g, _):
        kept = []
        for h in range(2):
            leaf = 2 * g + h
            for j in range(per_leaf):
                ids = order_ref[pl.ds(leaf * per_leaf + j, 1), :]
                got_x, got_p = gather_lanes([loads(xx), loads(p_ref)], jnp.broadcast_to(ids, (8, 128)))
                kept.append(got_x)
                halo_ref[pl.ds(pl.multiple_of(32 + leaf * 8, 8), 8), j * 128 : (j + 1) * 128] = got_p
        for j in range(per_leaf):
            both = jnp.where(row_ids((8, 128)) < 4, kept[j], kept[per_leaf + j])
            halo_ref[pl.ds(pl.multiple_of(g * 8, 8), 8), j * 128 : (j + 1) * 128] = both
        return 0

    lax.fori_loop(0, leaf_dev // 2, two_leaves, 0)
    moves[4].wait()
    for leaf in range(leaf_dev):
        coef = contract(halo_ref[32 + leaf * 8 : 40 + leaf * 8, :], bases_ref[leaf], ((1,), (1,)), EXACT)
        halo_ref[96:104, leaf * rank : (leaf + 1) * rank] = coef


def node_work(order_ref, halo_ref, transfer_ref, skel_ref, node_ref, own_ref, inv_ref, slot):
    chunks = order_ref.shape[0]
    rank = transfer_ref.shape[0]
    leaf_dev = halo_ref.shape[0] // 13
    upper = row_ids((8, 128)) < 4
    for g in range(leaf_dev // 2):
        both = halo_ref[g * 8 : g * 8 + 8, 0:128]
        turned = pltpu.roll(both, 4, 0)
        slot[:, 2 * g * rank : (2 * g + 1) * rank] = jnp.where(upper, both, turned)[:, :rank]
        slot[:, (2 * g + 1) * rank : (2 * g + 2) * rank] = jnp.where(upper, turned, both)[:, :rank]
    weights = contract(halo_ref[96:104, :], transfer_ref[...], ((1,), (1,)), EXACT)
    slots = [lambda s=s: slot[:, s * 128 : (s + 1) * 128] for s in range(leaf_dev * rank // 128)]
    ids = jnp.concatenate([skel_ref[...], skel_ref[...]], axis=1)
    (node_x,) = gather_lanes([slots], jnp.broadcast_to(ids, (8, 128)))
    tile = jnp.concatenate([weights, node_x[:, :rank]], axis=1)
    own_ref[...] = tile
    node_ref[...] = jnp.broadcast_to(tile[None], node_ref.shape)
    tally = jnp.zeros((2 * chunks, 128), F32)
    for c in range(chunks):
        ids = order_ref[c : c + 1, :]
        low = jnp.where(row_ids((128, 128)) == (ids & 127), 1.0, 0.0).astype(BF16)
        row = row_ids((chunks, 128)) == (ids >> 7)
        lane = lane_ids((chunks, 128))
        digit1 = jnp.where(row, (2 * c + (lane >> 6)).astype(F32), 0.0)
        digit0 = jnp.where(row, (lane & 63).astype(F32), 0.0)
        digits = jnp.concatenate([digit1, digit0], axis=0).astype(BF16)
        tally = tally + contract(digits, low, ((1,), (1,)))
    inv_ref[...] = (64.0 * tally[0:chunks] + tally[chunks : 2 * chunks] + 0.5).astype(jnp.int32)


def scale_rows(scale_ref, shape):
    row = row_ids(shape) & 3
    picked = jnp.where(row == 0, scale_ref[0], jnp.where(row == 1, scale_ref[1], jnp.where(row == 2, scale_ref[2], scale_ref[3])))
    return picked * UNIT


def prepare(ref, scale, base, src, wgt=None, tgt=None, coef=None):
    leaf_dev = ref.shape[0] // 13
    width = scale.shape[1]
    row = row_ids(scale.shape)
    for g in range(leaf_dev // 2):
        both = ref[g * 8 : g * 8 + 8, 0:width] * scale
        turned = pltpu.roll(both, 4, 0)
        for h in range(2):
            leaf = 2 * g + h
            xx = jnp.where(row < 4, both, turned) if h == 0 else jnp.where(row < 4, turned, both)
            made = features(xx, True, tgt is not None)
            src[base + leaf, :, 0:width] = made[0]
            if tgt is not None:
                tgt[leaf, :, 0:width] = made[1]
            if wgt is not None:
                wgt[base + leaf] = halves(ref[32 + leaf * 8 : 40 + leaf * 8, :] * FACTOR)
            if coef is not None:
                rank = coef.shape[2]
                coef[base + leaf] = halves(ref[96:104, leaf * rank : (leaf + 1) * rank] * FACTOR)


def list_pairs(near_ref, count_ref, inside, outside, sizes):
    leaf_dev, slots = near_ref.shape

    def leaf_step(leaf, sums):
        def entry(j, sums):
            w = near_ref[leaf, j]
            here = jnp.where((w // leaf_dev == 4) & (sums[0] < FIRST_PAIRS), 1, 0)
            code = leaf * 128 + w
            inside[sums[0]] = code
            outside[sums[1]] = code
            return sums[0] + here, sums[1] + 1 - here

        return lax.fori_loop(0, count_ref[leaf], entry, sums)

    sums = lax.fori_loop(0, leaf_dev, leaf_step, (0, 0))
    idle = 9 * leaf_dev
    for extra in range(3):
        inside[sums[0] + extra] = idle
        outside[sums[1] + extra] = idle
    sizes[0], sizes[1] = sums
    return sums[0]


def near_pairs(pairs, n, first, src, tgt, wgt, out, z, high, low):
    parts = wgt.shape[2] // PART

    def where(p):
        return pairs[p] >> 7, (pairs[p] & 127) - first

    def distances(p, c, b):
        leaf, w = where(p)
        z[b] = contract(src[w, :, c * PART : (c + 1) * PART], tgt[leaf], ((0,), (0,)))

    def values(b):
        high[b], low[b] = split(kernel_of(z[b]))

    def product(p, c, b):
        _, w = where(p)
        weight = wgt[w, :, c * PART : (c + 1) * PART]
        got = jnp.dot(weight, high[b], preferred_element_type=F32)
        return got + jnp.dot(weight, low[b], preferred_element_type=F32)

    distances(0, 0, 0)
    distances(0, 1, 1)
    values(0)

    def two_pairs(g, _):
        for h in range(2):
            p = 2 * g + h
            got = None
            for c in range(parts):
                b = c % 2
                values(1 - b)
                mine = product(p, c, b)
                got = mine if got is None else got + mine
                distances(p + (c + 2) // parts, (c + 2) % parts, b)
            leaf, _ = where(p)
            out[leaf] += got[:8] + got[8:]
        return 0

    lax.fori_loop(0, (n + 1) // 2, two_pairs, 0)


def inside_body(near_ref, count_ref, scale_ref, halo_hbm, order_ref, transfer_ref, skel_ref, out_ref, node_ref, own_ref, inv_ref, pairs_ref, sizes_ref, pairs, halo_ref, slot, src, tgt, wgt, z, high, low, sem):
    leaf_dev, rhs, leaf_pts = out_ref.shape
    move = pltpu.make_async_copy(halo_hbm, halo_ref, sem)
    move.start()
    n = list_pairs(near_ref, count_ref, pairs, pairs_ref, sizes_ref)
    for extra in range(3):
        pairs[n + extra] = 5 * leaf_dev
    src[leaf_dev] = jnp.zeros(src.shape[1:], BF16)
    wgt[leaf_dev] = jnp.zeros(wgt.shape[1:], BF16)
    out_ref[...] = jnp.zeros_like(out_ref)
    move.wait()
    node_work(order_ref, halo_ref, transfer_ref, skel_ref, node_ref, own_ref, inv_ref, slot)
    prepare(halo_ref, scale_rows(scale_ref, (8, leaf_pts)), 0, src, wgt, tgt)
    near_pairs(pairs, n, 4 * leaf_dev, src, tgt, wgt, out_ref, z, high, low)


def node_field(tm_size, place_ref, scale, node_ref, own_ref, transfer_ref, node_src, node_wgt):
    devices = node_ref.shape[0]
    rank = own_ref.shape[1] // 2
    lane = lane_ids((8, 128))

    def distant(e):
        far_a = jnp.abs(e // tm_size - place_ref[0]) > 1
        far_b = jnp.abs(e % tm_size - place_ref[1]) > 1
        return jnp.where(far_a | far_b, FACTOR, 0.0)

    def unpack(g, _):
        xs, ws = [], []
        for k in range(4):
            e = 8 * g + 2 * k
            one, two = node_ref[e], node_ref[e + 1]
            xs.append(jnp.where(lane < rank, pltpu.roll(one, rank, 1), two))
            ws.append(jnp.where(lane < rank, one * distant(e), pltpu.roll(two, rank, 1) * distant(e + 1)))
        at = pl.ds(pl.multiple_of(g * 512, 512), 512)
        node_src[:, at] = features(jnp.concatenate(xs, axis=1) * scale, True, False)[0]
        node_wgt[:, at] = halves(jnp.concatenate(ws, axis=1))
        return 0

    lax.fori_loop(0, devices // 8, unpack, 0, unroll=4)
    own_xx = pltpu.roll(own_ref[...], rank, 1) * scale[:, 0 : 2 * rank]
    target = features(own_xx, False, True)[0][:, :rank]
    total = jnp.zeros((16, rank), F32)
    step = 512
    for q in range(0, devices * rank, step):
        z_far = contract(target, node_src[:, q : q + step], ((0,), (0,)))
        k_high, k_low = split(kernel_of(z_far))
        weight = node_wgt[:, q : q + step]
        total = total + contract(weight, k_high, ((1,), (1,)))
        total = total + contract(weight, k_low, ((1,), (1,)))
    return jnp.dot(total[:8] + total[8:], transfer_ref[...], precision=EXACT, preferred_element_type=F32)


def outside_body(pairs_ref, sizes_ref, far_ref, scale_ref, left_ref, mid_ref, right_ref, up_ref, down_ref, inside_ref, out_ref, far_out_ref, src, tgt, wgt, coef, far_src, far_wgt, z, high, low):
    leaf_dev, rhs, leaf_pts = out_ref.shape
    rank = coef.shape[2]
    scale = scale_rows(scale_ref, (8, leaf_pts))
    idle = 9 * leaf_dev
    src[idle] = jnp.zeros(src.shape[1:], BF16)
    wgt[idle] = jnp.zeros(wgt.shape[1:], BF16)
    for k in range(3):
        prepare(up_ref.at[k], scale, k * leaf_dev, src, wgt, None, coef)
        prepare(down_ref.at[k], scale, (6 + k) * leaf_dev, src, wgt, None, coef)
    prepare(left_ref, scale, 3 * leaf_dev, src, wgt, None, coef)
    prepare(mid_ref, scale, 4 * leaf_dev, src, wgt, tgt, coef)
    prepare(right_ref, scale, 5 * leaf_dev, src, wgt, None, coef)
    out_ref[...] = inside_ref[...]
    near_pairs(pairs_ref, sizes_ref[1], 0, src, tgt, wgt, out_ref, z, high, low)
    for leaf in range(leaf_dev):
        for j in range(far_ref.shape[1]):
            w = far_ref[leaf, j]
            at = slice(j * rank, (j + 1) * rank)
            far_src[leaf, :, at] = src[w, :, 0:rank]
            far_wgt[leaf, :, at] = coef[w]
    for leaf in range(leaf_dev):
        k_high, k_low = split(kernel_of(contract(tgt[leaf, :, 0:rank], far_src[leaf], ((0,), (0,)))))
        far = contract(far_wgt[leaf], k_high, ((1,), (1,))) + contract(far_wgt[leaf], k_low, ((1,), (1,)))
        far_out_ref[leaf] = far[:8] + far[8:]


def tail_body(tm_size, place_ref, scale_ref, noise_ref, near_ref, far_ref, node_ref, own_ref, transfer_ref, bases_ref, inv_ref, p_ref, res_ref, image_ref, sums_ref, flat, node_src, node_wgt):
    leaf_dev, rank, leaf_pts = bases_ref.shape
    scale = scale_rows(scale_ref, (8, 4 * 128))
    pushed = node_field(tm_size, place_ref, scale, node_ref, own_ref, transfer_ref, node_src, node_wgt)
    for leaf in range(leaf_dev):
        incoming = halves(far_ref[leaf] + pushed[:, leaf * rank : (leaf + 1) * rank])
        base_high, base_low = split(bases_ref[leaf])
        got = jnp.dot(incoming, base_high, preferred_element_type=F32)
        got = got + jnp.dot(incoming, base_low, preferred_element_type=F32)
        flat[:, leaf * leaf_pts : (leaf + 1) * leaf_pts] = near_ref[leaf] + got[:8] + got[8:]

    chunks = flat.shape[1] // 128
    row = row_ids((8, 128))
    lane = lane_ids((8, 128))
    source = [lambda s=s: flat[:, s * 128 : (s + 1) * 128] for s in range(chunks)]
    noise = jnp.zeros((8, 128), F32)
    for r in range(8):
        noise = jnp.where(row == r, noise_ref[r], noise)

    def place(g, sums):
        along, squares = sums
        for h in range(4):
            c = 4 * g + h
            at = pl.ds(pl.multiple_of(c * 128, 128), 128)
            ids = jnp.broadcast_to(inv_ref[pl.ds(c, 1), :], (8, 128))
            (part,) = gather_lanes([source], ids)
            image = part + noise * p_ref[:, at]
            image_ref[:, at] = image
            along, squares = along + res_ref[:, at] * image, squares + image * image
        return along, squares

    zero = jnp.zeros((8, 128), F32)
    along, squares = lax.fori_loop(0, chunks // 4, place, (zero, zero))
    along = jnp.sum(along, axis=1, keepdims=True)
    squares = jnp.sum(squares, axis=1, keepdims=True)
    both = jnp.where(lane == row, along, 0.0) + jnp.where(lane == row + 8, squares, 0.0)
    sums_ref[...] = jnp.broadcast_to(jnp.sum(both, axis=0, keepdims=True), sums_ref.shape)


def update_body(sums_ref, it_ref, p_ref, res_ref, image_ref, new_it_ref, new_res_ref):
    total = jnp.sum(sums_ref[...], axis=0, keepdims=True)
    row = row_ids((8, 128))
    lane = lane_ids((8, 128))
    along = jnp.sum(jnp.where(lane == row, total, 0.0), axis=1, keepdims=True)
    squares = jnp.sum(jnp.where(lane == row + 8, total, 0.0), axis=1, keepdims=True)
    alpha = along / (squares + 1e-06)
    new_it_ref[...] = it_ref[...] + alpha * p_ref[...]
    new_res_ref[...] = res_ref[...] - alpha * image_ref[...]


def shifted(x, axis, by):
    n = lax.axis_size(axis)
    return lax.ppermute(x, axis, [(i, i + by) for i in range(n) if 0 <= i + by < n])


def shards(coords, direction, iterate, residual, order, bases, transfer, near_list, near_count, far_list, device_skel, inv_scale, noise):
    leaf_dev, rank, leaf_pts = bases.shape
    rhs, points = direction.shape
    axes = ("leaf", "tm")
    devices = lax.axis_size("leaf") * lax.axis_size("tm")
    chunks = points // 128
    shape = jax.ShapeDtypeStruct
    by_row = order.reshape(chunks, 128)
    halo = pl.pallas_call(
        gather_body,
        in_specs=[ANY] * 4,
        out_specs=VMEM,
        out_shape=shape((13 * leaf_dev, leaf_pts), F32),
        scratch_shapes=[
            pltpu.VMEM((chunks, 128), jnp.int32),
            pltpu.VMEM((8, points), F32),
            pltpu.VMEM((rhs, points), F32),
            pltpu.VMEM(bases.shape, F32),
            pltpu.SemaphoreType.DMA((5,)),
        ],
        compiler_params=params(60),
        name="gather",
    )(by_row, coords, direction, bases)
    left = shifted(halo, "tm", 1)
    right = shifted(halo, "tm", -1)

    def pipeline(sources):
        return [
            pltpu.VMEM((sources + 1, 32, leaf_pts), BF16),
            pltpu.VMEM((leaf_dev, 32, leaf_pts), BF16),
            pltpu.VMEM((sources + 1, 16, leaf_pts), BF16),
        ]

    buffers = [
        pltpu.VMEM((2, PART, leaf_pts), F32),
        pltpu.VMEM((2, PART, leaf_pts), BF16),
        pltpu.VMEM((2, PART, leaf_pts), BF16),
    ]
    entries = near_list.size + 4
    inside, node, own, inverse, pairs, sizes = pl.pallas_call(
        inside_body,
        in_specs=[SMEM] * 3 + [ANY] + [VMEM] * 3,
        out_specs=[VMEM] * 4 + [SMEM] * 2,
        out_shape=[
            shape((leaf_dev, rhs, leaf_pts), F32),
            shape((devices, 8, 128), F32),
            shape((8, 128), F32),
            shape((chunks, 128), jnp.int32),
            shape((entries,), jnp.int32),
            shape((2,), jnp.int32),
        ],
        scratch_shapes=[
            pltpu.SMEM((entries,), jnp.int32),
            pltpu.VMEM(halo.shape, F32),
            pltpu.VMEM((8, leaf_dev * rank), F32),
        ]
        + pipeline(leaf_dev)
        + buffers
        + [pltpu.SemaphoreType.DMA(())],
        compiler_params=params(58),
        cost_estimate=pl.CostEstimate(flops=10**10, bytes_accessed=2**21, transcendentals=10**7),
        name="inside",
    )(near_list, near_count, inv_scale, halo, by_row, transfer[0], device_skel)
    left, right, inside, node = lax.optimization_barrier((left, right, inside, node))
    nodes = lax.all_to_all(node, axes, 0, 0)
    row = jnp.stack([left, halo, right])
    up = shifted(row, "leaf", 1)
    down = shifted(row, "leaf", -1)
    place = jnp.stack([lax.axis_index("leaf"), lax.axis_index("tm")]).astype(jnp.int32)

    near, far = pl.pallas_call(
        outside_body,
        in_specs=[SMEM] * 4 + [VMEM] * 6,
        out_specs=[VMEM] * 2,
        out_shape=[shape((leaf_dev, rhs, leaf_pts), F32), shape((leaf_dev, rhs, rank), F32)],
        scratch_shapes=pipeline(9 * leaf_dev)
        + [
            pltpu.VMEM((9 * leaf_dev, 16, rank), BF16),
            pltpu.VMEM((leaf_dev, 32, far_list.shape[1] * rank), BF16),
            pltpu.VMEM((leaf_dev, 16, far_list.shape[1] * rank), BF16),
        ]
        + buffers,
        compiler_params=params(14),
        cost_estimate=pl.CostEstimate(flops=3 * 10**10, bytes_accessed=2**21, transcendentals=3 * 10**7),
        name="outside",
    )(pairs, sizes, far_list, inv_scale, left, halo, right, up, down, inside)
    image, sums = pl.pallas_call(
        functools.partial(tail_body, lax.axis_size("tm")),
        in_specs=[SMEM] * 3 + [VMEM] * 9,
        out_specs=[VMEM] * 2,
        out_shape=[shape((rhs, points), F32), shape((devices, 128), F32)],
        scratch_shapes=[
            pltpu.VMEM((rhs, points), F32),
            pltpu.VMEM((32, devices * rank), BF16),
            pltpu.VMEM((16, devices * rank), BF16),
        ],
        compiler_params=params(10),
        name="tail",
    )(place, inv_scale, noise, near, far, nodes, own, transfer[0], bases, inverse, direction, residual)
    all_sums = lax.all_to_all(sums, axes, 0, 0, tiled=True)
    return pl.pallas_call(
        update_body,
        in_specs=[VMEM] * 5,
        out_specs=[VMEM] * 2,
        out_shape=[shape((rhs, points), F32)] * 2,
        compiler_params=params(8),
        name="update",
    )(all_sums, iterate, direction, residual, image)


def solution(mesh):
    whole = P(None, ("leaf", "tm"))
    first = P(("leaf", "tm"))
    return jax.shard_map(
        shards,
        mesh=mesh,
        in_specs=(whole,) * 4 + (first,) * 7 + (P(), P()),
        out_specs=(whole, whole),
        check_vma=False,
    )
```

```python
import functools
import math

import jax
import jax.numpy as jnp
from jax import lax
from jax.experimental import pallas as pl
from jax.experimental.pallas import tpu as pltpu
from jax.sharding import PartitionSpec as P

F32 = jnp.float32
BF16 = jnp.bfloat16
EXACT = lax.Precision.HIGHEST
LN2 = math.log(2.0)
LOG2E = 1.0 / LN2
UNIT = math.sqrt(3.0) * LOG2E
FACTOR = -LN2 * math.e
VMEM = pl.BlockSpec(memory_space=pltpu.VMEM)
SMEM = pl.BlockSpec(memory_space=pltpu.SMEM)
ANY = pl.BlockSpec(memory_space=pl.ANY)
PART = 256
FIRST_PAIRS = 10


def params(mib, **kw):
    return pltpu.CompilerParams(vmem_limit_bytes=mib * 2**20, **kw)


def contract(a, b, dims, precision=None):
    return lax.dot_general(
        a, b, ((dims[0], dims[1]), ((), ())), precision=precision, preferred_element_type=F32
    )


def rounded(x):
    return x.astype(BF16).astype(F32)


def row_ids(shape):
    return lax.broadcasted_iota(jnp.int32, shape, 0)


def lane_ids(shape):
    return lax.broadcasted_iota(jnp.int32, shape, 1)


def features(xx, want_source, want_target):
    row = row_ids(xx.shape)
    high = rounded(xx)
    low = rounded(xx - high)
    held = high + low
    square = held * held
    square = square + pltpu.roll(square, 1, 0)
    norm = square + pltpu.roll(square, 2, 0)
    n0 = rounded(norm)
    rest = norm - n0
    n1 = rounded(rest)
    n2 = rest - n1
    zero = jnp.zeros_like(xx)
    out = []
    if want_source:
        parts = jnp.where(row < 4, high, low)
        tail = jnp.where(row == 0, n0, jnp.where(row == 1, n1, jnp.where(row == 2, n2, jnp.where(row < 6, 1.0, 0.0))))
        out.append(jnp.concatenate([parts, parts, tail, zero], axis=0).astype(BF16))
    if want_target:
        tail = jnp.where(row < 3, 1.0, jnp.where(row == 3, n0, jnp.where(row == 4, n1, jnp.where(row == 5, n2, 0.0))))
        out.append(jnp.concatenate([-2.0 * high, -2.0 * low, tail, zero], axis=0).astype(BF16))
    return out


def halves(w):
    high = rounded(w)
    return jnp.concatenate([high, w - high], axis=0).astype(BF16)


def kernel_of(z):
    z = jnp.maximum(z, 1e-30)
    q = -LOG2E - z * lax.rsqrt(z)
    return q * jnp.exp2(q)


def split(k):
    high = k.astype(BF16)
    return high, (k - high.astype(F32)).astype(BF16)


def gather_lanes(chunks, ids):
    lane = ids & 127
    chunk = ids >> 7
    picked = [None] * len(chunks)
    for s in range(len(chunks[0])):
        here = chunk == s
        for i, source in enumerate(chunks):
            got = jnp.take_along_axis(source[s](), lane, axis=1, mode="promise_in_bounds")
            picked[i] = got if s == 0 else jnp.where(here, got, picked[i])
    return picked


def gather_body(order_hbm, x_hbm, p_hbm, bases_hbm, halo_ref, order_ref, xx, p_ref, bases_ref, sems):
    leaf_dev, rank, leaf_pts = bases_ref.shape
    points = p_ref.shape[1]
    chunks = points // 128
    per_leaf = leaf_pts // 128
    moves = [
        pltpu.make_async_copy(source, target, sems.at[i])
        for i, (source, target) in enumerate(
            [
                (order_hbm, order_ref),
                (x_hbm, xx.at[0:4, :]),
                (x_hbm, xx.at[4:8, :]),
                (p_hbm, p_ref),
                (bases_hbm, bases_ref),
            ]
        )
    ]
    for move in moves:
        move.start()
    for move in moves[:4]:
        move.wait()

    def loads(ref):
        return [lambda s=s: ref[:, s * 128 : (s + 1) * 128] for s in range(chunks)]

    def two_leaves(g, _):
        kept = []
        for h in range(2):
            leaf = 2 * g + h
            for j in range(per_leaf):
                ids = order_ref[pl.ds(leaf * per_leaf + j, 1), :]
                got_x, got_p = gather_lanes([loads(xx), loads(p_ref)], jnp.broadcast_to(ids, (8, 128)))
                kept.append(got_x)
                halo_ref[pl.ds(pl.multiple_of(32 + leaf * 8, 8), 8), j * 128 : (j + 1) * 128] = got_p
        for j in range(per_leaf):
            both = jnp.where(row_ids((8, 128)) < 4, kept[j], kept[per_leaf + j])
            halo_ref[pl.ds(pl.multiple_of(g * 8, 8), 8), j * 128 : (j + 1) * 128] = both
        return 0

    lax.fori_loop(0, leaf_dev // 2, two_leaves, 0)
    moves[4].wait()
    for leaf in range(leaf_dev):
        coef = contract(halo_ref[32 + leaf * 8 : 40 + leaf * 8, :], bases_ref[leaf], ((1,), (1,)), EXACT)
        halo_ref[96:104, leaf * rank : (leaf + 1) * rank] = coef


def node_work(order_ref, halo_ref, transfer_ref, skel_ref, node_ref, own_ref, inv_ref, slot):
    chunks = order_ref.shape[0]
    rank = transfer_ref.shape[0]
    leaf_dev = halo_ref.shape[0] // 13
    upper = row_ids((8, 128)) < 4
    for g in range(leaf_dev // 2):
        both = halo_ref[g * 8 : g * 8 + 8, 0:128]
        turned = pltpu.roll(both, 4, 0)
        slot[:, 2 * g * rank : (2 * g + 1) * rank] = jnp.where(upper, both, turned)[:, :rank]
        slot[:, (2 * g + 1) * rank : (2 * g + 2) * rank] = jnp.where(upper, turned, both)[:, :rank]
    weights = contract(halo_ref[96:104, :], transfer_ref[...], ((1,), (1,)), EXACT)
    slots = [lambda s=s: slot[:, s * 128 : (s + 1) * 128] for s in range(leaf_dev * rank // 128)]
    ids = jnp.concatenate([skel_ref[...], skel_ref[...]], axis=1)
    (node_x,) = gather_lanes([slots], jnp.broadcast_to(ids, (8, 128)))
    tile = jnp.concatenate([weights, node_x[:, :rank]], axis=1)
    own_ref[...] = tile
    node_ref[...] = jnp.broadcast_to(tile[None], node_ref.shape)
    tally = jnp.zeros((2 * chunks, 128), F32)
    for c in range(chunks):
        ids = order_ref[c : c + 1, :]
        low = jnp.where(row_ids((128, 128)) == (ids & 127), 1.0, 0.0).astype(BF16)
        row = row_ids((chunks, 128)) == (ids >> 7)
        lane = lane_ids((chunks, 128))
        digit1 = jnp.where(row, (2 * c + (lane >> 6)).astype(F32), 0.0)
        digit0 = jnp.where(row, (lane & 63).astype(F32), 0.0)
        digits = jnp.concatenate([digit1, digit0], axis=0).astype(BF16)
        tally = tally + contract(digits, low, ((1,), (1,)))
    inv_ref[...] = (64.0 * tally[0:chunks] + tally[chunks : 2 * chunks] + 0.5).astype(jnp.int32)


def fetch(sources, targets, sems):
    moves = [pltpu.make_async_copy(a, b, sems.at[i]) for i, (a, b) in enumerate(zip(sources, targets))]
    for move in moves:
        move.start()
    return moves


def scale_rows(scale_ref, shape):
    row = row_ids(shape) & 3
    picked = jnp.where(row == 0, scale_ref[0], jnp.where(row == 1, scale_ref[1], jnp.where(row == 2, scale_ref[2], scale_ref[3])))
    return picked * UNIT


def prepare(ref, scale, base, src, wgt=None, tgt=None, coef=None):
    leaf_dev = ref.shape[0] // 13
    width = scale.shape[1]
    row = row_ids(scale.shape)
    for g in range(leaf_dev // 2):
        both = ref[g * 8 : g * 8 + 8, 0:width] * scale
        turned = pltpu.roll(both, 4, 0)
        for h in range(2):
            leaf = 2 * g + h
            xx = jnp.where(row < 4, both, turned) if h == 0 else jnp.where(row < 4, turned, both)
            made = features(xx, True, tgt is not None)
            src[base + leaf, :, 0:width] = made[0]
            if tgt is not None:
                tgt[leaf, :, 0:width] = made[1]
            if wgt is not None:
                wgt[base + leaf] = halves(ref[32 + leaf * 8 : 40 + leaf * 8, :] * FACTOR)
            if coef is not None:
                rank = coef.shape[2]
                coef[base + leaf] = halves(ref[96:104, leaf * rank : (leaf + 1) * rank] * FACTOR)


def list_pairs(near_ref, count_ref, inside, outside, sizes):
    leaf_dev, slots = near_ref.shape

    def leaf_step(leaf, sums):
        def entry(j, sums):
            w = near_ref[leaf, j]
            here = jnp.where((w // leaf_dev == 4) & (sums[0] < FIRST_PAIRS), 1, 0)
            code = leaf * 128 + w
            inside[sums[0]] = code
            outside[sums[1]] = code
            return sums[0] + here, sums[1] + 1 - here

        return lax.fori_loop(0, count_ref[leaf], entry, sums)

    sums = lax.fori_loop(0, leaf_dev, leaf_step, (0, 0))
    idle = 9 * leaf_dev
    for extra in range(3):
        inside[sums[0] + extra] = idle
        outside[sums[1] + extra] = idle
    sizes[0], sizes[1] = sums
    return sums[0]


def near_pairs(pairs, n, first, src, tgt, wgt, out, z, high, low):
    parts = wgt.shape[2] // PART

    def where(p):
        return pairs[p] >> 7, (pairs[p] & 127) - first

    def distances(p, c, b):
        leaf, w = where(p)
        z[b] = contract(src[w, :, c * PART : (c + 1) * PART], tgt[leaf], ((0,), (0,)))

    def values(b):
        high[b], low[b] = split(kernel_of(z[b]))

    def product(p, c, b):
        _, w = where(p)
        weight = wgt[w, :, c * PART : (c + 1) * PART]
        got = jnp.dot(weight, high[b], preferred_element_type=F32)
        return got + jnp.dot(weight, low[b], preferred_element_type=F32)

    distances(0, 0, 0)
    distances(0, 1, 1)
    values(0)

    def two_pairs(g, _):
        for h in range(2):
            p = 2 * g + h
            got = None
            for c in range(parts):
                b = c % 2
                values(1 - b)
                mine = product(p, c, b)
                got = mine if got is None else got + mine
                distances(p + (c + 2) // parts, (c + 2) % parts, b)
            leaf, _ = where(p)
            out[leaf] += got[:8] + got[8:]
        return 0

    lax.fori_loop(0, (n + 1) // 2, two_pairs, 0)


def inside_body(near_ref, count_ref, scale_ref, halo_hbm, order_ref, transfer_ref, skel_ref, out_ref, node_ref, own_ref, inv_ref, pairs_ref, sizes_ref, pairs, halo_ref, slot, src, tgt, wgt, z, high, low, sem):
    leaf_dev, rhs, leaf_pts = out_ref.shape
    move = pltpu.make_async_copy(halo_hbm, halo_ref, sem)
    move.start()
    n = list_pairs(near_ref, count_ref, pairs, pairs_ref, sizes_ref)
    for extra in range(3):
        pairs[n + extra] = 5 * leaf_dev
    src[leaf_dev] = jnp.zeros(src.shape[1:], BF16)
    wgt[leaf_dev] = jnp.zeros(wgt.shape[1:], BF16)
    out_ref[...] = jnp.zeros_like(out_ref)
    move.wait()
    node_work(order_ref, halo_ref, transfer_ref, skel_ref, node_ref, own_ref, inv_ref, slot)
    prepare(halo_ref, scale_rows(scale_ref, (8, leaf_pts)), 0, src, wgt, tgt)
    near_pairs(pairs, n, 4 * leaf_dev, src, tgt, wgt, out_ref, z, high, low)


def node_field(tm_size, place_ref, scale, node_ref, own_ref, transfer_ref, node_src, node_wgt):
    devices = node_ref.shape[0]
    rank = own_ref.shape[1] // 2
    lane = lane_ids((8, 128))

    def distant(e):
        far_a = jnp.abs(e // tm_size - place_ref[0]) > 1
        far_b = jnp.abs(e % tm_size - place_ref[1]) > 1
        return jnp.where(far_a | far_b, FACTOR, 0.0)

    def unpack(g, _):
        xs, ws = [], []
        for k in range(4):
            e = 8 * g + 2 * k
            one, two = node_ref[e], node_ref[e + 1]
            xs.append(jnp.where(lane < rank, pltpu.roll(one, rank, 1), two))
            ws.append(jnp.where(lane < rank, one * distant(e), pltpu.roll(two, rank, 1) * distant(e + 1)))
        at = pl.ds(pl.multiple_of(g * 512, 512), 512)
        node_src[:, at] = features(jnp.concatenate(xs, axis=1) * scale, True, False)[0]
        node_wgt[:, at] = halves(jnp.concatenate(ws, axis=1))
        return 0

    lax.fori_loop(0, devices // 8, unpack, 0, unroll=4)
    own_xx = pltpu.roll(own_ref[...], rank, 1) * scale[:, 0 : 2 * rank]
    target = features(own_xx, False, True)[0][:, :rank]
    total = jnp.zeros((16, rank), F32)
    step = 512
    for q in range(0, devices * rank, step):
        z_far = contract(target, node_src[:, q : q + step], ((0,), (0,)))
        k_high, k_low = split(kernel_of(z_far))
        weight = node_wgt[:, q : q + step]
        total = total + contract(weight, k_high, ((1,), (1,)))
        total = total + contract(weight, k_low, ((1,), (1,)))
    return jnp.dot(total[:8] + total[8:], transfer_ref[...], precision=EXACT, preferred_element_type=F32)


def outside_body(pairs_ref, sizes_ref, far_ref, scale_ref, left_hbm, mid_hbm, right_hbm, up_hbm, down_hbm, inside_hbm, out_ref, far_out_ref, row, up, down, src, tgt, wgt, coef, far_src, far_wgt, z, high, low, sems):
    moves = fetch(
        [left_hbm, mid_hbm, right_hbm, up_hbm, down_hbm, inside_hbm],
        [row.at[0], row.at[1], row.at[2], up, down, out_ref],
        sems,
    )
    leaf_dev, rhs, leaf_pts = out_ref.shape
    rank = coef.shape[2]
    scale = scale_rows(scale_ref, (8, leaf_pts))
    idle = 9 * leaf_dev
    src[idle] = jnp.zeros(src.shape[1:], BF16)
    wgt[idle] = jnp.zeros(wgt.shape[1:], BF16)
    for k in range(3):
        moves[k].wait()
        prepare(row.at[k], scale, (3 + k) * leaf_dev, src, wgt, tgt if k == 1 else None, coef)
    moves[3].wait()
    for k in range(3):
        prepare(up.at[k], scale, k * leaf_dev, src, wgt, None, coef)
    moves[4].wait()
    for k in range(3):
        prepare(down.at[k], scale, (6 + k) * leaf_dev, src, wgt, None, coef)
    moves[5].wait()
    near_pairs(pairs_ref, sizes_ref[1], 0, src, tgt, wgt, out_ref, z, high, low)
    for leaf in range(leaf_dev):
        for j in range(far_ref.shape[1]):
            w = far_ref[leaf, j]
            at = slice(j * rank, (j + 1) * rank)
            far_src[leaf, :, at] = src[w, :, 0:rank]
            far_wgt[leaf, :, at] = coef[w]
    for leaf in range(leaf_dev):
        k_high, k_low = split(kernel_of(contract(tgt[leaf, :, 0:rank], far_src[leaf], ((0,), (0,)))))
        far = contract(far_wgt[leaf], k_high, ((1,), (1,))) + contract(far_wgt[leaf], k_low, ((1,), (1,)))
        far_out_ref[leaf] = far[:8] + far[8:]


def tail_body(tm_size, place_ref, scale_ref, noise_ref, node_hbm, own_hbm, transfer_hbm, near_hbm, far_hbm, bases_hbm, inv_hbm, p_hbm, res_hbm, image_ref, sums_ref, node_ref, own_ref, transfer_ref, near_ref, far_ref, bases_ref, inv_ref, p_ref, res_ref, flat, node_src, node_wgt, sems):
    leaf_dev, rank, leaf_pts = bases_ref.shape
    moves = fetch(
        [node_hbm, own_hbm, transfer_hbm, near_hbm, far_hbm, bases_hbm, inv_hbm, p_hbm, res_hbm],
        [node_ref, own_ref, transfer_ref, near_ref, far_ref, bases_ref, inv_ref, p_ref, res_ref],
        sems,
    )
    scale = scale_rows(scale_ref, (8, 4 * 128))
    for move in moves[:3]:
        move.wait()
    pushed = node_field(tm_size, place_ref, scale, node_ref, own_ref, transfer_ref, node_src, node_wgt)
    for move in moves[3:]:
        move.wait()
    for leaf in range(leaf_dev):
        incoming = halves(far_ref[leaf] + pushed[:, leaf * rank : (leaf + 1) * rank])
        base_high, base_low = split(bases_ref[leaf])
        got = jnp.dot(incoming, base_high, preferred_element_type=F32)
        got = got + jnp.dot(incoming, base_low, preferred_element_type=F32)
        flat[:, leaf * leaf_pts : (leaf + 1) * leaf_pts] = near_ref[leaf] + got[:8] + got[8:]

    chunks = flat.shape[1] // 128
    row = row_ids((8, 128))
    lane = lane_ids((8, 128))
    source = [lambda s=s: flat[:, s * 128 : (s + 1) * 128] for s in range(chunks)]
    noise = jnp.zeros((8, 128), F32)
    for r in range(8):
        noise = jnp.where(row == r, noise_ref[r], noise)

    def place(g, sums):
        along, squares = sums
        for h in range(4):
            c = 4 * g + h
            at = pl.ds(pl.multiple_of(c * 128, 128), 128)
            ids = jnp.broadcast_to(inv_ref[pl.ds(c, 1), :], (8, 128))
            (part,) = gather_lanes([source], ids)
            image = part + noise * p_ref[:, at]
            image_ref[:, at] = image
            along, squares = along + res_ref[:, at] * image, squares + image * image
        return along, squares

    zero = jnp.zeros((8, 128), F32)
    along, squares = lax.fori_loop(0, chunks // 4, place, (zero, zero))
    along = jnp.sum(along, axis=1, keepdims=True)
    squares = jnp.sum(squares, axis=1, keepdims=True)
    both = jnp.where(lane == row, along, 0.0) + jnp.where(lane == row + 8, squares, 0.0)
    sums_ref[...] = jnp.broadcast_to(jnp.sum(both, axis=0, keepdims=True), sums_ref.shape)


def update_body(sums_ref, it_ref, p_ref, res_ref, image_ref, new_it_ref, new_res_ref):
    total = jnp.sum(sums_ref[...], axis=0, keepdims=True)
    row = row_ids((8, 128))
    lane = lane_ids((8, 128))
    along = jnp.sum(jnp.where(lane == row, total, 0.0), axis=1, keepdims=True)
    squares = jnp.sum(jnp.where(lane == row + 8, total, 0.0), axis=1, keepdims=True)
    alpha = along / (squares + 1e-06)
    new_it_ref[...] = it_ref[...] + alpha * p_ref[...]
    new_res_ref[...] = res_ref[...] - alpha * image_ref[...]


def shifted(x, axis, by):
    n = lax.axis_size(axis)
    return lax.ppermute(x, axis, [(i, i + by) for i in range(n) if 0 <= i + by < n])


def shards(coords, direction, iterate, residual, order, bases, transfer, near_list, near_count, far_list, device_skel, inv_scale, noise):
    leaf_dev, rank, leaf_pts = bases.shape
    rhs, points = direction.shape
    axes = ("leaf", "tm")
    devices = lax.axis_size("leaf") * lax.axis_size("tm")
    chunks = points // 128
    shape = jax.ShapeDtypeStruct
    by_row = order.reshape(chunks, 128)
    halo = pl.pallas_call(
        gather_body,
        in_specs=[ANY] * 4,
        out_specs=VMEM,
        out_shape=shape((13 * leaf_dev, leaf_pts), F32),
        scratch_shapes=[
            pltpu.VMEM((chunks, 128), jnp.int32),
            pltpu.VMEM((8, points), F32),
            pltpu.VMEM((rhs, points), F32),
            pltpu.VMEM(bases.shape, F32),
            pltpu.SemaphoreType.DMA((5,)),
        ],
        compiler_params=params(60),
        name="gather",
    )(by_row, coords, direction, bases)
    left = shifted(halo, "tm", 1)
    right = shifted(halo, "tm", -1)

    def pipeline(sources):
        return [
            pltpu.VMEM((sources + 1, 32, leaf_pts), BF16),
            pltpu.VMEM((leaf_dev, 32, leaf_pts), BF16),
            pltpu.VMEM((sources + 1, 16, leaf_pts), BF16),
        ]

    buffers = [
        pltpu.VMEM((2, PART, leaf_pts), F32),
        pltpu.VMEM((2, PART, leaf_pts), BF16),
        pltpu.VMEM((2, PART, leaf_pts), BF16),
    ]
    entries = near_list.size + 4
    inside, node, own, inverse, pairs, sizes = pl.pallas_call(
        inside_body,
        in_specs=[SMEM] * 3 + [ANY] + [VMEM] * 3,
        out_specs=[VMEM] * 4 + [SMEM] * 2,
        out_shape=[
            shape((leaf_dev, rhs, leaf_pts), F32),
            shape((devices, 8, 128), F32),
            shape((8, 128), F32),
            shape((chunks, 128), jnp.int32),
            shape((entries,), jnp.int32),
            shape((2,), jnp.int32),
        ],
        scratch_shapes=[
            pltpu.SMEM((entries,), jnp.int32),
            pltpu.VMEM(halo.shape, F32),
            pltpu.VMEM((8, leaf_dev * rank), F32),
        ]
        + pipeline(leaf_dev)
        + buffers
        + [pltpu.SemaphoreType.DMA(())],
        compiler_params=params(58),
        cost_estimate=pl.CostEstimate(flops=10**10, bytes_accessed=2**21, transcendentals=10**7),
        name="inside",
    )(near_list, near_count, inv_scale, halo, by_row, transfer[0], device_skel)
    left, right, inside, node = lax.optimization_barrier((left, right, inside, node))
    nodes = lax.all_to_all(node, axes, 0, 0)
    row = jnp.stack([left, halo, right])
    up = shifted(row, "leaf", 1)
    down = shifted(row, "leaf", -1)
    place = jnp.stack([lax.axis_index("leaf"), lax.axis_index("tm")]).astype(jnp.int32)

    near, far = pl.pallas_call(
        outside_body,
        in_specs=[SMEM] * 4 + [ANY] * 6,
        out_specs=[VMEM] * 2,
        out_shape=[shape((leaf_dev, rhs, leaf_pts), F32), shape((leaf_dev, rhs, rank), F32)],
        scratch_shapes=[pltpu.VMEM(row.shape, F32)] * 3
        + pipeline(9 * leaf_dev)
        + [
            pltpu.VMEM((9 * leaf_dev, 16, rank), BF16),
            pltpu.VMEM((leaf_dev, 32, far_list.shape[1] * rank), BF16),
            pltpu.VMEM((leaf_dev, 16, far_list.shape[1] * rank), BF16),
        ]
        + buffers
        + [pltpu.SemaphoreType.DMA((6,))],
        compiler_params=params(58),
        cost_estimate=pl.CostEstimate(flops=3 * 10**10, bytes_accessed=2**21, transcendentals=3 * 10**7),
        name="outside",
    )(pairs, sizes, far_list, inv_scale, left, halo, right, up, down, inside)
    image, sums = pl.pallas_call(
        functools.partial(tail_body, lax.axis_size("tm")),
        in_specs=[SMEM] * 3 + [ANY] * 9,
        out_specs=[VMEM] * 2,
        out_shape=[shape((rhs, points), F32), shape((devices, 128), F32)],
        scratch_shapes=[
            pltpu.VMEM((devices, 8, 128), F32),
            pltpu.VMEM((8, 128), F32),
            pltpu.VMEM(transfer.shape[1:], F32),
            pltpu.VMEM((leaf_dev, rhs, leaf_pts), F32),
            pltpu.VMEM((leaf_dev, rhs, rank), F32),
            pltpu.VMEM(bases.shape, F32),
            pltpu.VMEM((chunks, 128), jnp.int32),
            pltpu.VMEM((rhs, points), F32),
            pltpu.VMEM((rhs, points), F32),
            pltpu.VMEM((rhs, points), F32),
            pltpu.VMEM((32, devices * rank), BF16),
            pltpu.VMEM((16, devices * rank), BF16),
            pltpu.SemaphoreType.DMA((9,)),
        ],
        compiler_params=params(58),
        name="tail",
    )(place, inv_scale, noise, nodes, own, transfer[0], near, far, bases, inverse, direction, residual)
    all_sums = lax.all_to_all(sums, axes, 0, 0, tiled=True)
    return pl.pallas_call(
        update_body,
        in_specs=[VMEM] * 5,
        out_specs=[VMEM] * 2,
        out_shape=[shape((rhs, points), F32)] * 2,
        compiler_params=params(58),
        name="update",
    )(all_sums, iterate, direction, residual, image)


def solution(mesh):
    whole = P(None, ("leaf", "tm"))
    first = P(("leaf", "tm"))
    return jax.shard_map(
        shards,
        mesh=mesh,
        in_specs=(whole,) * 4 + (first,) * 7 + (P(), P()),
        out_specs=(whole, whole),
        check_vma=False,
    )
```

```python
import functools
import math

import jax
import jax.numpy as jnp
from jax import lax
from jax.experimental import pallas as pl
from jax.experimental.pallas import tpu as pltpu
from jax.sharding import PartitionSpec as P

F32 = jnp.float32
BF16 = jnp.bfloat16
EXACT = lax.Precision.HIGHEST
LN2 = math.log(2.0)
LOG2E = 1.0 / LN2
UNIT = math.sqrt(3.0) * LOG2E
FACTOR = -LN2 * math.e
VMEM = pl.BlockSpec(memory_space=pltpu.VMEM)
SMEM = pl.BlockSpec(memory_space=pltpu.SMEM)
ANY = pl.BlockSpec(memory_space=pl.ANY)
PART = 256
FIRST_PAIRS = 10


def params(mib, **kw):
    return pltpu.CompilerParams(vmem_limit_bytes=mib * 2**20, **kw)


def contract(a, b, dims, precision=None):
    return lax.dot_general(
        a, b, ((dims[0], dims[1]), ((), ())), precision=precision, preferred_element_type=F32
    )


def rounded(x):
    return x.astype(BF16).astype(F32)


def row_ids(shape):
    return lax.broadcasted_iota(jnp.int32, shape, 0)


def lane_ids(shape):
    return lax.broadcasted_iota(jnp.int32, shape, 1)


def features(xx, want_source, want_target):
    row = row_ids(xx.shape)
    high = rounded(xx)
    low = rounded(xx - high)
    held = high + low
    square = held * held
    square = square + pltpu.roll(square, 1, 0)
    norm = square + pltpu.roll(square, 2, 0)
    n0 = rounded(norm)
    rest = norm - n0
    n1 = rounded(rest)
    n2 = rest - n1
    zero = jnp.zeros_like(xx)
    out = []
    if want_source:
        parts = jnp.where(row < 4, high, low)
        tail = jnp.where(row == 0, n0, jnp.where(row == 1, n1, jnp.where(row == 2, n2, jnp.where(row < 6, 1.0, 0.0))))
        out.append(jnp.concatenate([parts, parts, tail, zero], axis=0).astype(BF16))
    if want_target:
        tail = jnp.where(row < 3, 1.0, jnp.where(row == 3, n0, jnp.where(row == 4, n1, jnp.where(row == 5, n2, 0.0))))
        out.append(jnp.concatenate([-2.0 * high, -2.0 * low, tail, zero], axis=0).astype(BF16))
    return out


def halves(w):
    high = rounded(w)
    return jnp.concatenate([high, w - high], axis=0).astype(BF16)


def kernel_of(z):
    z = jnp.maximum(z, 1e-30)
    q = -LOG2E - z * lax.rsqrt(z)
    return q * jnp.exp2(q)


def split(k):
    high = k.astype(BF16)
    return high, (k - high.astype(F32)).astype(BF16)


def gather_lanes(chunks, ids):
    lane = ids & 127
    chunk = ids >> 7
    picked = [None] * len(chunks)
    for s in range(len(chunks[0])):
        here = chunk == s
        for i, source in enumerate(chunks):
            got = jnp.take_along_axis(source[s](), lane, axis=1, mode="promise_in_bounds")
            picked[i] = got if s == 0 else jnp.where(here, got, picked[i])
    return picked


def scale_rows(scale_ref, shape):
    row = row_ids(shape) & 3
    picked = jnp.where(row == 0, scale_ref[0], jnp.where(row == 1, scale_ref[1], jnp.where(row == 2, scale_ref[2], scale_ref[3])))
    return picked * UNIT


def gather_body(scale_ref, order_hbm, x_hbm, p_hbm, bases_hbm, halo_ref, order_ref, xx, p_ref, bases_ref, sems):
    leaf_dev, rank, leaf_pts = bases_ref.shape
    points = p_ref.shape[1]
    chunks = points // 128
    per_leaf = leaf_pts // 128
    moves = [
        pltpu.make_async_copy(source, target, sems.at[i])
        for i, (source, target) in enumerate(
            [
                (order_hbm, order_ref),
                (x_hbm, xx.at[0:4, :]),
                (x_hbm, xx.at[4:8, :]),
                (p_hbm, p_ref),
                (bases_hbm, bases_ref),
            ]
        )
    ]
    for move in moves:
        move.start()
    for move in moves[:4]:
        move.wait()
    scale = scale_rows(scale_ref, (8, 128))

    def loads(ref):
        return [lambda s=s: ref[:, s * 128 : (s + 1) * 128] for s in range(chunks)]

    def two_leaves(g, _):
        kept = []
        for h in range(2):
            leaf = 2 * g + h
            for j in range(per_leaf):
                ids = order_ref[pl.ds(leaf * per_leaf + j, 1), :]
                got_x, got_p = gather_lanes([loads(xx), loads(p_ref)], jnp.broadcast_to(ids, (8, 128)))
                kept.append(got_x * scale)
                halo_ref[pl.ds(pl.multiple_of(32 + leaf * 8, 8), 8), j * 128 : (j + 1) * 128] = got_p
        for j in range(per_leaf):
            both = jnp.where(row_ids((8, 128)) < 4, kept[j], kept[per_leaf + j])
            halo_ref[pl.ds(pl.multiple_of(g * 8, 8), 8), j * 128 : (j + 1) * 128] = both
        return 0

    lax.fori_loop(0, leaf_dev // 2, two_leaves, 0)
    moves[4].wait()
    for leaf in range(leaf_dev):
        coef = contract(halo_ref[32 + leaf * 8 : 40 + leaf * 8, :], bases_ref[leaf], ((1,), (1,)), EXACT)
        halo_ref[96:104, leaf * rank : (leaf + 1) * rank] = coef


def node_work(order_ref, halo_ref, transfer_ref, skel_ref, node_ref, own_ref, inv_ref, slot):
    chunks = order_ref.shape[0]
    rank = transfer_ref.shape[0]
    leaf_dev = halo_ref.shape[0] // 13
    upper = row_ids((8, 128)) < 4
    for g in range(leaf_dev // 2):
        both = halo_ref[g * 8 : g * 8 + 8, 0:128]
        turned = pltpu.roll(both, 4, 0)
        slot[:, 2 * g * rank : (2 * g + 1) * rank] = jnp.where(upper, both, turned)[:, :rank]
        slot[:, (2 * g + 1) * rank : (2 * g + 2) * rank] = jnp.where(upper, turned, both)[:, :rank]
    weights = contract(halo_ref[96:104, :], transfer_ref[...], ((1,), (1,)), EXACT)
    slots = [lambda s=s: slot[:, s * 128 : (s + 1) * 128] for s in range(leaf_dev * rank // 128)]
    ids = jnp.concatenate([skel_ref[...], skel_ref[...]], axis=1)
    (node_x,) = gather_lanes([slots], jnp.broadcast_to(ids, (8, 128)))
    tile = jnp.concatenate([weights, node_x[:, :rank]], axis=1)
    own_ref[...] = tile
    node_ref[...] = jnp.broadcast_to(tile[None], node_ref.shape)
    tally = jnp.zeros((2 * chunks, 128), F32)
    for c in range(chunks):
        ids = order_ref[c : c + 1, :]
        low = jnp.where(row_ids((128, 128)) == (ids & 127), 1.0, 0.0).astype(BF16)
        row = row_ids((chunks, 128)) == (ids >> 7)
        lane = lane_ids((chunks, 128))
        digit1 = jnp.where(row, (2 * c + (lane >> 6)).astype(F32), 0.0)
        digit0 = jnp.where(row, (lane & 63).astype(F32), 0.0)
        digits = jnp.concatenate([digit1, digit0], axis=0).astype(BF16)
        tally = tally + contract(digits, low, ((1,), (1,)))
    inv_ref[...] = (64.0 * tally[0:chunks] + tally[chunks : 2 * chunks] + 0.5).astype(jnp.int32)


def prepare(ref, base, src, wgt, tgt=None, coef=None):
    leaf_dev = ref.shape[0] // 13
    row = row_ids((8, ref.shape[1]))
    for g in range(leaf_dev // 2):
        both = ref[g * 8 : g * 8 + 8, :]
        turned = pltpu.roll(both, 4, 0)
        for h in range(2):
            leaf = 2 * g + h
            xx = jnp.where(row < 4, both, turned) if h == 0 else jnp.where(row < 4, turned, both)
            made = features(xx, True, tgt is not None)
            src[base + leaf] = made[0]
            if tgt is not None:
                tgt[leaf] = made[1]
            wgt[base + leaf] = halves(ref[32 + leaf * 8 : 40 + leaf * 8, :] * FACTOR)
            if coef is not None:
                rank = coef.shape[2]
                coef[base + leaf] = halves(ref[96:104, leaf * rank : (leaf + 1) * rank] * FACTOR)


def list_pairs(near_ref, count_ref, inside, outside, sizes):
    leaf_dev, slots = near_ref.shape

    def leaf_step(leaf, sums):
        def entry(j, sums):
            w = near_ref[leaf, j]
            here = jnp.where((w // leaf_dev == 4) & (sums[0] < FIRST_PAIRS), 1, 0)
            code = leaf * 128 + w
            inside[sums[0]] = code
            outside[sums[1]] = code
            return sums[0] + here, sums[1] + 1 - here

        return lax.fori_loop(0, count_ref[leaf], entry, sums)

    sums = lax.fori_loop(0, leaf_dev, leaf_step, (0, 0))
    idle = 9 * leaf_dev
    for extra in range(3):
        inside[sums[0] + extra] = idle
        outside[sums[1] + extra] = idle
    sizes[0], sizes[1] = sums
    return sums[0]


def near_pairs(pairs, n, first, src, tgt, wgt, out, z, high, low):
    parts = wgt.shape[2] // PART

    def where(p):
        return pairs[p] >> 7, (pairs[p] & 127) - first

    def distances(p, c, b):
        leaf, w = where(p)
        z[b] = contract(src[w, :, c * PART : (c + 1) * PART], tgt[leaf], ((0,), (0,)))

    def values(b):
        high[b], low[b] = split(kernel_of(z[b]))

    def product(p, c, b):
        _, w = where(p)
        weight = wgt[w, :, c * PART : (c + 1) * PART]
        got = jnp.dot(weight, high[b], preferred_element_type=F32)
        return got + jnp.dot(weight, low[b], preferred_element_type=F32)

    distances(0, 0, 0)
    distances(0, 1, 1)
    values(0)

    def two_pairs(g, _):
        for h in range(2):
            p = 2 * g + h
            got = None
            for c in range(parts):
                b = c % 2
                values(1 - b)
                mine = product(p, c, b)
                got = mine if got is None else got + mine
                distances(p + (c + 2) // parts, (c + 2) % parts, b)
            leaf, _ = where(p)
            out[leaf] += got[:8] + got[8:]
        return 0

    lax.fori_loop(0, (n + 1) // 2, two_pairs, 0)


def inside_body(near_ref, count_ref, halo_hbm, order_ref, transfer_ref, skel_ref, out_ref, node_ref, own_ref, inv_ref, pairs_ref, sizes_ref, pairs, halo_ref, slot, src, tgt, wgt, z, high, low, sem):
    leaf_dev, rhs, leaf_pts = out_ref.shape
    move = pltpu.make_async_copy(halo_hbm, halo_ref, sem)
    move.start()
    n = list_pairs(near_ref, count_ref, pairs, pairs_ref, sizes_ref)
    for extra in range(3):
        pairs[n + extra] = 5 * leaf_dev
    src[leaf_dev] = jnp.zeros(src.shape[1:], BF16)
    wgt[leaf_dev] = jnp.zeros(wgt.shape[1:], BF16)
    out_ref[...] = jnp.zeros_like(out_ref)
    move.wait()
    node_work(order_ref, halo_ref, transfer_ref, skel_ref, node_ref, own_ref, inv_ref, slot)
    prepare(halo_ref, 0, src, wgt, tgt)
    near_pairs(pairs, n, 4 * leaf_dev, src, tgt, wgt, out_ref, z, high, low)


def node_field(tm_size, place_ref, node_ref, own_ref, transfer_ref, node_src, node_wgt):
    devices = node_ref.shape[0]
    rank = own_ref.shape[1] // 2
    lane = lane_ids((8, 128))

    def distant(e):
        far_a = jnp.abs(e // tm_size - place_ref[0]) > 1
        far_b = jnp.abs(e % tm_size - place_ref[1]) > 1
        return jnp.where(far_a | far_b, FACTOR, 0.0)

    def unpack(g, _):
        xs, ws = [], []
        for k in range(4):
            e = 8 * g + 2 * k
            one, two = node_ref[e], node_ref[e + 1]
            xs.append(jnp.where(lane < rank, pltpu.roll(one, rank, 1), two))
            ws.append(jnp.where(lane < rank, one * distant(e), pltpu.roll(two, rank, 1) * distant(e + 1)))
        at = pl.ds(pl.multiple_of(g * 512, 512), 512)
        node_src[:, at] = features(jnp.concatenate(xs, axis=1), True, False)[0]
        node_wgt[:, at] = halves(jnp.concatenate(ws, axis=1))
        return 0

    lax.fori_loop(0, devices // 8, unpack, 0, unroll=4)
    own_xx = pltpu.roll(own_ref[...], rank, 1)
    target = features(own_xx, False, True)[0][:, :rank]
    total = jnp.zeros((16, rank), F32)
    step = 512
    for q in range(0, devices * rank, step):
        z_far = contract(target, node_src[:, q : q + step], ((0,), (0,)))
        k_high, k_low = split(kernel_of(z_far))
        weight = node_wgt[:, q : q + step]
        total = total + contract(weight, k_high, ((1,), (1,)))
        total = total + contract(weight, k_low, ((1,), (1,)))
    return jnp.dot(total[:8] + total[8:], transfer_ref[...], precision=EXACT, preferred_element_type=F32)


def outside_body(pairs_ref, sizes_ref, far_ref, row_ref, up_ref, down_ref, out_ref, far_out_ref, src, tgt, wgt, coef, far_src, far_wgt, z, high, low):
    leaf_dev, rhs, leaf_pts = out_ref.shape
    rank = coef.shape[2]
    idle = 9 * leaf_dev
    src[idle] = jnp.zeros(src.shape[1:], BF16)
    wgt[idle] = jnp.zeros(wgt.shape[1:], BF16)
    for k in range(3):
        prepare(up_ref.at[k], k * leaf_dev, src, wgt, None, coef)
        prepare(row_ref.at[k], (3 + k) * leaf_dev, src, wgt, tgt if k == 1 else None, coef)
        prepare(down_ref.at[k], (6 + k) * leaf_dev, src, wgt, None, coef)
    out_ref[...] = jnp.zeros_like(out_ref)
    near_pairs(pairs_ref, sizes_ref[1], 0, src, tgt, wgt, out_ref, z, high, low)
    for leaf in range(leaf_dev):
        for j in range(far_ref.shape[1]):
            w = far_ref[leaf, j]
            at = slice(j * rank, (j + 1) * rank)
            far_src[leaf, :, at] = src[w, :, 0:rank]
            far_wgt[leaf, :, at] = coef[w]
    for leaf in range(leaf_dev):
        k_high, k_low = split(kernel_of(contract(tgt[leaf, :, 0:rank], far_src[leaf], ((0,), (0,)))))
        far = contract(far_wgt[leaf], k_high, ((1,), (1,))) + contract(far_wgt[leaf], k_low, ((1,), (1,)))
        far_out_ref[leaf] = far[:8] + far[8:]


def tail_body(tm_size, place_ref, noise_ref, inside_ref, near_ref, far_ref, node_ref, own_ref, transfer_ref, bases_ref, inv_ref, p_ref, res_ref, image_ref, sums_ref, flat, node_src, node_wgt):
    leaf_dev, rank, leaf_pts = bases_ref.shape
    pushed = node_field(tm_size, place_ref, node_ref, own_ref, transfer_ref, node_src, node_wgt)
    for leaf in range(leaf_dev):
        incoming = halves(far_ref[leaf] + pushed[:, leaf * rank : (leaf + 1) * rank])
        base_high, base_low = split(bases_ref[leaf])
        got = jnp.dot(incoming, base_high, preferred_element_type=F32)
        got = got + jnp.dot(incoming, base_low, preferred_element_type=F32)
        flat[:, leaf * leaf_pts : (leaf + 1) * leaf_pts] = inside_ref[leaf] + near_ref[leaf] + got[:8] + got[8:]

    chunks = flat.shape[1] // 128
    row = row_ids((8, 128))
    lane = lane_ids((8, 128))
    source = [lambda s=s: flat[:, s * 128 : (s + 1) * 128] for s in range(chunks)]
    noise = jnp.zeros((8, 128), F32)
    for r in range(8):
        noise = jnp.where(row == r, noise_ref[r], noise)

    def place(g, sums):
        along, squares = sums
        for h in range(4):
            c = 4 * g + h
            at = pl.ds(pl.multiple_of(c * 128, 128), 128)
            ids = jnp.broadcast_to(inv_ref[pl.ds(c, 1), :], (8, 128))
            (part,) = gather_lanes([source], ids)
            image = part + noise * p_ref[:, at]
            image_ref[:, at] = image
            along, squares = along + res_ref[:, at] * image, squares + image * image
        return along, squares

    zero = jnp.zeros((8, 128), F32)
    along, squares = lax.fori_loop(0, chunks // 4, place, (zero, zero))
    along = jnp.sum(along, axis=1, keepdims=True)
    squares = jnp.sum(squares, axis=1, keepdims=True)
    both = jnp.where(lane == row, along, 0.0) + jnp.where(lane == row + 8, squares, 0.0)
    sums_ref[...] = jnp.broadcast_to(jnp.sum(both, axis=0, keepdims=True), sums_ref.shape)


def update_body(sums_ref, it_ref, p_ref, res_ref, image_ref, new_it_ref, new_res_ref):
    total = jnp.sum(sums_ref[...], axis=0, keepdims=True)
    row = row_ids((8, 128))
    lane = lane_ids((8, 128))
    along = jnp.sum(jnp.where(lane == row, total, 0.0), axis=1, keepdims=True)
    squares = jnp.sum(jnp.where(lane == row + 8, total, 0.0), axis=1, keepdims=True)
    alpha = along / (squares + 1e-06)
    new_it_ref[...] = it_ref[...] + alpha * p_ref[...]
    new_res_ref[...] = res_ref[...] - alpha * image_ref[...]


def shifted(x, axis, by):
    n = lax.axis_size(axis)
    return lax.ppermute(x, axis, [(i, i + by) for i in range(n) if 0 <= i + by < n])


def shards(coords, direction, iterate, residual, order, bases, transfer, near_list, near_count, far_list, device_skel, inv_scale, noise):
    leaf_dev, rank, leaf_pts = bases.shape
    rhs, points = direction.shape
    axes = ("leaf", "tm")
    devices = lax.axis_size("leaf") * lax.axis_size("tm")
    chunks = points // 128
    shape = jax.ShapeDtypeStruct
    by_row = order.reshape(chunks, 128)
    halo = pl.pallas_call(
        gather_body,
        in_specs=[SMEM] + [ANY] * 4,
        out_specs=VMEM,
        out_shape=shape((13 * leaf_dev, leaf_pts), F32),
        scratch_shapes=[
            pltpu.VMEM((chunks, 128), jnp.int32),
            pltpu.VMEM((8, points), F32),
            pltpu.VMEM((rhs, points), F32),
            pltpu.VMEM(bases.shape, F32),
            pltpu.SemaphoreType.DMA((5,)),
        ],
        compiler_params=params(60),
        name="gather",
    )(inv_scale, by_row, coords, direction, bases)
    left = shifted(halo, "tm", 1)
    right = shifted(halo, "tm", -1)

    def pipeline(sources):
        return [
            pltpu.VMEM((sources + 1, 32, leaf_pts), BF16),
            pltpu.VMEM((leaf_dev, 32, leaf_pts), BF16),
            pltpu.VMEM((sources + 1, 16, leaf_pts), BF16),
        ]

    buffers = [
        pltpu.VMEM((2, PART, leaf_pts), F32),
        pltpu.VMEM((2, PART, leaf_pts), BF16),
        pltpu.VMEM((2, PART, leaf_pts), BF16),
    ]
    entries = near_list.size + 4
    inside, node, own, inverse, pairs, sizes = pl.pallas_call(
        inside_body,
        in_specs=[SMEM] * 2 + [ANY] + [VMEM] * 3,
        out_specs=[VMEM] * 4 + [SMEM] * 2,
        out_shape=[
            shape((leaf_dev, rhs, leaf_pts), F32),
            shape((devices, 8, 128), F32),
            shape((8, 128), F32),
            shape((chunks, 128), jnp.int32),
            shape((entries,), jnp.int32),
            shape((2,), jnp.int32),
        ],
        scratch_shapes=[
            pltpu.SMEM((entries,), jnp.int32),
            pltpu.VMEM(halo.shape, F32),
            pltpu.VMEM((8, leaf_dev * rank), F32),
        ]
        + pipeline(leaf_dev)
        + buffers
        + [pltpu.SemaphoreType.DMA(())],
        compiler_params=params(58),
        cost_estimate=pl.CostEstimate(flops=10**10, bytes_accessed=2**21, transcendentals=10**7),
        name="inside",
    )(near_list, near_count, halo, by_row, transfer[0], device_skel)
    left, right, inside, node = lax.optimization_barrier((left, right, inside, node))
    nodes = lax.all_to_all(node, axes, 0, 0)
    row = jnp.stack([left, halo, right])
    up = shifted(row, "leaf", 1)
    down = shifted(row, "leaf", -1)
    place = jnp.stack([lax.axis_index("leaf"), lax.axis_index("tm")]).astype(jnp.int32)

    near, far = pl.pallas_call(
        outside_body,
        in_specs=[SMEM] * 3 + [VMEM] * 3,
        out_specs=[VMEM] * 2,
        out_shape=[shape((leaf_dev, rhs, leaf_pts), F32), shape((leaf_dev, rhs, rank), F32)],
        scratch_shapes=pipeline(9 * leaf_dev)
        + [
            pltpu.VMEM((9 * leaf_dev, 16, rank), BF16),
            pltpu.VMEM((leaf_dev, 32, far_list.shape[1] * rank), BF16),
            pltpu.VMEM((leaf_dev, 16, far_list.shape[1] * rank), BF16),
        ]
        + buffers,
        compiler_params=params(14),
        cost_estimate=pl.CostEstimate(flops=3 * 10**10, bytes_accessed=2**21, transcendentals=3 * 10**7),
        name="outside",
    )(pairs, sizes, far_list, row, up, down)
    image, sums = pl.pallas_call(
        functools.partial(tail_body, lax.axis_size("tm")),
        in_specs=[SMEM] * 2 + [VMEM] * 10,
        out_specs=[VMEM] * 2,
        out_shape=[shape((rhs, points), F32), shape((devices, 128), F32)],
        scratch_shapes=[
            pltpu.VMEM((rhs, points), F32),
            pltpu.VMEM((32, devices * rank), BF16),
            pltpu.VMEM((16, devices * rank), BF16),
        ],
        compiler_params=params(10),
        name="tail",
    )(place, noise, inside, near, far, nodes, own, transfer[0], bases, inverse, direction, residual)
    all_sums = lax.all_to_all(sums, axes, 0, 0, tiled=True)
    return pl.pallas_call(
        update_body,
        in_specs=[VMEM] * 5,
        out_specs=[VMEM] * 2,
        out_shape=[shape((rhs, points), F32)] * 2,
        compiler_params=params(8),
        name="update",
    )(all_sums, iterate, direction, residual, image)


def solution(mesh):
    whole = P(None, ("leaf", "tm"))
    first = P(("leaf", "tm"))
    return jax.shard_map(
        shards,
        mesh=mesh,
        in_specs=(whole,) * 4 + (first,) * 7 + (P(), P()),
        out_specs=(whole, whole),
        check_vma=False,
    )
```

```python
import functools
import math

import jax
import jax.numpy as jnp
from jax import lax
from jax.experimental import pallas as pl
from jax.experimental.pallas import tpu as pltpu
from jax.sharding import PartitionSpec as P

F32 = jnp.float32
BF16 = jnp.bfloat16
EXACT = lax.Precision.HIGHEST
LN2 = math.log(2.0)
LOG2E = 1.0 / LN2
UNIT = math.sqrt(3.0) * LOG2E
FACTOR = -LN2 * math.e
VMEM = pl.BlockSpec(memory_space=pltpu.VMEM)
SMEM = pl.BlockSpec(memory_space=pltpu.SMEM)
ANY = pl.BlockSpec(memory_space=pl.ANY)
PART = 256
FIRST_PAIRS = 10


def params(mib, **kw):
    return pltpu.CompilerParams(vmem_limit_bytes=mib * 2**20, **kw)


def contract(a, b, dims, precision=None):
    return lax.dot_general(
        a, b, ((dims[0], dims[1]), ((), ())), precision=precision, preferred_element_type=F32
    )


def rounded(x):
    return x.astype(BF16).astype(F32)


def row_ids(shape):
    return lax.broadcasted_iota(jnp.int32, shape, 0)


def lane_ids(shape):
    return lax.broadcasted_iota(jnp.int32, shape, 1)


def features(xx, want_source, want_target):
    row = row_ids(xx.shape)
    high = rounded(xx)
    low = rounded(xx - high)
    held = high + low
    square = held * held
    square = square + pltpu.roll(square, 1, 0)
    norm = square + pltpu.roll(square, 2, 0)
    n0 = rounded(norm)
    rest = norm - n0
    n1 = rounded(rest)
    n2 = rest - n1
    zero = jnp.zeros_like(xx)
    out = []
    if want_source:
        parts = jnp.where(row < 4, high, low)
        tail = jnp.where(row == 0, n0, jnp.where(row == 1, n1, jnp.where(row == 2, n2, jnp.where(row < 6, 1.0, 0.0))))
        out.append(jnp.concatenate([parts, parts, tail, zero], axis=0).astype(BF16))
    if want_target:
        tail = jnp.where(row < 3, 1.0, jnp.where(row == 3, n0, jnp.where(row == 4, n1, jnp.where(row == 5, n2, 0.0))))
        out.append(jnp.concatenate([-2.0 * high, -2.0 * low, tail, zero], axis=0).astype(BF16))
    return out


def halves(w):
    high = rounded(w)
    return jnp.concatenate([high, w - high], axis=0).astype(BF16)


def kernel_of(z):
    z = jnp.maximum(z, 1e-30)
    q = -LOG2E - z * lax.rsqrt(z)
    return q * jnp.exp2(q)


def split(k):
    high = k.astype(BF16)
    return high, (k - high.astype(F32)).astype(BF16)


def gather_lanes(chunks, ids):
    lane = ids & 127
    chunk = ids >> 7
    picked = [None] * len(chunks)
    for s in range(len(chunks[0])):
        here = chunk == s
        for i, source in enumerate(chunks):
            got = jnp.take_along_axis(source[s](), lane, axis=1, mode="promise_in_bounds")
            picked[i] = got if s == 0 else jnp.where(here, got, picked[i])
    return picked


def fetch(sources, targets, sems):
    moves = [pltpu.make_async_copy(a, b, sems.at[i]) for i, (a, b) in enumerate(zip(sources, targets))]
    for move in moves:
        move.start()
    return moves


def scale_rows(scale_ref, shape):
    row = row_ids(shape) & 3
    picked = jnp.where(row == 0, scale_ref[0], jnp.where(row == 1, scale_ref[1], jnp.where(row == 2, scale_ref[2], scale_ref[3])))
    return picked * UNIT


def gather_body(scale_hbm, order_hbm, x_hbm, p_hbm, bases_hbm, transfer_hbm, skel_hbm, halo_ref, node_ref, own_ref, scale_ref, order_ref, xx, p_ref, bases_ref, transfer_ref, skel_ref, slot, sems):
    leaf_dev, rank, leaf_pts = bases_ref.shape
    points = p_ref.shape[1]
    chunks = points // 128
    per_leaf = leaf_pts // 128
    moves = fetch(
        [order_hbm, x_hbm, x_hbm, p_hbm, scale_hbm, bases_hbm, transfer_hbm, skel_hbm],
        [order_ref, xx.at[0:4, :], xx.at[4:8, :], p_ref, scale_ref, bases_ref, transfer_ref, skel_ref],
        sems,
    )
    for move in moves[:5]:
        move.wait()
    scale = scale_rows(scale_ref, (8, 128))

    def loads(ref):
        return [lambda s=s: ref[:, s * 128 : (s + 1) * 128] for s in range(chunks)]

    def two_leaves(g, _):
        kept = []
        for h in range(2):
            leaf = 2 * g + h
            for j in range(per_leaf):
                ids = order_ref[pl.ds(leaf * per_leaf + j, 1), :]
                got_x, got_p = gather_lanes([loads(xx), loads(p_ref)], jnp.broadcast_to(ids, (8, 128)))
                kept.append(got_x * scale)
                halo_ref[pl.ds(pl.multiple_of(32 + leaf * 8, 8), 8), j * 128 : (j + 1) * 128] = got_p
        for j in range(per_leaf):
            both = jnp.where(row_ids((8, 128)) < 4, kept[j], kept[per_leaf + j])
            halo_ref[pl.ds(pl.multiple_of(g * 8, 8), 8), j * 128 : (j + 1) * 128] = both
        return 0

    lax.fori_loop(0, leaf_dev // 2, two_leaves, 0)
    for move in moves[5:]:
        move.wait()
    for leaf in range(leaf_dev):
        coef = contract(halo_ref[32 + leaf * 8 : 40 + leaf * 8, :], bases_ref[leaf], ((1,), (1,)), EXACT)
        halo_ref[96:104, leaf * rank : (leaf + 1) * rank] = coef
    upper = row_ids((8, 128)) < 4
    for g in range(leaf_dev // 2):
        both = halo_ref[g * 8 : g * 8 + 8, 0:128]
        turned = pltpu.roll(both, 4, 0)
        slot[:, 2 * g * rank : (2 * g + 1) * rank] = jnp.where(upper, both, turned)[:, :rank]
        slot[:, (2 * g + 1) * rank : (2 * g + 2) * rank] = jnp.where(upper, turned, both)[:, :rank]
    weights = contract(halo_ref[96:104, :], transfer_ref[...], ((1,), (1,)), EXACT)
    slots = [lambda s=s: slot[:, s * 128 : (s + 1) * 128] for s in range(leaf_dev * rank // 128)]
    ids = jnp.concatenate([skel_ref[...], skel_ref[...]], axis=1)
    (node_x,) = gather_lanes([slots], jnp.broadcast_to(ids, (8, 128)))
    tile = jnp.concatenate([weights, node_x[:, :rank]], axis=1)
    own_ref[...] = tile
    node_ref[...] = jnp.broadcast_to(tile[None], node_ref.shape)


def place_of(order_ref):
    chunks = order_ref.shape[0]
    tally = jnp.zeros((2 * chunks, 128), F32)
    for c in range(chunks):
        ids = order_ref[c : c + 1, :]
        low = jnp.where(row_ids((128, 128)) == (ids & 127), 1.0, 0.0).astype(BF16)
        row = row_ids((chunks, 128)) == (ids >> 7)
        lane = lane_ids((chunks, 128))
        digit1 = jnp.where(row, (2 * c + (lane >> 6)).astype(F32), 0.0)
        digit0 = jnp.where(row, (lane & 63).astype(F32), 0.0)
        digits = jnp.concatenate([digit1, digit0], axis=0).astype(BF16)
        tally = tally + contract(digits, low, ((1,), (1,)))
    return (64.0 * tally[0:chunks] + tally[chunks : 2 * chunks] + 0.5).astype(jnp.int32)


def prepare(ref, base, src, wgt, tgt=None, coef=None):
    leaf_dev = ref.shape[0] // 13
    row = row_ids((8, ref.shape[1]))
    for g in range(leaf_dev // 2):
        both = ref[g * 8 : g * 8 + 8, :]
        turned = pltpu.roll(both, 4, 0)
        for h in range(2):
            leaf = 2 * g + h
            xx = jnp.where(row < 4, both, turned) if h == 0 else jnp.where(row < 4, turned, both)
            made = features(xx, True, tgt is not None)
            src[base + leaf] = made[0]
            if tgt is not None:
                tgt[leaf] = made[1]
            wgt[base + leaf] = halves(ref[32 + leaf * 8 : 40 + leaf * 8, :] * FACTOR)
            if coef is not None:
                rank = coef.shape[2]
                coef[base + leaf] = halves(ref[96:104, leaf * rank : (leaf + 1) * rank] * FACTOR)


def list_pairs(near_ref, count_ref, inside, outside, sizes):
    leaf_dev, slots = near_ref.shape

    def leaf_step(leaf, sums):
        def entry(j, sums):
            w = near_ref[leaf, j]
            here = jnp.where((w // leaf_dev == 4) & (sums[0] < FIRST_PAIRS), 1, 0)
            code = leaf * 128 + w
            inside[sums[0]] = code
            outside[sums[1]] = code
            return sums[0] + here, sums[1] + 1 - here

        return lax.fori_loop(0, count_ref[leaf], entry, sums)

    sums = lax.fori_loop(0, leaf_dev, leaf_step, (0, 0))
    idle = 9 * leaf_dev
    for extra in range(3):
        inside[sums[0] + extra] = idle
        outside[sums[1] + extra] = idle
    sizes[0], sizes[1] = sums
    return sums[0]


def near_pairs(pairs, n, first, src, tgt, wgt, out, z, high, low):
    parts = wgt.shape[2] // PART

    def where(p):
        return pairs[p] >> 7, (pairs[p] & 127) - first

    def distances(p, c, b):
        leaf, w = where(p)
        z[b] = contract(src[w, :, c * PART : (c + 1) * PART], tgt[leaf], ((0,), (0,)))

    def values(b):
        high[b], low[b] = split(kernel_of(z[b]))

    def product(p, c, b):
        _, w = where(p)
        weight = wgt[w, :, c * PART : (c + 1) * PART]
        got = jnp.dot(weight, high[b], preferred_element_type=F32)
        return got + jnp.dot(weight, low[b], preferred_element_type=F32)

    distances(0, 0, 0)
    distances(0, 1, 1)
    values(0)

    def two_pairs(g, _):
        for h in range(2):
            p = 2 * g + h
            got = None
            for c in range(parts):
                b = c % 2
                values(1 - b)
                mine = product(p, c, b)
                got = mine if got is None else got + mine
                distances(p + (c + 2) // parts, (c + 2) % parts, b)
            leaf, _ = where(p)
            out[leaf] += got[:8] + got[8:]
        return 0

    lax.fori_loop(0, (n + 1) // 2, two_pairs, 0)


def inside_body(near_ref, count_ref, halo_hbm, order_ref, out_ref, inv_ref, pairs_ref, sizes_ref, pairs, halo_ref, src, tgt, wgt, z, high, low, sem):
    leaf_dev, rhs, leaf_pts = out_ref.shape
    move = pltpu.make_async_copy(halo_hbm, halo_ref, sem)
    move.start()
    n = list_pairs(near_ref, count_ref, pairs, pairs_ref, sizes_ref)
    for extra in range(3):
        pairs[n + extra] = 5 * leaf_dev
    src[leaf_dev] = jnp.zeros(src.shape[1:], BF16)
    wgt[leaf_dev] = jnp.zeros(wgt.shape[1:], BF16)
    out_ref[...] = jnp.zeros_like(out_ref)
    move.wait()
    inv_ref[...] = place_of(order_ref)
    prepare(halo_ref, 0, src, wgt, tgt)
    near_pairs(pairs, n, 4 * leaf_dev, src, tgt, wgt, out_ref, z, high, low)


def node_field(leaf_size, place_ref, node_ref, own_ref, transfer_ref, node_src, node_wgt):
    devices = node_ref.shape[0]
    rank = own_ref.shape[1] // 2
    lane = lane_ids((8, 128))

    def distant(e):
        far_a = jnp.abs(e % leaf_size - place_ref[0]) > 1
        far_b = jnp.abs(e // leaf_size - place_ref[1]) > 1
        return jnp.where(far_a | far_b, FACTOR, 0.0)

    def unpack(g, _):
        xs, ws = [], []
        for k in range(4):
            e = 8 * g + 2 * k
            one, two = node_ref[e], node_ref[e + 1]
            xs.append(jnp.where(lane < rank, pltpu.roll(one, rank, 1), two))
            ws.append(jnp.where(lane < rank, one * distant(e), pltpu.roll(two, rank, 1) * distant(e + 1)))
        at = pl.ds(pl.multiple_of(g * 512, 512), 512)
        node_src[:, at] = features(jnp.concatenate(xs, axis=1), True, False)[0]
        node_wgt[:, at] = halves(jnp.concatenate(ws, axis=1))
        return 0

    lax.fori_loop(0, devices // 8, unpack, 0, unroll=4)
    own_xx = pltpu.roll(own_ref[...], rank, 1)
    target = features(own_xx, False, True)[0][:, :rank]
    total = jnp.zeros((16, rank), F32)
    step = 512
    for q in range(0, devices * rank, step):
        z_far = contract(target, node_src[:, q : q + step], ((0,), (0,)))
        k_high, k_low = split(kernel_of(z_far))
        weight = node_wgt[:, q : q + step]
        total = total + contract(weight, k_high, ((1,), (1,)))
        total = total + contract(weight, k_low, ((1,), (1,)))
    return jnp.dot(total[:8] + total[8:], transfer_ref[...], precision=EXACT, preferred_element_type=F32)


def outside_body(pairs_ref, sizes_ref, far_ref, row_ref, up_ref, down_ref, out_ref, far_out_ref, src, tgt, wgt, coef, far_src, far_wgt, z, high, low):
    leaf_dev, rhs, leaf_pts = out_ref.shape
    rank = coef.shape[2]
    idle = 9 * leaf_dev
    src[idle] = jnp.zeros(src.shape[1:], BF16)
    wgt[idle] = jnp.zeros(wgt.shape[1:], BF16)
    for k in range(3):
        prepare(up_ref.at[k], k * leaf_dev, src, wgt, None, coef)
        prepare(row_ref.at[k], (3 + k) * leaf_dev, src, wgt, tgt if k == 1 else None, coef)
        prepare(down_ref.at[k], (6 + k) * leaf_dev, src, wgt, None, coef)
    out_ref[...] = jnp.zeros_like(out_ref)
    near_pairs(pairs_ref, sizes_ref[1], 0, src, tgt, wgt, out_ref, z, high, low)
    for leaf in range(leaf_dev):
        for j in range(far_ref.shape[1]):
            w = far_ref[leaf, j]
            at = slice(j * rank, (j + 1) * rank)
            far_src[leaf, :, at] = src[w, :, 0:rank]
            far_wgt[leaf, :, at] = coef[w]
    for leaf in range(leaf_dev):
        k_high, k_low = split(kernel_of(contract(tgt[leaf, :, 0:rank], far_src[leaf], ((0,), (0,)))))
        far = contract(far_wgt[leaf], k_high, ((1,), (1,))) + contract(far_wgt[leaf], k_low, ((1,), (1,)))
        far_out_ref[leaf] = far[:8] + far[8:]


def tail_body(leaf_size, place_ref, noise_ref, inside_ref, near_ref, far_ref, node_ref, own_ref, transfer_ref, bases_ref, inv_ref, p_ref, res_ref, image_ref, sums_ref, flat, node_src, node_wgt):
    leaf_dev, rank, leaf_pts = bases_ref.shape
    pushed = node_field(leaf_size, place_ref, node_ref, own_ref, transfer_ref, node_src, node_wgt)
    for leaf in range(leaf_dev):
        incoming = halves(far_ref[leaf] + pushed[:, leaf * rank : (leaf + 1) * rank])
        base_high, base_low = split(bases_ref[leaf])
        got = jnp.dot(incoming, base_high, preferred_element_type=F32)
        got = got + jnp.dot(incoming, base_low, preferred_element_type=F32)
        flat[:, leaf * leaf_pts : (leaf + 1) * leaf_pts] = inside_ref[leaf] + near_ref[leaf] + got[:8] + got[8:]

    chunks = flat.shape[1] // 128
    row = row_ids((8, 128))
    lane = lane_ids((8, 128))
    source = [lambda s=s: flat[:, s * 128 : (s + 1) * 128] for s in range(chunks)]
    noise = jnp.zeros((8, 128), F32)
    for r in range(8):
        noise = jnp.where(row == r, noise_ref[r], noise)

    def place(g, sums):
        along, squares = sums
        for h in range(4):
            c = 4 * g + h
            at = pl.ds(pl.multiple_of(c * 128, 128), 128)
            ids = jnp.broadcast_to(inv_ref[pl.ds(c, 1), :], (8, 128))
            (part,) = gather_lanes([source], ids)
            image = part + noise * p_ref[:, at]
            image_ref[:, at] = image
            along, squares = along + res_ref[:, at] * image, squares + image * image
        return along, squares

    zero = jnp.zeros((8, 128), F32)
    along, squares = lax.fori_loop(0, chunks // 4, place, (zero, zero))
    along = jnp.sum(along, axis=1, keepdims=True)
    squares = jnp.sum(squares, axis=1, keepdims=True)
    both = jnp.where(lane == row, along, 0.0) + jnp.where(lane == row + 8, squares, 0.0)
    sums_ref[...] = jnp.broadcast_to(jnp.sum(both, axis=0, keepdims=True), sums_ref.shape)


def update_body(sums_ref, it_ref, p_ref, res_ref, image_ref, new_it_ref, new_res_ref):
    total = jnp.sum(sums_ref[...], axis=0, keepdims=True)
    row = row_ids((8, 128))
    lane = lane_ids((8, 128))
    along = jnp.sum(jnp.where(lane == row, total, 0.0), axis=1, keepdims=True)
    squares = jnp.sum(jnp.where(lane == row + 8, total, 0.0), axis=1, keepdims=True)
    alpha = along / (squares + 1e-06)
    new_it_ref[...] = it_ref[...] + alpha * p_ref[...]
    new_res_ref[...] = res_ref[...] - alpha * image_ref[...]


def shifted(x, axis, by):
    n = lax.axis_size(axis)
    return lax.ppermute(x, axis, [(i, i + by) for i in range(n) if 0 <= i + by < n])


def shards(coords, direction, iterate, residual, order, bases, transfer, near_list, near_count, far_list, device_skel, inv_scale, noise):
    leaf_dev, rank, leaf_pts = bases.shape
    rhs, points = direction.shape
    axes = ("leaf", "tm")
    devices = lax.axis_size("leaf") * lax.axis_size("tm")
    chunks = points // 128
    shape = jax.ShapeDtypeStruct
    by_row = order.reshape(chunks, 128)
    halo, node, own = pl.pallas_call(
        gather_body,
        in_specs=[ANY] * 7,
        out_specs=[VMEM] * 3,
        out_shape=[
            shape((13 * leaf_dev, leaf_pts), F32),
            shape((lax.axis_size("leaf"), 8, 128), F32),
            shape((8, 128), F32),
        ],
        scratch_shapes=[
            pltpu.SMEM(inv_scale.shape, F32),
            pltpu.VMEM((chunks, 128), jnp.int32),
            pltpu.VMEM((8, points), F32),
            pltpu.VMEM((rhs, points), F32),
            pltpu.VMEM(bases.shape, F32),
            pltpu.VMEM(transfer.shape[1:], F32),
            pltpu.VMEM(device_skel.shape, jnp.int32),
            pltpu.VMEM((8, leaf_dev * rank), F32),
            pltpu.SemaphoreType.DMA((8,)),
        ],
        compiler_params=params(60),
        name="gather",
    )(inv_scale, by_row, coords, direction, bases, transfer[0], device_skel)
    left = shifted(halo, "tm", 1)
    right = shifted(halo, "tm", -1)

    def pipeline(sources):
        return [
            pltpu.VMEM((sources + 1, 32, leaf_pts), BF16),
            pltpu.VMEM((leaf_dev, 32, leaf_pts), BF16),
            pltpu.VMEM((sources + 1, 16, leaf_pts), BF16),
        ]

    buffers = [
        pltpu.VMEM((2, PART, leaf_pts), F32),
        pltpu.VMEM((2, PART, leaf_pts), BF16),
        pltpu.VMEM((2, PART, leaf_pts), BF16),
    ]
    entries = near_list.size + 4
    column = lax.all_to_all(node, "leaf", 0, 0)
    inside, inverse, pairs, sizes = pl.pallas_call(
        inside_body,
        in_specs=[SMEM] * 2 + [ANY] + [VMEM],
        out_specs=[VMEM] * 2 + [SMEM] * 2,
        out_shape=[
            shape((leaf_dev, rhs, leaf_pts), F32),
            shape((chunks, 128), jnp.int32),
            shape((entries,), jnp.int32),
            shape((2,), jnp.int32),
        ],
        scratch_shapes=[
            pltpu.SMEM((entries,), jnp.int32),
            pltpu.VMEM(halo.shape, F32),
        ]
        + pipeline(leaf_dev)
        + buffers
        + [pltpu.SemaphoreType.DMA(())],
        compiler_params=params(58),
        cost_estimate=pl.CostEstimate(flops=10**10, bytes_accessed=2**21, transcendentals=10**7),
        name="inside",
    )(near_list, near_count, halo, by_row)
    left, right, inside, column = lax.optimization_barrier((left, right, inside, column))
    nodes = lax.all_to_all(jnp.broadcast_to(column[None], (lax.axis_size("tm"),) + column.shape), "tm", 0, 0)
    nodes = nodes.reshape(devices, 8, 128)
    row = jnp.stack([left, halo, right])
    up = shifted(row, "leaf", 1)
    down = shifted(row, "leaf", -1)
    place = jnp.stack([lax.axis_index("leaf"), lax.axis_index("tm")]).astype(jnp.int32)

    near, far = pl.pallas_call(
        outside_body,
        in_specs=[SMEM] * 3 + [VMEM] * 3,
        out_specs=[VMEM] * 2,
        out_shape=[shape((leaf_dev, rhs, leaf_pts), F32), shape((leaf_dev, rhs, rank), F32)],
        scratch_shapes=pipeline(9 * leaf_dev)
        + [
            pltpu.VMEM((9 * leaf_dev, 16, rank), BF16),
            pltpu.VMEM((leaf_dev, 32, far_list.shape[1] * rank), BF16),
            pltpu.VMEM((leaf_dev, 16, far_list.shape[1] * rank), BF16),
        ]
        + buffers,
        compiler_params=params(14),
        cost_estimate=pl.CostEstimate(flops=3 * 10**10, bytes_accessed=2**21, transcendentals=3 * 10**7),
        name="outside",
    )(pairs, sizes, far_list, row, up, down)
    image, sums = pl.pallas_call(
        functools.partial(tail_body, lax.axis_size("leaf")),
        in_specs=[SMEM] * 2 + [VMEM] * 10,
        out_specs=[VMEM] * 2,
        out_shape=[shape((rhs, points), F32), shape((devices, 128), F32)],
        scratch_shapes=[
            pltpu.VMEM((rhs, points), F32),
            pltpu.VMEM((32, devices * rank), BF16),
            pltpu.VMEM((16, devices * rank), BF16),
        ],
        compiler_params=params(10),
        name="tail",
    )(place, noise, inside, near, far, nodes, own, transfer[0], bases, inverse, direction, residual)
    all_sums = lax.all_to_all(sums, axes, 0, 0, tiled=True)
    return pl.pallas_call(
        update_body,
        in_specs=[VMEM] * 5,
        out_specs=[VMEM] * 2,
        out_shape=[shape((rhs, points), F32)] * 2,
        compiler_params=params(8),
        name="update",
    )(all_sums, iterate, direction, residual, image)


def solution(mesh):
    whole = P(None, ("leaf", "tm"))
    first = P(("leaf", "tm"))
    return jax.shard_map(
        shards,
        mesh=mesh,
        in_specs=(whole,) * 4 + (first,) * 7 + (P(), P()),
        out_specs=(whole, whole),
        check_vma=False,
    )
```

```python
import functools
import math

import jax
import jax.numpy as jnp
from jax import lax
from jax.experimental import pallas as pl
from jax.experimental.pallas import tpu as pltpu
from jax.sharding import PartitionSpec as P

F32 = jnp.float32
BF16 = jnp.bfloat16
EXACT = lax.Precision.HIGHEST
LN2 = math.log(2.0)
LOG2E = 1.0 / LN2
UNIT = math.sqrt(3.0) * LOG2E
FACTOR = -LN2 * math.e
VMEM = pl.BlockSpec(memory_space=pltpu.VMEM)
SMEM = pl.BlockSpec(memory_space=pltpu.SMEM)
ANY = pl.BlockSpec(memory_space=pl.ANY)
PART = 256
FIRST_PAIRS = 10


def params(mib, **kw):
    return pltpu.CompilerParams(vmem_limit_bytes=mib * 2**20, **kw)


def contract(a, b, dims, precision=None):
    return lax.dot_general(
        a, b, ((dims[0], dims[1]), ((), ())), precision=precision, preferred_element_type=F32
    )


def rounded(x):
    return x.astype(BF16).astype(F32)


def row_ids(shape):
    return lax.broadcasted_iota(jnp.int32, shape, 0)


def lane_ids(shape):
    return lax.broadcasted_iota(jnp.int32, shape, 1)


def features(xx, want_source, want_target):
    row = row_ids(xx.shape)
    high = rounded(xx)
    low = rounded(xx - high)
    held = high + low
    square = held * held
    square = square + pltpu.roll(square, 1, 0)
    norm = square + pltpu.roll(square, 2, 0)
    n0 = rounded(norm)
    rest = norm - n0
    n1 = rounded(rest)
    n2 = rest - n1
    zero = jnp.zeros_like(xx)
    out = []
    if want_source:
        parts = jnp.where(row < 4, high, low)
        tail = jnp.where(row == 0, n0, jnp.where(row == 1, n1, jnp.where(row == 2, n2, jnp.where(row < 6, 1.0, 0.0))))
        out.append(jnp.concatenate([parts, parts, tail, zero], axis=0).astype(BF16))
    if want_target:
        tail = jnp.where(row < 3, 1.0, jnp.where(row == 3, n0, jnp.where(row == 4, n1, jnp.where(row == 5, n2, 0.0))))
        out.append(jnp.concatenate([-2.0 * high, -2.0 * low, tail, zero], axis=0).astype(BF16))
    return out


def halves(w):
    high = rounded(w)
    return jnp.concatenate([high, w - high], axis=0).astype(BF16)


def kernel_of(z):
    z = jnp.maximum(z, 1e-30)
    q = -LOG2E - z * lax.rsqrt(z)
    return q * jnp.exp2(q)


def split(k):
    high = k.astype(BF16)
    return high, (k - high.astype(F32)).astype(BF16)


def gather_lanes(chunks, ids):
    lane = ids & 127
    chunk = ids >> 7
    picked = [None] * len(chunks)
    for s in range(len(chunks[0])):
        here = chunk == s
        for i, source in enumerate(chunks):
            got = jnp.take_along_axis(source[s](), lane, axis=1, mode="promise_in_bounds")
            picked[i] = got if s == 0 else jnp.where(here, got, picked[i])
    return picked


def fetch(sources, targets, sems):
    moves = [pltpu.make_async_copy(a, b, sems.at[i]) for i, (a, b) in enumerate(zip(sources, targets))]
    for move in moves:
        move.start()
    return moves


def scale_rows(scale_ref, shape):
    row = row_ids(shape) & 3
    picked = jnp.where(row == 0, scale_ref[0], jnp.where(row == 1, scale_ref[1], jnp.where(row == 2, scale_ref[2], scale_ref[3])))
    return picked * UNIT


def gather_body(scale_hbm, order_hbm, x_hbm, p_hbm, bases_hbm, transfer_hbm, skel_hbm, halo_ref, own_ref, scale_ref, order_ref, xx, p_ref, bases_ref, transfer_ref, skel_ref, slot, sems):
    leaf_dev, rank, leaf_pts = bases_ref.shape
    points = p_ref.shape[1]
    chunks = points // 128
    per_leaf = leaf_pts // 128
    moves = fetch(
        [order_hbm, x_hbm, x_hbm, p_hbm, scale_hbm, bases_hbm, transfer_hbm, skel_hbm],
        [order_ref, xx.at[0:4, :], xx.at[4:8, :], p_ref, scale_ref, bases_ref, transfer_ref, skel_ref],
        sems,
    )
    for move in moves[:5]:
        move.wait()
    scale = scale_rows(scale_ref, (8, 128))

    def loads(ref):
        return [lambda s=s: ref[:, s * 128 : (s + 1) * 128] for s in range(chunks)]

    def two_leaves(g, _):
        kept = []
        for h in range(2):
            leaf = 2 * g + h
            for j in range(per_leaf):
                ids = order_ref[pl.ds(leaf * per_leaf + j, 1), :]
                got_x, got_p = gather_lanes([loads(xx), loads(p_ref)], jnp.broadcast_to(ids, (8, 128)))
                kept.append(got_x * scale)
                halo_ref[pl.ds(pl.multiple_of(32 + leaf * 8, 8), 8), j * 128 : (j + 1) * 128] = got_p
        for j in range(per_leaf):
            both = jnp.where(row_ids((8, 128)) < 4, kept[j], kept[per_leaf + j])
            halo_ref[pl.ds(pl.multiple_of(g * 8, 8), 8), j * 128 : (j + 1) * 128] = both
        return 0

    lax.fori_loop(0, leaf_dev // 2, two_leaves, 0)
    for move in moves[5:]:
        move.wait()
    for leaf in range(leaf_dev):
        coef = contract(halo_ref[32 + leaf * 8 : 40 + leaf * 8, :], bases_ref[leaf], ((1,), (1,)), EXACT)
        halo_ref[96:104, leaf * rank : (leaf + 1) * rank] = coef
    upper = row_ids((8, 128)) < 4
    for g in range(leaf_dev // 2):
        both = halo_ref[g * 8 : g * 8 + 8, 0:128]
        turned = pltpu.roll(both, 4, 0)
        slot[:, 2 * g * rank : (2 * g + 1) * rank] = jnp.where(upper, both, turned)[:, :rank]
        slot[:, (2 * g + 1) * rank : (2 * g + 2) * rank] = jnp.where(upper, turned, both)[:, :rank]
    weights = contract(halo_ref[96:104, :], transfer_ref[...], ((1,), (1,)), EXACT)
    slots = [lambda s=s: slot[:, s * 128 : (s + 1) * 128] for s in range(leaf_dev * rank // 128)]
    ids = jnp.concatenate([skel_ref[...], skel_ref[...]], axis=1)
    (node_x,) = gather_lanes([slots], jnp.broadcast_to(ids, (8, 128)))
    tile = jnp.concatenate([weights, node_x[:, :rank]], axis=1)
    own_ref[...] = tile


def place_of(order_ref):
    chunks = order_ref.shape[0]
    tally = jnp.zeros((2 * chunks, 128), F32)
    for c in range(chunks):
        ids = order_ref[c : c + 1, :]
        low = jnp.where(row_ids((128, 128)) == (ids & 127), 1.0, 0.0).astype(BF16)
        row = row_ids((chunks, 128)) == (ids >> 7)
        lane = lane_ids((chunks, 128))
        digit1 = jnp.where(row, (2 * c + (lane >> 6)).astype(F32), 0.0)
        digit0 = jnp.where(row, (lane & 63).astype(F32), 0.0)
        digits = jnp.concatenate([digit1, digit0], axis=0).astype(BF16)
        tally = tally + contract(digits, low, ((1,), (1,)))
    return (64.0 * tally[0:chunks] + tally[chunks : 2 * chunks] + 0.5).astype(jnp.int32)


def prepare(ref, base, src, wgt, tgt=None, coef=None):
    leaf_dev = ref.shape[0] // 13
    row = row_ids((8, ref.shape[1]))
    for g in range(leaf_dev // 2):
        both = ref[g * 8 : g * 8 + 8, :]
        turned = pltpu.roll(both, 4, 0)
        for h in range(2):
            leaf = 2 * g + h
            xx = jnp.where(row < 4, both, turned) if h == 0 else jnp.where(row < 4, turned, both)
            made = features(xx, True, tgt is not None)
            src[base + leaf] = made[0]
            if tgt is not None:
                tgt[leaf] = made[1]
            wgt[base + leaf] = halves(ref[32 + leaf * 8 : 40 + leaf * 8, :] * FACTOR)
            if coef is not None:
                rank = coef.shape[2]
                coef[base + leaf] = halves(ref[96:104, leaf * rank : (leaf + 1) * rank] * FACTOR)


def list_pairs(near_ref, count_ref, inside, outside, sizes):
    leaf_dev, slots = near_ref.shape

    def leaf_step(leaf, sums):
        def entry(j, sums):
            w = near_ref[leaf, j]
            here = jnp.where((w // leaf_dev == 4) & (sums[0] < FIRST_PAIRS), 1, 0)
            code = leaf * 128 + w
            inside[sums[0]] = code
            outside[sums[1]] = code
            return sums[0] + here, sums[1] + 1 - here

        return lax.fori_loop(0, count_ref[leaf], entry, sums)

    sums = lax.fori_loop(0, leaf_dev, leaf_step, (0, 0))
    idle = 9 * leaf_dev
    for extra in range(3):
        inside[sums[0] + extra] = idle
        outside[sums[1] + extra] = idle
    sizes[0], sizes[1] = sums
    return sums[0]


def near_pairs(pairs, n, first, src, tgt, wgt, out, z, high, low):
    parts = wgt.shape[2] // PART

    def where(p):
        return pairs[p] >> 7, (pairs[p] & 127) - first

    def distances(p, c, b):
        leaf, w = where(p)
        z[b] = contract(src[w, :, c * PART : (c + 1) * PART], tgt[leaf], ((0,), (0,)))

    def values(b):
        high[b], low[b] = split(kernel_of(z[b]))

    def product(p, c, b):
        _, w = where(p)
        weight = wgt[w, :, c * PART : (c + 1) * PART]
        got = jnp.dot(weight, high[b], preferred_element_type=F32)
        return got + jnp.dot(weight, low[b], preferred_element_type=F32)

    distances(0, 0, 0)
    distances(0, 1, 1)
    values(0)

    def two_pairs(g, _):
        for h in range(2):
            p = 2 * g + h
            got = None
            for c in range(parts):
                b = c % 2
                values(1 - b)
                mine = product(p, c, b)
                got = mine if got is None else got + mine
                distances(p + (c + 2) // parts, (c + 2) % parts, b)
            leaf, _ = where(p)
            out[leaf] += got[:8] + got[8:]
        return 0

    lax.fori_loop(0, (n + 1) // 2, two_pairs, 0)


def inside_body(near_ref, count_ref, halo_hbm, order_ref, out_ref, inv_ref, pairs_ref, sizes_ref, pairs, halo_ref, src, tgt, wgt, z, high, low, sem):
    leaf_dev, rhs, leaf_pts = out_ref.shape
    move = pltpu.make_async_copy(halo_hbm, halo_ref, sem)
    move.start()
    n = list_pairs(near_ref, count_ref, pairs, pairs_ref, sizes_ref)
    for extra in range(3):
        pairs[n + extra] = 5 * leaf_dev
    src[leaf_dev] = jnp.zeros(src.shape[1:], BF16)
    wgt[leaf_dev] = jnp.zeros(wgt.shape[1:], BF16)
    out_ref[...] = jnp.zeros_like(out_ref)
    move.wait()
    inv_ref[...] = place_of(order_ref)
    prepare(halo_ref, 0, src, wgt, tgt)
    near_pairs(pairs, n, 4 * leaf_dev, src, tgt, wgt, out_ref, z, high, low)


def node_field(cores, columns, place_ref, node_ref, own_ref, transfer_ref, node_src, node_wgt):
    devices = node_ref.shape[0]
    rank = own_ref.shape[1] // 2
    lane = lane_ids((8, 128))

    def distant(e):
        leaf = e // (cores * columns) * cores + e % cores
        far_a = jnp.abs(leaf - place_ref[0]) > 1
        far_b = jnp.abs(e // cores % columns - place_ref[1]) > 1
        return jnp.where(far_a | far_b, FACTOR, 0.0)

    def unpack(g, _):
        xs, ws = [], []
        for k in range(4):
            e = 8 * g + 2 * k
            one, two = node_ref[e], node_ref[e + 1]
            xs.append(jnp.where(lane < rank, pltpu.roll(one, rank, 1), two))
            ws.append(jnp.where(lane < rank, one * distant(e), pltpu.roll(two, rank, 1) * distant(e + 1)))
        at = pl.ds(pl.multiple_of(g * 512, 512), 512)
        node_src[:, at] = features(jnp.concatenate(xs, axis=1), True, False)[0]
        node_wgt[:, at] = halves(jnp.concatenate(ws, axis=1))
        return 0

    lax.fori_loop(0, devices // 8, unpack, 0, unroll=4)
    own_xx = pltpu.roll(own_ref[...], rank, 1)
    target = features(own_xx, False, True)[0][:, :rank]
    total = jnp.zeros((16, rank), F32)
    step = 512
    for q in range(0, devices * rank, step):
        z_far = contract(target, node_src[:, q : q + step], ((0,), (0,)))
        k_high, k_low = split(kernel_of(z_far))
        weight = node_wgt[:, q : q + step]
        total = total + contract(weight, k_high, ((1,), (1,)))
        total = total + contract(weight, k_low, ((1,), (1,)))
    return jnp.dot(total[:8] + total[8:], transfer_ref[...], precision=EXACT, preferred_element_type=F32)


def outside_body(pairs_ref, sizes_ref, far_ref, row_ref, up_ref, down_ref, out_ref, far_out_ref, src, tgt, wgt, coef, far_src, far_wgt, z, high, low):
    leaf_dev, rhs, leaf_pts = out_ref.shape
    rank = coef.shape[2]
    idle = 9 * leaf_dev
    src[idle] = jnp.zeros(src.shape[1:], BF16)
    wgt[idle] = jnp.zeros(wgt.shape[1:], BF16)
    for k in range(3):
        prepare(up_ref.at[k], k * leaf_dev, src, wgt, None, coef)
        prepare(row_ref.at[k], (3 + k) * leaf_dev, src, wgt, tgt if k == 1 else None, coef)
        prepare(down_ref.at[k], (6 + k) * leaf_dev, src, wgt, None, coef)
    out_ref[...] = jnp.zeros_like(out_ref)
    near_pairs(pairs_ref, sizes_ref[1], 0, src, tgt, wgt, out_ref, z, high, low)
    for leaf in range(leaf_dev):
        for j in range(far_ref.shape[1]):
            w = far_ref[leaf, j]
            at = slice(j * rank, (j + 1) * rank)
            far_src[leaf, :, at] = src[w, :, 0:rank]
            far_wgt[leaf, :, at] = coef[w]
    for leaf in range(leaf_dev):
        k_high, k_low = split(kernel_of(contract(tgt[leaf, :, 0:rank], far_src[leaf], ((0,), (0,)))))
        far = contract(far_wgt[leaf], k_high, ((1,), (1,))) + contract(far_wgt[leaf], k_low, ((1,), (1,)))
        far_out_ref[leaf] = far[:8] + far[8:]


def tail_body(cores, columns, place_ref, noise_ref, inside_ref, near_ref, far_ref, node_ref, own_ref, transfer_ref, bases_ref, inv_ref, p_ref, res_ref, image_ref, sums_ref, flat, node_src, node_wgt):
    leaf_dev, rank, leaf_pts = bases_ref.shape
    pushed = node_field(cores, columns, place_ref, node_ref, own_ref, transfer_ref, node_src, node_wgt)
    for leaf in range(leaf_dev):
        incoming = halves(far_ref[leaf] + pushed[:, leaf * rank : (leaf + 1) * rank])
        base_high, base_low = split(bases_ref[leaf])
        got = jnp.dot(incoming, base_high, preferred_element_type=F32)
        got = got + jnp.dot(incoming, base_low, preferred_element_type=F32)
        flat[:, leaf * leaf_pts : (leaf + 1) * leaf_pts] = inside_ref[leaf] + near_ref[leaf] + got[:8] + got[8:]

    chunks = flat.shape[1] // 128
    row = row_ids((8, 128))
    lane = lane_ids((8, 128))
    source = [lambda s=s: flat[:, s * 128 : (s + 1) * 128] for s in range(chunks)]
    noise = jnp.zeros((8, 128), F32)
    for r in range(8):
        noise = jnp.where(row == r, noise_ref[r], noise)

    def place(g, sums):
        along, squares = sums
        for h in range(4):
            c = 4 * g + h
            at = pl.ds(pl.multiple_of(c * 128, 128), 128)
            ids = jnp.broadcast_to(inv_ref[pl.ds(c, 1), :], (8, 128))
            (part,) = gather_lanes([source], ids)
            image = part + noise * p_ref[:, at]
            image_ref[:, at] = image
            along, squares = along + res_ref[:, at] * image, squares + image * image
        return along, squares

    zero = jnp.zeros((8, 128), F32)
    along, squares = lax.fori_loop(0, chunks // 4, place, (zero, zero))
    along = jnp.sum(along, axis=1, keepdims=True)
    squares = jnp.sum(squares, axis=1, keepdims=True)
    both = jnp.where(lane == row, along, 0.0) + jnp.where(lane == row + 8, squares, 0.0)
    sums_ref[...] = jnp.broadcast_to(jnp.sum(both, axis=0, keepdims=True), sums_ref.shape)


def update_body(sums_ref, it_ref, p_ref, res_ref, image_ref, new_it_ref, new_res_ref):
    total = jnp.sum(sums_ref[...], axis=0, keepdims=True)
    row = row_ids((8, 128))
    lane = lane_ids((8, 128))
    along = jnp.sum(jnp.where(lane == row, total, 0.0), axis=1, keepdims=True)
    squares = jnp.sum(jnp.where(lane == row + 8, total, 0.0), axis=1, keepdims=True)
    alpha = along / (squares + 1e-06)
    new_it_ref[...] = it_ref[...] + alpha * p_ref[...]
    new_res_ref[...] = res_ref[...] - alpha * image_ref[...]


def shifted(x, axis, by):
    n = math.prod(lax.axis_size(part) for part in axis)
    return lax.ppermute(x, axis, [(i, i + by) for i in range(n) if 0 <= i + by < n])


def shards(coords, direction, iterate, residual, order, bases, transfer, near_list, near_count, far_list, device_skel, inv_scale, noise):
    leaf_dev, rank, leaf_pts = bases.shape
    rhs, points = direction.shape
    axes = ("chip", "core", "tm")
    leaf_axes = ("chip", "core")
    chips, cores, columns = (lax.axis_size(axis) for axis in axes)
    devices = chips * cores * columns
    chunks = points // 128
    shape = jax.ShapeDtypeStruct
    by_row = order.reshape(chunks, 128)
    halo, own = pl.pallas_call(
        gather_body,
        in_specs=[ANY] * 7,
        out_specs=[VMEM] * 2,
        out_shape=[shape((13 * leaf_dev, leaf_pts), F32), shape((8, 128), F32)],
        scratch_shapes=[
            pltpu.SMEM(inv_scale.shape, F32),
            pltpu.VMEM((chunks, 128), jnp.int32),
            pltpu.VMEM((8, points), F32),
            pltpu.VMEM((rhs, points), F32),
            pltpu.VMEM(bases.shape, F32),
            pltpu.VMEM(transfer.shape[1:], F32),
            pltpu.VMEM(device_skel.shape, jnp.int32),
            pltpu.VMEM((8, leaf_dev * rank), F32),
            pltpu.SemaphoreType.DMA((8,)),
        ],
        compiler_params=params(60),
        name="gather",
    )(inv_scale, by_row, coords, direction, bases, transfer[0], device_skel)
    left = shifted(halo, ("tm",), 1)
    right = shifted(halo, ("tm",), -1)

    def pipeline(sources):
        return [
            pltpu.VMEM((sources + 1, 32, leaf_pts), BF16),
            pltpu.VMEM((leaf_dev, 32, leaf_pts), BF16),
            pltpu.VMEM((sources + 1, 16, leaf_pts), BF16),
        ]

    buffers = [
        pltpu.VMEM((2, PART, leaf_pts), F32),
        pltpu.VMEM((2, PART, leaf_pts), BF16),
        pltpu.VMEM((2, PART, leaf_pts), BF16),
    ]
    entries = near_list.size + 4
    other = lax.ppermute(own, "core", [(i, cores - 1 - i) for i in range(cores)])
    inside, inverse, pairs, sizes = pl.pallas_call(
        inside_body,
        in_specs=[SMEM] * 2 + [ANY] + [VMEM],
        out_specs=[VMEM] * 2 + [SMEM] * 2,
        out_shape=[
            shape((leaf_dev, rhs, leaf_pts), F32),
            shape((chunks, 128), jnp.int32),
            shape((entries,), jnp.int32),
            shape((2,), jnp.int32),
        ],
        scratch_shapes=[
            pltpu.SMEM((entries,), jnp.int32),
            pltpu.VMEM(halo.shape, F32),
        ]
        + pipeline(leaf_dev)
        + buffers
        + [pltpu.SemaphoreType.DMA(())],
        compiler_params=params(58),
        cost_estimate=pl.CostEstimate(flops=10**10, bytes_accessed=2**21, transcendentals=10**7),
        name="inside",
    )(near_list, near_count, halo, by_row)
    left, right, inside, other = lax.optimization_barrier((left, right, inside, other))
    core = lax.axis_index("core")
    both = jnp.stack([jnp.where(core == 0, own, other), jnp.where(core == 0, other, own)])
    nodes = lax.all_to_all(jnp.broadcast_to(both[None], (chips * columns,) + both.shape), ("chip", "tm"), 0, 0)
    nodes = nodes.reshape(devices, 8, 128)
    row = jnp.stack([left, halo, right])
    up = shifted(row, leaf_axes, 1)
    down = shifted(row, leaf_axes, -1)
    place = jnp.stack([lax.axis_index(leaf_axes), lax.axis_index("tm")]).astype(jnp.int32)

    near, far = pl.pallas_call(
        outside_body,
        in_specs=[SMEM] * 3 + [VMEM] * 3,
        out_specs=[VMEM] * 2,
        out_shape=[shape((leaf_dev, rhs, leaf_pts), F32), shape((leaf_dev, rhs, rank), F32)],
        scratch_shapes=pipeline(9 * leaf_dev)
        + [
            pltpu.VMEM((9 * leaf_dev, 16, rank), BF16),
            pltpu.VMEM((leaf_dev, 32, far_list.shape[1] * rank), BF16),
            pltpu.VMEM((leaf_dev, 16, far_list.shape[1] * rank), BF16),
        ]
        + buffers,
        compiler_params=params(14),
        cost_estimate=pl.CostEstimate(flops=3 * 10**10, bytes_accessed=2**21, transcendentals=3 * 10**7),
        name="outside",
    )(pairs, sizes, far_list, row, up, down)
    image, sums = pl.pallas_call(
        functools.partial(tail_body, cores, columns),
        in_specs=[SMEM] * 2 + [VMEM] * 10,
        out_specs=[VMEM] * 2,
        out_shape=[shape((rhs, points), F32), shape((devices, 128), F32)],
        scratch_shapes=[
            pltpu.VMEM((rhs, points), F32),
            pltpu.VMEM((32, devices * rank), BF16),
            pltpu.VMEM((16, devices * rank), BF16),
        ],
        compiler_params=params(10),
        name="tail",
    )(place, noise, inside, near, far, nodes, own, transfer[0], bases, inverse, direction, residual)
    all_sums = lax.all_to_all(sums, axes, 0, 0, tiled=True)
    return pl.pallas_call(
        update_body,
        in_specs=[VMEM] * 5,
        out_specs=[VMEM] * 2,
        out_shape=[shape((rhs, points), F32)] * 2,
        compiler_params=params(8),
        name="update",
    )(all_sums, iterate, direction, residual, image)


def solution(mesh):
    leaf, columns = mesh.devices.shape
    finer = jax.sharding.Mesh(mesh.devices.reshape(leaf // 2, 2, columns), ("chip", "core", "tm"))
    whole = P(None, ("chip", "core", "tm"))
    first = P(("chip", "core", "tm"))
    return jax.shard_map(
        shards,
        mesh=finer,
        in_specs=(whole,) * 4 + (first,) * 7 + (P(), P()),
        out_specs=(whole, whole),
        check_vma=False,
    )
```

```python
import functools
import math

import jax
import jax.numpy as jnp
from jax import lax
from jax.experimental import pallas as pl
from jax.experimental.pallas import tpu as pltpu
from jax.sharding import PartitionSpec as P

F32 = jnp.float32
BF16 = jnp.bfloat16
EXACT = lax.Precision.HIGHEST
LN2 = math.log(2.0)
LOG2E = 1.0 / LN2
UNIT = math.sqrt(3.0) * LOG2E
FACTOR = -LN2 * math.e
VMEM = pl.BlockSpec(memory_space=pltpu.VMEM)
SMEM = pl.BlockSpec(memory_space=pltpu.SMEM)
ANY = pl.BlockSpec(memory_space=pl.ANY)
PART = 256
FIRST_PAIRS = 10


def params(mib, **kw):
    return pltpu.CompilerParams(vmem_limit_bytes=mib * 2**20, **kw)


def contract(a, b, dims, precision=None):
    return lax.dot_general(
        a, b, ((dims[0], dims[1]), ((), ())), precision=precision, preferred_element_type=F32
    )


def rounded(x):
    return x.astype(BF16).astype(F32)


def row_ids(shape):
    return lax.broadcasted_iota(jnp.int32, shape, 0)


def lane_ids(shape):
    return lax.broadcasted_iota(jnp.int32, shape, 1)


def features(xx, want_source, want_target):
    row = row_ids(xx.shape)
    high = rounded(xx)
    low = rounded(xx - high)
    held = high + low
    square = held * held
    square = square + pltpu.roll(square, 1, 0)
    norm = square + pltpu.roll(square, 2, 0)
    n0 = rounded(norm)
    rest = norm - n0
    n1 = rounded(rest)
    n2 = rest - n1
    zero = jnp.zeros_like(xx)
    out = []
    if want_source:
        parts = jnp.where(row < 4, high, low)
        tail = jnp.where(row == 0, n0, jnp.where(row == 1, n1, jnp.where(row == 2, n2, jnp.where(row < 6, 1.0, 0.0))))
        out.append(jnp.concatenate([parts, parts, tail, zero], axis=0).astype(BF16))
    if want_target:
        tail = jnp.where(row < 3, 1.0, jnp.where(row == 3, n0, jnp.where(row == 4, n1, jnp.where(row == 5, n2, 0.0))))
        out.append(jnp.concatenate([-2.0 * high, -2.0 * low, tail, zero], axis=0).astype(BF16))
    return out


def halves(w):
    high = rounded(w)
    return jnp.concatenate([high, w - high], axis=0).astype(BF16)


def kernel_of(z):
    z = jnp.maximum(z, 1e-30)
    q = -LOG2E - z * lax.rsqrt(z)
    return q * jnp.exp2(q)


def split(k):
    high = k.astype(BF16)
    return high, (k - high.astype(F32)).astype(BF16)


def gather_lanes(chunks, ids):
    lane = ids & 127
    chunk = ids >> 7
    picked = [None] * len(chunks)
    for s in range(len(chunks[0])):
        here = chunk == s
        for i, source in enumerate(chunks):
            got = jnp.take_along_axis(source[s](), lane, axis=1, mode="promise_in_bounds")
            picked[i] = got if s == 0 else jnp.where(here, got, picked[i])
    return picked


def fetch(sources, targets, sems):
    moves = [pltpu.make_async_copy(a, b, sems.at[i]) for i, (a, b) in enumerate(zip(sources, targets))]
    for move in moves:
        move.start()
    return moves


def scale_rows(scale_ref, shape):
    row = row_ids(shape) & 3
    picked = jnp.where(row == 0, scale_ref[0], jnp.where(row == 1, scale_ref[1], jnp.where(row == 2, scale_ref[2], scale_ref[3])))
    return picked * UNIT


def gather_body(scale_hbm, order_hbm, x_hbm, p_hbm, bases_hbm, transfer_hbm, skel_hbm, halo_ref, own_ref, scale_ref, order_ref, xx, p_ref, bases_ref, transfer_ref, skel_ref, slot, sems):
    leaf_dev, rank, leaf_pts = bases_ref.shape
    points = p_ref.shape[1]
    chunks = points // 128
    per_leaf = leaf_pts // 128
    moves = fetch(
        [order_hbm, x_hbm, x_hbm, p_hbm, scale_hbm, bases_hbm, transfer_hbm, skel_hbm],
        [order_ref, xx.at[0:4, :], xx.at[4:8, :], p_ref, scale_ref, bases_ref, transfer_ref, skel_ref],
        sems,
    )
    for move in moves[:5]:
        move.wait()
    scale = scale_rows(scale_ref, (8, 128))

    def loads(ref):
        return [lambda s=s: ref[:, s * 128 : (s + 1) * 128] for s in range(chunks)]

    def two_leaves(g, _):
        kept = []
        for h in range(2):
            leaf = 2 * g + h
            for j in range(per_leaf):
                ids = order_ref[pl.ds(leaf * per_leaf + j, 1), :]
                got_x, got_p = gather_lanes([loads(xx), loads(p_ref)], jnp.broadcast_to(ids, (8, 128)))
                kept.append(got_x * scale)
                halo_ref[pl.ds(pl.multiple_of(32 + leaf * 8, 8), 8), j * 128 : (j + 1) * 128] = got_p
        for j in range(per_leaf):
            both = jnp.where(row_ids((8, 128)) < 4, kept[j], kept[per_leaf + j])
            halo_ref[pl.ds(pl.multiple_of(g * 8, 8), 8), j * 128 : (j + 1) * 128] = both
        return 0

    lax.fori_loop(0, leaf_dev // 2, two_leaves, 0)
    for move in moves[5:]:
        move.wait()
    for leaf in range(leaf_dev):
        coef = contract(halo_ref[32 + leaf * 8 : 40 + leaf * 8, :], bases_ref[leaf], ((1,), (1,)), EXACT)
        halo_ref[96:104, leaf * rank : (leaf + 1) * rank] = coef
    upper = row_ids((8, 128)) < 4
    for g in range(leaf_dev // 2):
        both = halo_ref[g * 8 : g * 8 + 8, 0:128]
        turned = pltpu.roll(both, 4, 0)
        slot[:, 2 * g * rank : (2 * g + 1) * rank] = jnp.where(upper, both, turned)[:, :rank]
        slot[:, (2 * g + 1) * rank : (2 * g + 2) * rank] = jnp.where(upper, turned, both)[:, :rank]
    weights = contract(halo_ref[96:104, :], transfer_ref[...], ((1,), (1,)), EXACT)
    slots = [lambda s=s: slot[:, s * 128 : (s + 1) * 128] for s in range(leaf_dev * rank // 128)]
    ids = jnp.concatenate([skel_ref[...], skel_ref[...]], axis=1)
    (node_x,) = gather_lanes([slots], jnp.broadcast_to(ids, (8, 128)))
    tile = jnp.concatenate([weights, node_x[:, :rank]], axis=1)
    own_ref[...] = tile


def place_of(order_ref):
    chunks = order_ref.shape[0]
    tally = jnp.zeros((2 * chunks, 128), F32)
    for c in range(chunks):
        ids = order_ref[c : c + 1, :]
        low = jnp.where(row_ids((128, 128)) == (ids & 127), 1.0, 0.0).astype(BF16)
        row = row_ids((chunks, 128)) == (ids >> 7)
        lane = lane_ids((chunks, 128))
        digit1 = jnp.where(row, (2 * c + (lane >> 6)).astype(F32), 0.0)
        digit0 = jnp.where(row, (lane & 63).astype(F32), 0.0)
        digits = jnp.concatenate([digit1, digit0], axis=0).astype(BF16)
        tally = tally + contract(digits, low, ((1,), (1,)))
    return (64.0 * tally[0:chunks] + tally[chunks : 2 * chunks] + 0.5).astype(jnp.int32)


def prepare(ref, base, src, wgt, tgt=None, coef=None):
    leaf_dev = ref.shape[0] // 13
    row = row_ids((8, ref.shape[1]))
    for g in range(leaf_dev // 2):
        both = ref[g * 8 : g * 8 + 8, :]
        turned = pltpu.roll(both, 4, 0)
        for h in range(2):
            leaf = 2 * g + h
            xx = jnp.where(row < 4, both, turned) if h == 0 else jnp.where(row < 4, turned, both)
            made = features(xx, True, tgt is not None)
            src[base + leaf] = made[0]
            if tgt is not None:
                tgt[leaf] = made[1]
            wgt[base + leaf] = halves(ref[32 + leaf * 8 : 40 + leaf * 8, :] * FACTOR)
            if coef is not None:
                rank = coef.shape[2]
                coef[base + leaf] = halves(ref[96:104, leaf * rank : (leaf + 1) * rank] * FACTOR)


def lists_body(near_ref, count_ref, order_ref, inv_ref, inside_ref, outside_ref, sizes_ref):
    leaf_dev, slots = near_ref.shape

    def leaf_step(leaf, sums):
        def entry(j, sums):
            w = near_ref[leaf, j]
            here = jnp.where((w // leaf_dev == 4) & (sums[0] < FIRST_PAIRS), 1, 0)
            inside_ref[sums[0]] = leaf * 128 + w
            outside_ref[sums[1]] = leaf * 128 + w
            return sums[0] + here, sums[1] + 1 - here

        return lax.fori_loop(0, count_ref[leaf], entry, sums)

    sums = lax.fori_loop(0, leaf_dev, leaf_step, (0, 0))
    for extra in range(3):
        inside_ref[sums[0] + extra] = 5 * leaf_dev
        outside_ref[sums[1] + extra] = 9 * leaf_dev
    sizes_ref[0], sizes_ref[1] = sums
    inv_ref[...] = place_of(order_ref)


def near_pairs(pairs, n, first, src, tgt, wgt, out, z, high, low):
    parts = wgt.shape[2] // PART

    def where(p):
        return pairs[p] >> 7, (pairs[p] & 127) - first

    def distances(p, c, b):
        leaf, w = where(p)
        z[b] = contract(src[w, :, c * PART : (c + 1) * PART], tgt[leaf], ((0,), (0,)))

    def values(b):
        high[b], low[b] = split(kernel_of(z[b]))

    def product(p, c, b):
        _, w = where(p)
        weight = wgt[w, :, c * PART : (c + 1) * PART]
        got = jnp.dot(weight, high[b], preferred_element_type=F32)
        return got + jnp.dot(weight, low[b], preferred_element_type=F32)

    distances(0, 0, 0)
    distances(0, 1, 1)
    values(0)

    def two_pairs(g, _):
        for h in range(2):
            p = 2 * g + h
            got = None
            for c in range(parts):
                b = c % 2
                values(1 - b)
                mine = product(p, c, b)
                got = mine if got is None else got + mine
                distances(p + (c + 2) // parts, (c + 2) % parts, b)
            leaf, _ = where(p)
            out[leaf] += got[:8] + got[8:]
        return 0

    lax.fori_loop(0, (n + 1) // 2, two_pairs, 0)


def inside_body(pairs_ref, sizes_ref, halo_ref, out_ref, src, tgt, wgt, z, high, low):
    leaf_dev = out_ref.shape[0]
    src[leaf_dev] = jnp.zeros(src.shape[1:], BF16)
    wgt[leaf_dev] = jnp.zeros(wgt.shape[1:], BF16)
    prepare(halo_ref, 0, src, wgt, tgt)
    out_ref[...] = jnp.zeros_like(out_ref)
    near_pairs(pairs_ref, sizes_ref[0], 4 * leaf_dev, src, tgt, wgt, out_ref, z, high, low)


def node_field(cores, columns, place_ref, node_ref, own_ref, transfer_ref, node_src, node_wgt):
    devices = node_ref.shape[0]
    rank = own_ref.shape[1] // 2
    lane = lane_ids((8, 128))

    def distant(chip, core, column):
        far_a = jnp.abs(chip * cores + core - place_ref[0]) > 1
        far_b = jnp.abs(column - place_ref[1]) > 1
        return jnp.where(far_a | far_b, FACTOR, 0.0)

    width = columns * cores * rank

    def unpack(chip, _):
        xs, ws = [], []
        for column in range(columns):
            one, two = (node_ref[(chip * columns + column) * cores + core] for core in range(2))
            xs.append(jnp.where(lane < rank, pltpu.roll(one, rank, 1), two))
            ws.append(jnp.where(lane < rank, one * distant(chip, 0, column), pltpu.roll(two, rank, 1) * distant(chip, 1, column)))
        at = pl.ds(pl.multiple_of(chip * width, width), width)
        node_src[:, at] = features(jnp.concatenate(xs, axis=1), True, False)[0]
        node_wgt[:, at] = halves(jnp.concatenate(ws, axis=1))
        return 0

    lax.fori_loop(0, devices // (cores * columns), unpack, 0, unroll=4)
    own_xx = pltpu.roll(own_ref[...], rank, 1)
    target = features(own_xx, False, True)[0][:, :rank]
    total = jnp.zeros((16, rank), F32)
    step = 512
    for q in range(0, devices * rank, step):
        z_far = contract(target, node_src[:, q : q + step], ((0,), (0,)))
        k_high, k_low = split(kernel_of(z_far))
        weight = node_wgt[:, q : q + step]
        total = total + contract(weight, k_high, ((1,), (1,)))
        total = total + contract(weight, k_low, ((1,), (1,)))
    return jnp.dot(total[:8] + total[8:], transfer_ref[...], precision=EXACT, preferred_element_type=F32)


def outside_body(pairs_ref, sizes_ref, far_ref, row_ref, up_ref, down_ref, out_ref, far_out_ref, src, tgt, wgt, coef, far_src, far_wgt, z, high, low):
    leaf_dev, rhs, leaf_pts = out_ref.shape
    rank = coef.shape[2]
    idle = 9 * leaf_dev
    src[idle] = jnp.zeros(src.shape[1:], BF16)
    wgt[idle] = jnp.zeros(wgt.shape[1:], BF16)
    for k in range(3):
        prepare(up_ref.at[k], k * leaf_dev, src, wgt, None, coef)
        prepare(row_ref.at[k], (3 + k) * leaf_dev, src, wgt, tgt if k == 1 else None, coef)
        prepare(down_ref.at[k], (6 + k) * leaf_dev, src, wgt, None, coef)
    out_ref[...] = jnp.zeros_like(out_ref)
    near_pairs(pairs_ref, sizes_ref[1], 0, src, tgt, wgt, out_ref, z, high, low)
    for leaf in range(leaf_dev):
        for j in range(far_ref.shape[1]):
            w = far_ref[leaf, j]
            at = slice(j * rank, (j + 1) * rank)
            far_src[leaf, :, at] = src[w, :, 0:rank]
            far_wgt[leaf, :, at] = coef[w]
    for leaf in range(leaf_dev):
        k_high, k_low = split(kernel_of(contract(tgt[leaf, :, 0:rank], far_src[leaf], ((0,), (0,)))))
        far = contract(far_wgt[leaf], k_high, ((1,), (1,))) + contract(far_wgt[leaf], k_low, ((1,), (1,)))
        far_out_ref[leaf] = far[:8] + far[8:]


def tail_body(cores, columns, place_ref, noise_ref, inside_ref, near_ref, far_ref, node_ref, own_ref, transfer_ref, bases_ref, inv_ref, p_ref, res_ref, image_ref, sums_ref, flat, node_src, node_wgt):
    leaf_dev, rank, leaf_pts = bases_ref.shape
    pushed = node_field(cores, columns, place_ref, node_ref, own_ref, transfer_ref, node_src, node_wgt)
    for leaf in range(leaf_dev):
        incoming = halves(far_ref[leaf] + pushed[:, leaf * rank : (leaf + 1) * rank])
        base_high, base_low = split(bases_ref[leaf])
        got = jnp.dot(incoming, base_high, preferred_element_type=F32)
        got = got + jnp.dot(incoming, base_low, preferred_element_type=F32)
        flat[:, leaf * leaf_pts : (leaf + 1) * leaf_pts] = inside_ref[leaf] + near_ref[leaf] + got[:8] + got[8:]

    chunks = flat.shape[1] // 128
    row = row_ids((8, 128))
    lane = lane_ids((8, 128))
    source = [lambda s=s: flat[:, s * 128 : (s + 1) * 128] for s in range(chunks)]
    noise = jnp.zeros((8, 128), F32)
    for r in range(8):
        noise = jnp.where(row == r, noise_ref[r], noise)

    def place(g, sums):
        along, squares = sums
        for h in range(4):
            c = 4 * g + h
            at = pl.ds(pl.multiple_of(c * 128, 128), 128)
            ids = jnp.broadcast_to(inv_ref[pl.ds(c, 1), :], (8, 128))
            (part,) = gather_lanes([source], ids)
            image = part + noise * p_ref[:, at]
            image_ref[:, at] = image
            along, squares = along + res_ref[:, at] * image, squares + image * image
        return along, squares

    zero = jnp.zeros((8, 128), F32)
    along, squares = lax.fori_loop(0, chunks // 4, place, (zero, zero))
    along = jnp.sum(along, axis=1, keepdims=True)
    squares = jnp.sum(squares, axis=1, keepdims=True)
    both = jnp.where(lane == row, along, 0.0) + jnp.where(lane == row + 8, squares, 0.0)
    sums_ref[...] = jnp.broadcast_to(jnp.sum(both, axis=0, keepdims=True), sums_ref.shape)


def update_body(sums_ref, it_ref, p_ref, res_ref, image_ref, new_it_ref, new_res_ref):
    total = jnp.sum(sums_ref[...], axis=0, keepdims=True)
    row = row_ids((8, 128))
    lane = lane_ids((8, 128))
    along = jnp.sum(jnp.where(lane == row, total, 0.0), axis=1, keepdims=True)
    squares = jnp.sum(jnp.where(lane == row + 8, total, 0.0), axis=1, keepdims=True)
    alpha = along / (squares + 1e-06)
    new_it_ref[...] = it_ref[...] + alpha * p_ref[...]
    new_res_ref[...] = res_ref[...] - alpha * image_ref[...]


def shifted(x, axis, by):
    n = math.prod(lax.axis_size(part) for part in axis)
    return lax.ppermute(x, axis, [(i, i + by) for i in range(n) if 0 <= i + by < n])


def shards(coords, direction, iterate, residual, order, bases, transfer, near_list, near_count, far_list, device_skel, inv_scale, noise):
    leaf_dev, rank, leaf_pts = bases.shape
    rhs, points = direction.shape
    axes = ("chip", "core", "tm")
    leaf_axes = ("chip", "core")
    chips, cores, columns = (lax.axis_size(axis) for axis in axes)
    devices = chips * cores * columns
    chunks = points // 128
    shape = jax.ShapeDtypeStruct
    by_row = order.reshape(chunks, 128)
    halo, own = pl.pallas_call(
        gather_body,
        in_specs=[ANY] * 7,
        out_specs=[VMEM] * 2,
        out_shape=[shape((13 * leaf_dev, leaf_pts), F32), shape((8, 128), F32)],
        scratch_shapes=[
            pltpu.SMEM(inv_scale.shape, F32),
            pltpu.VMEM((chunks, 128), jnp.int32),
            pltpu.VMEM((8, points), F32),
            pltpu.VMEM((rhs, points), F32),
            pltpu.VMEM(bases.shape, F32),
            pltpu.VMEM(transfer.shape[1:], F32),
            pltpu.VMEM(device_skel.shape, jnp.int32),
            pltpu.VMEM((8, leaf_dev * rank), F32),
            pltpu.SemaphoreType.DMA((8,)),
        ],
        compiler_params=params(60),
        name="gather",
    )(inv_scale, by_row, coords, direction, bases, transfer[0], device_skel)
    left = shifted(halo, ("tm",), 1)
    right = shifted(halo, ("tm",), -1)

    def pipeline(sources):
        return [
            pltpu.VMEM((sources + 1, 32, leaf_pts), BF16),
            pltpu.VMEM((leaf_dev, 32, leaf_pts), BF16),
            pltpu.VMEM((sources + 1, 16, leaf_pts), BF16),
        ]

    buffers = [
        pltpu.VMEM((2, PART, leaf_pts), F32),
        pltpu.VMEM((2, PART, leaf_pts), BF16),
        pltpu.VMEM((2, PART, leaf_pts), BF16),
    ]
    entries = near_list.size + 4
    other = lax.ppermute(own, "core", [(i, cores - 1 - i) for i in range(cores)])
    core = lax.axis_index("core")
    both = jnp.stack([jnp.where(core == 0, own, other), jnp.where(core == 0, other, own)])
    nodes = lax.all_to_all(jnp.broadcast_to(both[None], (chips * columns,) + both.shape), ("chip", "tm"), 0, 0)
    nodes = nodes.reshape(devices, 8, 128)
    inverse, pairs, others, sizes = pl.pallas_call(
        lists_body,
        in_specs=[SMEM] * 2 + [VMEM],
        out_specs=[VMEM] + [SMEM] * 3,
        out_shape=[
            shape((chunks, 128), jnp.int32),
            shape((entries,), jnp.int32),
            shape((entries,), jnp.int32),
            shape((2,), jnp.int32),
        ],
        compiler_params=params(8),
        cost_estimate=pl.CostEstimate(flops=10**10, bytes_accessed=2**21, transcendentals=10**7),
        name="lists",
    )(near_list, near_count, by_row)
    left, right, nodes, pairs, halo = lax.optimization_barrier((left, right, nodes, pairs, halo))
    row = jnp.stack([left, halo, right])
    up = shifted(row, leaf_axes, 1)
    down = shifted(row, leaf_axes, -1)
    inside = pl.pallas_call(
        inside_body,
        in_specs=[SMEM] * 2 + [VMEM],
        out_specs=VMEM,
        out_shape=shape((leaf_dev, rhs, leaf_pts), F32),
        scratch_shapes=pipeline(leaf_dev) + buffers,
        compiler_params=params(14),
        cost_estimate=pl.CostEstimate(flops=10**10, bytes_accessed=2**21, transcendentals=10**7),
        name="inside",
    )(pairs, sizes, halo)
    up, down, inside = lax.optimization_barrier((up, down, inside))
    place = jnp.stack([lax.axis_index(leaf_axes), lax.axis_index("tm")]).astype(jnp.int32)

    near, far = pl.pallas_call(
        outside_body,
        in_specs=[SMEM] * 3 + [VMEM] * 3,
        out_specs=[VMEM] * 2,
        out_shape=[shape((leaf_dev, rhs, leaf_pts), F32), shape((leaf_dev, rhs, rank), F32)],
        scratch_shapes=pipeline(9 * leaf_dev)
        + [
            pltpu.VMEM((9 * leaf_dev, 16, rank), BF16),
            pltpu.VMEM((leaf_dev, 32, far_list.shape[1] * rank), BF16),
            pltpu.VMEM((leaf_dev, 16, far_list.shape[1] * rank), BF16),
        ]
        + buffers,
        compiler_params=params(14),
        cost_estimate=pl.CostEstimate(flops=3 * 10**10, bytes_accessed=2**21, transcendentals=3 * 10**7),
        name="outside",
    )(others, sizes, far_list, row, up, down)
    image, sums = pl.pallas_call(
        functools.partial(tail_body, cores, columns),
        in_specs=[SMEM] * 2 + [VMEM] * 10,
        out_specs=[VMEM] * 2,
        out_shape=[shape((rhs, points), F32), shape((devices, 128), F32)],
        scratch_shapes=[
            pltpu.VMEM((rhs, points), F32),
            pltpu.VMEM((32, devices * rank), BF16),
            pltpu.VMEM((16, devices * rank), BF16),
        ],
        compiler_params=params(10),
        name="tail",
    )(place, noise, inside, near, far, nodes, own, transfer[0], bases, inverse, direction, residual)
    all_sums = lax.all_to_all(sums, axes, 0, 0, tiled=True)
    return pl.pallas_call(
        update_body,
        in_specs=[VMEM] * 5,
        out_specs=[VMEM] * 2,
        out_shape=[shape((rhs, points), F32)] * 2,
        compiler_params=params(8),
        name="update",
    )(all_sums, iterate, direction, residual, image)


def solution(mesh):
    leaf, columns = mesh.devices.shape
    finer = jax.sharding.Mesh(mesh.devices.reshape(leaf // 2, 2, columns), ("chip", "core", "tm"))
    whole = P(None, ("chip", "core", "tm"))
    first = P(("chip", "core", "tm"))
    return jax.shard_map(
        shards,
        mesh=finer,
        in_specs=(whole,) * 4 + (first,) * 7 + (P(), P()),
        out_specs=(whole, whole),
        check_vma=False,
    )
```

```python
import functools
import math

import jax
import jax.numpy as jnp
from jax import lax
from jax.experimental import pallas as pl
from jax.experimental.pallas import tpu as pltpu
from jax.sharding import PartitionSpec as P

F32 = jnp.float32
BF16 = jnp.bfloat16
EXACT = lax.Precision.HIGHEST
LN2 = math.log(2.0)
LOG2E = 1.0 / LN2
UNIT = math.sqrt(3.0) * LOG2E
FACTOR = -LN2 * math.e
VMEM = pl.BlockSpec(memory_space=pltpu.VMEM)
SMEM = pl.BlockSpec(memory_space=pltpu.SMEM)
ANY = pl.BlockSpec(memory_space=pl.ANY)
PART = 256
FIRST_PAIRS = 10


def params(mib, **kw):
    return pltpu.CompilerParams(vmem_limit_bytes=mib * 2**20, **kw)


def contract(a, b, dims, precision=None):
    return lax.dot_general(
        a, b, ((dims[0], dims[1]), ((), ())), precision=precision, preferred_element_type=F32
    )


def rounded(x):
    return x.astype(BF16).astype(F32)


def row_ids(shape):
    return lax.broadcasted_iota(jnp.int32, shape, 0)


def lane_ids(shape):
    return lax.broadcasted_iota(jnp.int32, shape, 1)


def features(xx, want_source, want_target):
    row = row_ids(xx.shape)
    high = rounded(xx)
    low = rounded(xx - high)
    held = high + low
    square = held * held
    square = square + pltpu.roll(square, 1, 0)
    norm = square + pltpu.roll(square, 2, 0)
    n0 = rounded(norm)
    rest = norm - n0
    n1 = rounded(rest)
    n2 = rest - n1
    zero = jnp.zeros_like(xx)
    out = []
    if want_source:
        parts = jnp.where(row < 4, high, low)
        tail = jnp.where(row == 0, n0, jnp.where(row == 1, n1, jnp.where(row == 2, n2, jnp.where(row < 6, 1.0, 0.0))))
        out.append(jnp.concatenate([parts, parts, tail, zero], axis=0).astype(BF16))
    if want_target:
        tail = jnp.where(row < 3, 1.0, jnp.where(row == 3, n0, jnp.where(row == 4, n1, jnp.where(row == 5, n2, 0.0))))
        out.append(jnp.concatenate([-2.0 * high, -2.0 * low, tail, zero], axis=0).astype(BF16))
    return out


def halves(w):
    high = rounded(w)
    return jnp.concatenate([high, w - high], axis=0).astype(BF16)


def kernel_of(z):
    z = jnp.maximum(z, 1e-30)
    q = -LOG2E - z * lax.rsqrt(z)
    return q * jnp.exp2(q)


def split(k):
    high = k.astype(BF16)
    return high, (k - high.astype(F32)).astype(BF16)


def gather_lanes(chunks, ids):
    lane = ids & 127
    chunk = ids >> 7
    picked = [None] * len(chunks)
    for s in range(len(chunks[0])):
        here = chunk == s
        for i, source in enumerate(chunks):
            got = jnp.take_along_axis(source[s](), lane, axis=1, mode="promise_in_bounds")
            picked[i] = got if s == 0 else jnp.where(here, got, picked[i])
    return picked


def scale_rows(scale_ref, shape):
    row = row_ids(shape) & 3
    picked = jnp.where(row == 0, scale_ref[0], jnp.where(row == 1, scale_ref[1], jnp.where(row == 2, scale_ref[2], scale_ref[3])))
    return picked * UNIT


def gather_body(scale_hbm, order_hbm, x_hbm, p_hbm, bases_hbm, halo_ref, scale_ref, order_ref, xx, p_ref, bases_ref, sems):
    leaf_dev, rank, leaf_pts = bases_ref.shape
    points = p_ref.shape[1]
    chunks = points // 128
    per_leaf = leaf_pts // 128
    moves = [
        pltpu.make_async_copy(source, target, sems.at[i])
        for i, (source, target) in enumerate(
            [
                (order_hbm, order_ref),
                (x_hbm, xx.at[0:4, :]),
                (x_hbm, xx.at[4:8, :]),
                (p_hbm, p_ref),
                (scale_hbm, scale_ref),
                (bases_hbm, bases_ref),
            ]
        )
    ]
    for move in moves:
        move.start()
    for move in moves[:5]:
        move.wait()
    scale = scale_rows(scale_ref, (8, 128))

    def loads(ref):
        return [lambda s=s: ref[:, s * 128 : (s + 1) * 128] for s in range(chunks)]

    def two_leaves(g, _):
        kept = []
        for h in range(2):
            leaf = 2 * g + h
            for j in range(per_leaf):
                ids = order_ref[pl.ds(leaf * per_leaf + j, 1), :]
                got_x, got_p = gather_lanes([loads(xx), loads(p_ref)], jnp.broadcast_to(ids, (8, 128)))
                kept.append(got_x * scale)
                halo_ref[pl.ds(pl.multiple_of(32 + leaf * 8, 8), 8), j * 128 : (j + 1) * 128] = got_p
        for j in range(per_leaf):
            both = jnp.where(row_ids((8, 128)) < 4, kept[j], kept[per_leaf + j])
            halo_ref[pl.ds(pl.multiple_of(g * 8, 8), 8), j * 128 : (j + 1) * 128] = both
        return 0

    lax.fori_loop(0, leaf_dev // 2, two_leaves, 0)
    moves[5].wait()
    for leaf in range(leaf_dev):
        coef = contract(halo_ref[32 + leaf * 8 : 40 + leaf * 8, :], bases_ref[leaf], ((1,), (1,)), EXACT)
        halo_ref[96:104, leaf * rank : (leaf + 1) * rank] = coef


def node_work(order_ref, halo_ref, transfer_ref, skel_ref, node_ref, own_ref, inv_ref, slot):
    chunks = order_ref.shape[0]
    rank = transfer_ref.shape[0]
    leaf_dev = halo_ref.shape[0] // 13
    upper = row_ids((8, 128)) < 4
    for g in range(leaf_dev // 2):
        both = halo_ref[g * 8 : g * 8 + 8, 0:128]
        turned = pltpu.roll(both, 4, 0)
        slot[:, 2 * g * rank : (2 * g + 1) * rank] = jnp.where(upper, both, turned)[:, :rank]
        slot[:, (2 * g + 1) * rank : (2 * g + 2) * rank] = jnp.where(upper, turned, both)[:, :rank]
    weights = contract(halo_ref[96:104, :], transfer_ref[...], ((1,), (1,)), EXACT)
    slots = [lambda s=s: slot[:, s * 128 : (s + 1) * 128] for s in range(leaf_dev * rank // 128)]
    ids = jnp.concatenate([skel_ref[...], skel_ref[...]], axis=1)
    (node_x,) = gather_lanes([slots], jnp.broadcast_to(ids, (8, 128)))
    tile = jnp.concatenate([weights, node_x[:, :rank]], axis=1)
    own_ref[...] = tile
    node_ref[...] = jnp.broadcast_to(tile[None], node_ref.shape)
    tally = jnp.zeros((2 * chunks, 128), F32)
    for c in range(chunks):
        ids = order_ref[c : c + 1, :]
        low = jnp.where(row_ids((128, 128)) == (ids & 127), 1.0, 0.0).astype(BF16)
        row = row_ids((chunks, 128)) == (ids >> 7)
        lane = lane_ids((chunks, 128))
        digit1 = jnp.where(row, (2 * c + (lane >> 6)).astype(F32), 0.0)
        digit0 = jnp.where(row, (lane & 63).astype(F32), 0.0)
        digits = jnp.concatenate([digit1, digit0], axis=0).astype(BF16)
        tally = tally + contract(digits, low, ((1,), (1,)))
    inv_ref[...] = (64.0 * tally[0:chunks] + tally[chunks : 2 * chunks] + 0.5).astype(jnp.int32)


def prepare(ref, base, src, wgt, tgt=None, coef=None):
    leaf_dev = ref.shape[0] // 13
    row = row_ids((8, ref.shape[1]))
    for g in range(leaf_dev // 2):
        both = ref[g * 8 : g * 8 + 8, :]
        turned = pltpu.roll(both, 4, 0)
        for h in range(2):
            leaf = 2 * g + h
            xx = jnp.where(row < 4, both, turned) if h == 0 else jnp.where(row < 4, turned, both)
            made = features(xx, True, tgt is not None)
            src[base + leaf] = made[0]
            if tgt is not None:
                tgt[leaf] = made[1]
            wgt[base + leaf] = halves(ref[32 + leaf * 8 : 40 + leaf * 8, :] * FACTOR)
            if coef is not None:
                rank = coef.shape[2]
                coef[base + leaf] = halves(ref[96:104, leaf * rank : (leaf + 1) * rank] * FACTOR)


def list_pairs(near_ref, count_ref, inside, outside, sizes):
    leaf_dev, slots = near_ref.shape

    def leaf_step(leaf, sums):
        def entry(j, sums):
            w = near_ref[leaf, j]
            here = jnp.where((w // leaf_dev == 4) & (sums[0] < FIRST_PAIRS), 1, 0)
            code = leaf * 128 + w
            inside[sums[0]] = code
            outside[sums[1]] = code
            return sums[0] + here, sums[1] + 1 - here

        return lax.fori_loop(0, count_ref[leaf], entry, sums)

    sums = lax.fori_loop(0, leaf_dev, leaf_step, (0, 0))
    idle = 9 * leaf_dev
    for extra in range(3):
        inside[sums[0] + extra] = idle
        outside[sums[1] + extra] = idle
    sizes[0], sizes[1] = sums
    return sums[0]


def near_pairs(pairs, n, first, src, tgt, wgt, out, z, high, low):
    parts = wgt.shape[2] // PART

    def where(p):
        return pairs[p] >> 7, (pairs[p] & 127) - first

    def distances(p, c, b):
        leaf, w = where(p)
        z[b] = contract(src[w, :, c * PART : (c + 1) * PART], tgt[leaf], ((0,), (0,)))

    def values(b):
        high[b], low[b] = split(kernel_of(z[b]))

    def product(p, c, b):
        _, w = where(p)
        weight = wgt[w, :, c * PART : (c + 1) * PART]
        got = jnp.dot(weight, high[b], preferred_element_type=F32)
        return got + jnp.dot(weight, low[b], preferred_element_type=F32)

    distances(0, 0, 0)
    distances(0, 1, 1)
    values(0)

    def two_pairs(g, _):
        for h in range(2):
            p = 2 * g + h
            got = None
            for c in range(parts):
                b = c % 2
                values(1 - b)
                mine = product(p, c, b)
                got = mine if got is None else got + mine
                distances(p + (c + 2) // parts, (c + 2) % parts, b)
            leaf, _ = where(p)
            out[leaf] += got[:8] + got[8:]
        return 0

    lax.fori_loop(0, (n + 1) // 2, two_pairs, 0)


def inside_body(near_ref, count_ref, halo_hbm, order_ref, transfer_ref, skel_ref, out_ref, node_ref, own_ref, inv_ref, pairs_ref, sizes_ref, pairs, halo_ref, slot, src, tgt, wgt, z, high, low, sem):
    leaf_dev, rhs, leaf_pts = out_ref.shape
    move = pltpu.make_async_copy(halo_hbm, halo_ref, sem)
    move.start()
    n = list_pairs(near_ref, count_ref, pairs, pairs_ref, sizes_ref)
    for extra in range(3):
        pairs[n + extra] = 5 * leaf_dev
    src[leaf_dev] = jnp.zeros(src.shape[1:], BF16)
    wgt[leaf_dev] = jnp.zeros(wgt.shape[1:], BF16)
    out_ref[...] = jnp.zeros_like(out_ref)
    move.wait()
    node_work(order_ref, halo_ref, transfer_ref, skel_ref, node_ref, own_ref, inv_ref, slot)
    prepare(halo_ref, 0, src, wgt, tgt)
    near_pairs(pairs, n, 4 * leaf_dev, src, tgt, wgt, out_ref, z, high, low)


def node_field(tm_size, place_ref, node_ref, own_ref, transfer_ref, node_src, node_wgt):
    devices = node_ref.shape[0]
    rank = own_ref.shape[1] // 2
    lane = lane_ids((8, 128))

    def distant(leaf, column):
        far_a = jnp.abs(leaf - place_ref[0]) > 1
        far_b = jnp.abs(column - place_ref[1]) > 1
        return jnp.where(far_a | far_b, FACTOR, 0.0)

    group = 2 * tm_size

    def unpack(g, _):
        xs, ws = [], []
        for j in range(0, group, 2):
            one, two = node_ref[group * g + j], node_ref[group * g + j + 1]
            keep_one = distant(2 * g + j // tm_size, j % tm_size)
            keep_two = distant(2 * g + (j + 1) // tm_size, (j + 1) % tm_size)
            xs.append(jnp.where(lane < rank, pltpu.roll(one, rank, 1), two))
            ws.append(jnp.where(lane < rank, one * keep_one, pltpu.roll(two, rank, 1) * keep_two))
        at = pl.ds(pl.multiple_of(g * group * rank, group * rank), group * rank)
        node_src[:, at] = features(jnp.concatenate(xs, axis=1), True, False)[0]
        node_wgt[:, at] = halves(jnp.concatenate(ws, axis=1))
        return 0

    lax.fori_loop(0, devices // group, unpack, 0, unroll=4)
    own_xx = pltpu.roll(own_ref[...], rank, 1)
    target = features(own_xx, False, True)[0][:, :rank]
    total = jnp.zeros((16, rank), F32)
    step = 512
    for q in range(0, devices * rank, step):
        z_far = contract(target, node_src[:, q : q + step], ((0,), (0,)))
        k_high, k_low = split(kernel_of(z_far))
        weight = node_wgt[:, q : q + step]
        total = total + contract(weight, k_high, ((1,), (1,)))
        total = total + contract(weight, k_low, ((1,), (1,)))
    return jnp.dot(total[:8] + total[8:], transfer_ref[...], precision=EXACT, preferred_element_type=F32)


def outside_body(pairs_ref, sizes_ref, far_ref, row_ref, up_ref, down_ref, out_ref, far_out_ref, src, tgt, wgt, coef, far_src, far_wgt, z, high, low):
    leaf_dev, rhs, leaf_pts = out_ref.shape
    rank = coef.shape[2]
    idle = 9 * leaf_dev
    src[idle] = jnp.zeros(src.shape[1:], BF16)
    wgt[idle] = jnp.zeros(wgt.shape[1:], BF16)
    for k in range(3):
        prepare(up_ref.at[k], k * leaf_dev, src, wgt, None, coef)
        prepare(row_ref.at[k], (3 + k) * leaf_dev, src, wgt, tgt if k == 1 else None, coef)
        prepare(down_ref.at[k], (6 + k) * leaf_dev, src, wgt, None, coef)
    out_ref[...] = jnp.zeros_like(out_ref)
    near_pairs(pairs_ref, sizes_ref[1], 0, src, tgt, wgt, out_ref, z, high, low)
    for leaf in range(leaf_dev):
        for j in range(far_ref.shape[1]):
            w = far_ref[leaf, j]
            at = slice(j * rank, (j + 1) * rank)
            far_src[leaf, :, at] = src[w, :, 0:rank]
            far_wgt[leaf, :, at] = coef[w]
    for leaf in range(leaf_dev):
        k_high, k_low = split(kernel_of(contract(tgt[leaf, :, 0:rank], far_src[leaf], ((0,), (0,)))))
        far = contract(far_wgt[leaf], k_high, ((1,), (1,))) + contract(far_wgt[leaf], k_low, ((1,), (1,)))
        far_out_ref[leaf] = far[:8] + far[8:]


def tail_body(tm_size, place_ref, noise_ref, inside_ref, near_ref, far_ref, node_ref, own_ref, transfer_ref, bases_ref, inv_ref, p_ref, res_ref, image_ref, sums_ref, flat, node_src, node_wgt):
    leaf_dev, rank, leaf_pts = bases_ref.shape
    pushed = node_field(tm_size, place_ref, node_ref, own_ref, transfer_ref, node_src, node_wgt)
    for leaf in range(leaf_dev):
        incoming = halves(far_ref[leaf] + pushed[:, leaf * rank : (leaf + 1) * rank])
        base_high, base_low = split(bases_ref[leaf])
        got = jnp.dot(incoming, base_high, preferred_element_type=F32)
        got = got + jnp.dot(incoming, base_low, preferred_element_type=F32)
        flat[:, leaf * leaf_pts : (leaf + 1) * leaf_pts] = inside_ref[leaf] + near_ref[leaf] + got[:8] + got[8:]

    chunks = flat.shape[1] // 128
    row = row_ids((8, 128))
    lane = lane_ids((8, 128))
    source = [lambda s=s: flat[:, s * 128 : (s + 1) * 128] for s in range(chunks)]
    noise = jnp.zeros((8, 128), F32)
    for r in range(8):
        noise = jnp.where(row == r, noise_ref[r], noise)

    def place(g, sums):
        along, squares = sums
        for h in range(4):
            c = 4 * g + h
            at = pl.ds(pl.multiple_of(c * 128, 128), 128)
            ids = jnp.broadcast_to(inv_ref[pl.ds(c, 1), :], (8, 128))
            (part,) = gather_lanes([source], ids)
            image = part + noise * p_ref[:, at]
            image_ref[:, at] = image
            along, squares = along + res_ref[:, at] * image, squares + image * image
        return along, squares

    zero = jnp.zeros((8, 128), F32)
    along, squares = lax.fori_loop(0, chunks // 4, place, (zero, zero))
    along = jnp.sum(along, axis=1, keepdims=True)
    squares = jnp.sum(squares, axis=1, keepdims=True)
    both = jnp.where(lane == row, along, 0.0) + jnp.where(lane == row + 8, squares, 0.0)
    sums_ref[...] = jnp.broadcast_to(jnp.sum(both, axis=0, keepdims=True), sums_ref.shape)


def update_body(sums_ref, it_ref, p_ref, res_ref, image_ref, new_it_ref, new_res_ref):
    total = jnp.sum(sums_ref[...], axis=0, keepdims=True)
    row = row_ids((8, 128))
    lane = lane_ids((8, 128))
    along = jnp.sum(jnp.where(lane == row, total, 0.0), axis=1, keepdims=True)
    squares = jnp.sum(jnp.where(lane == row + 8, total, 0.0), axis=1, keepdims=True)
    alpha = along / (squares + 1e-06)
    new_it_ref[...] = it_ref[...] + alpha * p_ref[...]
    new_res_ref[...] = res_ref[...] - alpha * image_ref[...]


def shifted(x, axis, by):
    n = lax.axis_size(axis)
    return lax.ppermute(x, axis, [(i, i + by) for i in range(n) if 0 <= i + by < n])


def shards(coords, direction, iterate, residual, order, bases, transfer, near_list, near_count, far_list, device_skel, inv_scale, noise):
    leaf_dev, rank, leaf_pts = bases.shape
    rhs, points = direction.shape
    axes = ("leaf", "tm")
    devices = lax.axis_size("leaf") * lax.axis_size("tm")
    chunks = points // 128
    shape = jax.ShapeDtypeStruct
    by_row = order.reshape(chunks, 128)
    halo = pl.pallas_call(
        gather_body,
        in_specs=[ANY] * 5,
        out_specs=VMEM,
        out_shape=shape((13 * leaf_dev, leaf_pts), F32),
        scratch_shapes=[
            pltpu.SMEM(inv_scale.shape, F32),
            pltpu.VMEM((chunks, 128), jnp.int32),
            pltpu.VMEM((8, points), F32),
            pltpu.VMEM((rhs, points), F32),
            pltpu.VMEM(bases.shape, F32),
            pltpu.SemaphoreType.DMA((6,)),
        ],
        compiler_params=params(60),
        name="gather",
    )(inv_scale, by_row, coords, direction, bases)
    left = shifted(halo, "tm", 1)
    right = shifted(halo, "tm", -1)

    def pipeline(sources):
        return [
            pltpu.VMEM((sources + 1, 32, leaf_pts), BF16),
            pltpu.VMEM((leaf_dev, 32, leaf_pts), BF16),
            pltpu.VMEM((sources + 1, 16, leaf_pts), BF16),
        ]

    buffers = [
        pltpu.VMEM((2, PART, leaf_pts), F32),
        pltpu.VMEM((2, PART, leaf_pts), BF16),
        pltpu.VMEM((2, PART, leaf_pts), BF16),
    ]
    entries = near_list.size + 4
    inside, node, own, inverse, pairs, sizes = pl.pallas_call(
        inside_body,
        in_specs=[SMEM] * 2 + [ANY] + [VMEM] * 3,
        out_specs=[VMEM] * 4 + [SMEM] * 2,
        out_shape=[
            shape((leaf_dev, rhs, leaf_pts), F32),
            shape((devices, 8, 128), F32),
            shape((8, 128), F32),
            shape((chunks, 128), jnp.int32),
            shape((entries,), jnp.int32),
            shape((2,), jnp.int32),
        ],
        scratch_shapes=[
            pltpu.SMEM((entries,), jnp.int32),
            pltpu.VMEM(halo.shape, F32),
            pltpu.VMEM((8, leaf_dev * rank), F32),
        ]
        + pipeline(leaf_dev)
        + buffers
        + [pltpu.SemaphoreType.DMA(())],
        compiler_params=params(58),
        cost_estimate=pl.CostEstimate(flops=10**10, bytes_accessed=2**21, transcendentals=10**7),
        name="inside",
    )(near_list, near_count, halo, by_row, transfer[0], device_skel)
    left, right, inside, node = lax.optimization_barrier((left, right, inside, node))
    nodes = lax.all_to_all(node, axes, 0, 0)
    row = jnp.stack([left, halo, right])
    up = shifted(row, "leaf", 1)
    down = shifted(row, "leaf", -1)
    place = jnp.stack([lax.axis_index("leaf"), lax.axis_index("tm")]).astype(jnp.int32)

    near, far = pl.pallas_call(
        outside_body,
        in_specs=[SMEM] * 3 + [VMEM] * 3,
        out_specs=[VMEM] * 2,
        out_shape=[shape((leaf_dev, rhs, leaf_pts), F32), shape((leaf_dev, rhs, rank), F32)],
        scratch_shapes=pipeline(9 * leaf_dev)
        + [
            pltpu.VMEM((9 * leaf_dev, 16, rank), BF16),
            pltpu.VMEM((leaf_dev, 32, far_list.shape[1] * rank), BF16),
            pltpu.VMEM((leaf_dev, 16, far_list.shape[1] * rank), BF16),
        ]
        + buffers,
        compiler_params=params(14),
        cost_estimate=pl.CostEstimate(flops=3 * 10**10, bytes_accessed=2**21, transcendentals=3 * 10**7),
        name="outside",
    )(pairs, sizes, far_list, row, up, down)
    image, sums = pl.pallas_call(
        functools.partial(tail_body, lax.axis_size("tm")),
        in_specs=[SMEM] * 2 + [VMEM] * 10,
        out_specs=[VMEM] * 2,
        out_shape=[shape((rhs, points), F32), shape((devices, 128), F32)],
        scratch_shapes=[
            pltpu.VMEM((rhs, points), F32),
            pltpu.VMEM((32, devices * rank), BF16),
            pltpu.VMEM((16, devices * rank), BF16),
        ],
        compiler_params=params(10),
        name="tail",
    )(place, noise, inside, near, far, nodes, own, transfer[0], bases, inverse, direction, residual)
    all_sums = lax.all_to_all(sums, axes, 0, 0, tiled=True)
    return pl.pallas_call(
        update_body,
        in_specs=[VMEM] * 5,
        out_specs=[VMEM] * 2,
        out_shape=[shape((rhs, points), F32)] * 2,
        compiler_params=params(8),
        name="update",
    )(all_sums, iterate, direction, residual, image)


def solution(mesh):
    whole = P(None, ("leaf", "tm"))
    first = P(("leaf", "tm"))
    return jax.shard_map(
        shards,
        mesh=mesh,
        in_specs=(whole,) * 4 + (first,) * 7 + (P(), P()),
        out_specs=(whole, whole),
        check_vma=False,
    )
```

```python
import functools
import math

import jax
import jax.numpy as jnp
from jax import lax
from jax.experimental import pallas as pl
from jax.experimental.pallas import tpu as pltpu
from jax.sharding import PartitionSpec as P

F32 = jnp.float32
BF16 = jnp.bfloat16
EXACT = lax.Precision.HIGHEST
LN2 = math.log(2.0)
LOG2E = 1.0 / LN2
UNIT = math.sqrt(3.0) * LOG2E
FACTOR = -LN2 * math.e
VMEM = pl.BlockSpec(memory_space=pltpu.VMEM)
SMEM = pl.BlockSpec(memory_space=pltpu.SMEM)
ANY = pl.BlockSpec(memory_space=pl.ANY)
PART = 256
FIRST_PAIRS = 10


def params(mib, **kw):
    return pltpu.CompilerParams(vmem_limit_bytes=mib * 2**20, **kw)


def contract(a, b, dims, precision=None):
    return lax.dot_general(
        a, b, ((dims[0], dims[1]), ((), ())), precision=precision, preferred_element_type=F32
    )


def rounded(x):
    return x.astype(BF16).astype(F32)


def row_ids(shape):
    return lax.broadcasted_iota(jnp.int32, shape, 0)


def lane_ids(shape):
    return lax.broadcasted_iota(jnp.int32, shape, 1)


def features(xx, want_source, want_target):
    row = row_ids(xx.shape)
    high = rounded(xx)
    low = rounded(xx - high)
    held = high + low
    square = held * held
    square = square + pltpu.roll(square, 1, 0)
    norm = square + pltpu.roll(square, 2, 0)
    n0 = rounded(norm)
    rest = norm - n0
    n1 = rounded(rest)
    n2 = rest - n1
    zero = jnp.zeros_like(xx)
    out = []
    if want_source:
        parts = jnp.where(row < 4, high, low)
        tail = jnp.where(row == 0, n0, jnp.where(row == 1, n1, jnp.where(row == 2, n2, jnp.where(row < 6, 1.0, 0.0))))
        out.append(jnp.concatenate([parts, parts, tail, zero], axis=0).astype(BF16))
    if want_target:
        tail = jnp.where(row < 3, 1.0, jnp.where(row == 3, n0, jnp.where(row == 4, n1, jnp.where(row == 5, n2, 0.0))))
        out.append(jnp.concatenate([-2.0 * high, -2.0 * low, tail, zero], axis=0).astype(BF16))
    return out


def halves(w):
    high = rounded(w)
    return jnp.concatenate([high, w - high], axis=0).astype(BF16)


def kernel_of(z):
    z = jnp.maximum(z, 1e-30)
    q = -LOG2E - z * lax.rsqrt(z)
    return q * jnp.exp2(q)


def split(k):
    high = k.astype(BF16)
    return high, (k - high.astype(F32)).astype(BF16)


def gather_lanes(chunks, ids):
    lane = ids & 127
    chunk = ids >> 7
    picked = [None] * len(chunks)
    for s in range(len(chunks[0])):
        here = chunk == s
        for i, source in enumerate(chunks):
            got = jnp.take_along_axis(source[s](), lane, axis=1, mode="promise_in_bounds")
            picked[i] = got if s == 0 else jnp.where(here, got, picked[i])
    return picked


def scale_rows(scale_ref, shape):
    row = row_ids(shape) & 3
    picked = jnp.where(row == 0, scale_ref[0], jnp.where(row == 1, scale_ref[1], jnp.where(row == 2, scale_ref[2], scale_ref[3])))
    return picked * UNIT


def gather_body(scale_hbm, order_hbm, x_hbm, p_hbm, bases_hbm, halo_ref, scale_ref, order_ref, xx, p_ref, bases_ref, sems):
    leaf_dev, rank, leaf_pts = bases_ref.shape
    points = p_ref.shape[1]
    chunks = points // 128
    per_leaf = leaf_pts // 128
    moves = [
        pltpu.make_async_copy(source, target, sems.at[i])
        for i, (source, target) in enumerate(
            [
                (order_hbm, order_ref),
                (x_hbm, xx.at[0:4, :]),
                (x_hbm, xx.at[4:8, :]),
                (p_hbm, p_ref),
                (scale_hbm, scale_ref),
                (bases_hbm, bases_ref),
            ]
        )
    ]
    for move in moves:
        move.start()
    for move in moves[:5]:
        move.wait()
    scale = scale_rows(scale_ref, (8, 128))

    def loads(ref):
        return [lambda s=s: ref[:, s * 128 : (s + 1) * 128] for s in range(chunks)]

    def two_leaves(g, _):
        upper = row_ids((8, 128)) < 4
        for j in range(per_leaf):
            ids = []
            for h in range(2):
                leaf = 2 * g + h
                ids.append(jnp.broadcast_to(order_ref[pl.ds(leaf * per_leaf + j, 1), :], (8, 128)))
                (got_p,) = gather_lanes([loads(p_ref)], ids[h])
                halo_ref[pl.ds(pl.multiple_of(32 + leaf * 8, 8), 8), j * 128 : (j + 1) * 128] = got_p
            (got_x,) = gather_lanes([loads(xx)], jnp.where(upper, ids[0], ids[1]))
            halo_ref[pl.ds(pl.multiple_of(g * 8, 8), 8), j * 128 : (j + 1) * 128] = got_x * scale
        return 0

    lax.fori_loop(0, leaf_dev // 2, two_leaves, 0)
    moves[5].wait()
    for leaf in range(leaf_dev):
        weight = halves(halo_ref[32 + leaf * 8 : 40 + leaf * 8, :])
        base_high, base_low = split(bases_ref[leaf])
        got = contract(weight, base_high, ((1,), (1,))) + contract(weight, base_low, ((1,), (1,)))
        halo_ref[96:104, leaf * rank : (leaf + 1) * rank] = got[:8] + got[8:]


def node_work(order_ref, halo_ref, transfer_ref, skel_ref, node_ref, own_ref, inv_ref, slot):
    chunks = order_ref.shape[0]
    rank = transfer_ref.shape[0]
    leaf_dev = halo_ref.shape[0] // 13
    upper = row_ids((8, 128)) < 4
    for g in range(leaf_dev // 2):
        both = halo_ref[g * 8 : g * 8 + 8, 0:128]
        turned = pltpu.roll(both, 4, 0)
        slot[:, 2 * g * rank : (2 * g + 1) * rank] = jnp.where(upper, both, turned)[:, :rank]
        slot[:, (2 * g + 1) * rank : (2 * g + 2) * rank] = jnp.where(upper, turned, both)[:, :rank]
    weights = contract(halo_ref[96:104, :], transfer_ref[...], ((1,), (1,)), EXACT)
    slots = [lambda s=s: slot[:, s * 128 : (s + 1) * 128] for s in range(leaf_dev * rank // 128)]
    ids = jnp.concatenate([skel_ref[...], skel_ref[...]], axis=1)
    (node_x,) = gather_lanes([slots], jnp.broadcast_to(ids, (8, 128)))
    tile = jnp.concatenate([weights, node_x[:, :rank]], axis=1)
    own_ref[...] = tile
    node_ref[...] = jnp.broadcast_to(tile[None], node_ref.shape)
    tally = jnp.zeros((2 * chunks, 128), F32)
    for c in range(chunks):
        ids = order_ref[c : c + 1, :]
        low = jnp.where(row_ids((128, 128)) == (ids & 127), 1.0, 0.0).astype(BF16)
        row = row_ids((chunks, 128)) == (ids >> 7)
        lane = lane_ids((chunks, 128))
        digit1 = jnp.where(row, (2 * c + (lane >> 6)).astype(F32), 0.0)
        digit0 = jnp.where(row, (lane & 63).astype(F32), 0.0)
        digits = jnp.concatenate([digit1, digit0], axis=0).astype(BF16)
        tally = tally + contract(digits, low, ((1,), (1,)))
    inv_ref[...] = (64.0 * tally[0:chunks] + tally[chunks : 2 * chunks] + 0.5).astype(jnp.int32)


def prepare(ref, base, src, wgt, tgt=None, coef=None):
    leaf_dev = ref.shape[0] // 13
    row = row_ids((8, ref.shape[1]))
    for g in range(leaf_dev // 2):
        both = ref[g * 8 : g * 8 + 8, :]
        turned = pltpu.roll(both, 4, 0)
        for h in range(2):
            leaf = 2 * g + h
            xx = jnp.where(row < 4, both, turned) if h == 0 else jnp.where(row < 4, turned, both)
            made = features(xx, True, tgt is not None)
            src[base + leaf] = made[0]
            if tgt is not None:
                tgt[leaf] = made[1]
            wgt[base + leaf] = halves(ref[32 + leaf * 8 : 40 + leaf * 8, :] * FACTOR)
            if coef is not None:
                rank = coef.shape[2]
                coef[base + leaf] = halves(ref[96:104, leaf * rank : (leaf + 1) * rank] * FACTOR)


def list_pairs(near_ref, count_ref, inside, outside, sizes):
    leaf_dev, slots = near_ref.shape

    def leaf_step(leaf, sums):
        def entry(j, sums):
            w = near_ref[leaf, j]
            here = jnp.where((w // leaf_dev == 4) & (sums[0] < FIRST_PAIRS), 1, 0)
            code = leaf * 128 + w
            inside[sums[0]] = code
            outside[sums[1]] = code
            return sums[0] + here, sums[1] + 1 - here

        return lax.fori_loop(0, count_ref[leaf], entry, sums)

    sums = lax.fori_loop(0, leaf_dev, leaf_step, (0, 0))
    idle = 9 * leaf_dev
    for extra in range(3):
        inside[sums[0] + extra] = idle
        outside[sums[1] + extra] = idle
    sizes[0], sizes[1] = sums
    return sums[0]


def near_pairs(pairs, n, first, src, tgt, wgt, out, z, high, low):
    parts = wgt.shape[2] // PART

    def where(p):
        return pairs[p] >> 7, (pairs[p] & 127) - first

    def distances(p, c, b):
        leaf, w = where(p)
        z[b] = contract(src[w, :, c * PART : (c + 1) * PART], tgt[leaf], ((0,), (0,)))

    def values(b):
        high[b], low[b] = split(kernel_of(z[b]))

    def product(p, c, b):
        _, w = where(p)
        weight = wgt[w, :, c * PART : (c + 1) * PART]
        got = jnp.dot(weight, high[b], preferred_element_type=F32)
        return got + jnp.dot(weight, low[b], preferred_element_type=F32)

    distances(0, 0, 0)
    distances(0, 1, 1)
    values(0)

    def two_pairs(g, _):
        for h in range(2):
            p = 2 * g + h
            got = None
            for c in range(parts):
                b = c % 2
                values(1 - b)
                mine = product(p, c, b)
                got = mine if got is None else got + mine
                distances(p + (c + 2) // parts, (c + 2) % parts, b)
            leaf, _ = where(p)
            out[leaf] += got[:8] + got[8:]
        return 0

    lax.fori_loop(0, (n + 1) // 2, two_pairs, 0)


def inside_body(near_ref, count_ref, halo_hbm, order_ref, transfer_ref, skel_ref, out_ref, node_ref, own_ref, inv_ref, pairs_ref, sizes_ref, pairs, halo_ref, slot, src, tgt, wgt, z, high, low, sem):
    leaf_dev, rhs, leaf_pts = out_ref.shape
    move = pltpu.make_async_copy(halo_hbm, halo_ref, sem)
    move.start()
    n = list_pairs(near_ref, count_ref, pairs, pairs_ref, sizes_ref)
    for extra in range(3):
        pairs[n + extra] = 5 * leaf_dev
    src[leaf_dev] = jnp.zeros(src.shape[1:], BF16)
    wgt[leaf_dev] = jnp.zeros(wgt.shape[1:], BF16)
    out_ref[...] = jnp.zeros_like(out_ref)
    move.wait()
    node_work(order_ref, halo_ref, transfer_ref, skel_ref, node_ref, own_ref, inv_ref, slot)
    prepare(halo_ref, 0, src, wgt, tgt)
    near_pairs(pairs, n, 4 * leaf_dev, src, tgt, wgt, out_ref, z, high, low)


def node_field(tm_size, place_ref, node_ref, own_ref, transfer_ref, node_src, node_wgt):
    devices = node_ref.shape[0]
    rank = own_ref.shape[1] // 2
    lane = lane_ids((8, 128))

    def distant(leaf, column):
        far_a = jnp.abs(leaf - place_ref[0]) > 1
        far_b = jnp.abs(column - place_ref[1]) > 1
        return jnp.where(far_a | far_b, FACTOR, 0.0)

    group = 2 * tm_size

    def unpack(g, _):
        xs, ws = [], []
        for j in range(0, group, 2):
            one, two = node_ref[group * g + j], node_ref[group * g + j + 1]
            keep_one = distant(2 * g + j // tm_size, j % tm_size)
            keep_two = distant(2 * g + (j + 1) // tm_size, (j + 1) % tm_size)
            xs.append(jnp.where(lane < rank, pltpu.roll(one, rank, 1), two))
            ws.append(jnp.where(lane < rank, one * keep_one, pltpu.roll(two, rank, 1) * keep_two))
        at = pl.ds(pl.multiple_of(g * group * rank, group * rank), group * rank)
        node_src[:, at] = features(jnp.concatenate(xs, axis=1), True, False)[0]
        node_wgt[:, at] = halves(jnp.concatenate(ws, axis=1))
        return 0

    lax.fori_loop(0, devices // group, unpack, 0, unroll=4)
    own_xx = pltpu.roll(own_ref[...], rank, 1)
    target = features(own_xx, False, True)[0][:, :rank]
    total = jnp.zeros((16, rank), F32)
    step = 512
    for q in range(0, devices * rank, step):
        z_far = contract(target, node_src[:, q : q + step], ((0,), (0,)))
        k_high, k_low = split(kernel_of(z_far))
        weight = node_wgt[:, q : q + step]
        total = total + contract(weight, k_high, ((1,), (1,)))
        total = total + contract(weight, k_low, ((1,), (1,)))
    return jnp.dot(total[:8] + total[8:], transfer_ref[...], precision=EXACT, preferred_element_type=F32)


def outside_body(pairs_ref, sizes_ref, far_ref, row_ref, up_ref, down_ref, out_ref, far_out_ref, src, tgt, wgt, coef, far_src, far_wgt, z, high, low):
    leaf_dev, rhs, leaf_pts = out_ref.shape
    rank = coef.shape[2]
    idle = 9 * leaf_dev
    src[idle] = jnp.zeros(src.shape[1:], BF16)
    wgt[idle] = jnp.zeros(wgt.shape[1:], BF16)
    for k in range(3):
        prepare(up_ref.at[k], k * leaf_dev, src, wgt, None, coef)
        prepare(row_ref.at[k], (3 + k) * leaf_dev, src, wgt, tgt if k == 1 else None, coef)
        prepare(down_ref.at[k], (6 + k) * leaf_dev, src, wgt, None, coef)
    out_ref[...] = jnp.zeros_like(out_ref)
    near_pairs(pairs_ref, sizes_ref[1], 0, src, tgt, wgt, out_ref, z, high, low)
    for leaf in range(leaf_dev):
        for j in range(far_ref.shape[1]):
            w = far_ref[leaf, j]
            at = slice(j * rank, (j + 1) * rank)
            far_src[leaf, :, at] = src[w, :, 0:rank]
            far_wgt[leaf, :, at] = coef[w]
    for leaf in range(leaf_dev):
        k_high, k_low = split(kernel_of(contract(tgt[leaf, :, 0:rank], far_src[leaf], ((0,), (0,)))))
        far = contract(far_wgt[leaf], k_high, ((1,), (1,))) + contract(far_wgt[leaf], k_low, ((1,), (1,)))
        far_out_ref[leaf] = far[:8] + far[8:]


def tail_body(tm_size, place_ref, noise_ref, inside_ref, near_ref, far_ref, node_ref, own_ref, transfer_ref, bases_ref, inv_ref, p_ref, res_ref, image_ref, sums_ref, flat, node_src, node_wgt):
    leaf_dev, rank, leaf_pts = bases_ref.shape
    pushed = node_field(tm_size, place_ref, node_ref, own_ref, transfer_ref, node_src, node_wgt)
    for leaf in range(leaf_dev):
        incoming = halves(far_ref[leaf] + pushed[:, leaf * rank : (leaf + 1) * rank])
        base_high, base_low = split(bases_ref[leaf])
        got = jnp.dot(incoming, base_high, preferred_element_type=F32)
        got = got + jnp.dot(incoming, base_low, preferred_element_type=F32)
        flat[:, leaf * leaf_pts : (leaf + 1) * leaf_pts] = inside_ref[leaf] + near_ref[leaf] + got[:8] + got[8:]

    chunks = flat.shape[1] // 128
    row = row_ids((8, 128))
    lane = lane_ids((8, 128))
    source = [lambda s=s: flat[:, s * 128 : (s + 1) * 128] for s in range(chunks)]
    noise = jnp.zeros((8, 128), F32)
    for r in range(8):
        noise = jnp.where(row == r, noise_ref[r], noise)

    def place(g, sums):
        along, squares = sums
        for h in range(4):
            c = 4 * g + h
            at = pl.ds(pl.multiple_of(c * 128, 128), 128)
            ids = jnp.broadcast_to(inv_ref[pl.ds(c, 1), :], (8, 128))
            (part,) = gather_lanes([source], ids)
            image = part + noise * p_ref[:, at]
            image_ref[:, at] = image
            along, squares = along + res_ref[:, at] * image, squares + image * image
        return along, squares

    zero = jnp.zeros((8, 128), F32)
    along, squares = lax.fori_loop(0, chunks // 4, place, (zero, zero))
    along = jnp.sum(along, axis=1, keepdims=True)
    squares = jnp.sum(squares, axis=1, keepdims=True)
    both = jnp.where(lane == row, along, 0.0) + jnp.where(lane == row + 8, squares, 0.0)
    sums_ref[...] = jnp.broadcast_to(jnp.sum(both, axis=0, keepdims=True), sums_ref.shape)


def update_body(sums_ref, it_ref, p_ref, res_ref, image_ref, new_it_ref, new_res_ref):
    total = jnp.sum(sums_ref[...], axis=0, keepdims=True)
    row = row_ids((8, 128))
    lane = lane_ids((8, 128))
    along = jnp.sum(jnp.where(lane == row, total, 0.0), axis=1, keepdims=True)
    squares = jnp.sum(jnp.where(lane == row + 8, total, 0.0), axis=1, keepdims=True)
    alpha = along / (squares + 1e-06)
    new_it_ref[...] = it_ref[...] + alpha * p_ref[...]
    new_res_ref[...] = res_ref[...] - alpha * image_ref[...]


def shifted(x, axis, by):
    n = lax.axis_size(axis)
    return lax.ppermute(x, axis, [(i, i + by) for i in range(n) if 0 <= i + by < n])


def shards(coords, direction, iterate, residual, order, bases, transfer, near_list, near_count, far_list, device_skel, inv_scale, noise):
    leaf_dev, rank, leaf_pts = bases.shape
    rhs, points = direction.shape
    axes = ("leaf", "tm")
    devices = lax.axis_size("leaf") * lax.axis_size("tm")
    chunks = points // 128
    shape = jax.ShapeDtypeStruct
    by_row = order.reshape(chunks, 128)
    halo = pl.pallas_call(
        gather_body,
        in_specs=[ANY] * 5,
        out_specs=VMEM,
        out_shape=shape((13 * leaf_dev, leaf_pts), F32),
        scratch_shapes=[
            pltpu.SMEM(inv_scale.shape, F32),
            pltpu.VMEM((chunks, 128), jnp.int32),
            pltpu.VMEM((8, points), F32),
            pltpu.VMEM((rhs, points), F32),
            pltpu.VMEM(bases.shape, F32),
            pltpu.SemaphoreType.DMA((6,)),
        ],
        compiler_params=params(60),
        name="gather",
    )(inv_scale, by_row, coords, direction, bases)
    left = shifted(halo, "tm", 1)
    right = shifted(halo, "tm", -1)

    def pipeline(sources):
        return [
            pltpu.VMEM((sources + 1, 32, leaf_pts), BF16),
            pltpu.VMEM((leaf_dev, 32, leaf_pts), BF16),
            pltpu.VMEM((sources + 1, 16, leaf_pts), BF16),
        ]

    buffers = [
        pltpu.VMEM((2, PART, leaf_pts), F32),
        pltpu.VMEM((2, PART, leaf_pts), BF16),
        pltpu.VMEM((2, PART, leaf_pts), BF16),
    ]
    entries = near_list.size + 4
    inside, node, own, inverse, pairs, sizes = pl.pallas_call(
        inside_body,
        in_specs=[SMEM] * 2 + [ANY] + [VMEM] * 3,
        out_specs=[VMEM] * 4 + [SMEM] * 2,
        out_shape=[
            shape((leaf_dev, rhs, leaf_pts), F32),
            shape((devices, 8, 128), F32),
            shape((8, 128), F32),
            shape((chunks, 128), jnp.int32),
            shape((entries,), jnp.int32),
            shape((2,), jnp.int32),
        ],
        scratch_shapes=[
            pltpu.SMEM((entries,), jnp.int32),
            pltpu.VMEM(halo.shape, F32),
            pltpu.VMEM((8, leaf_dev * rank), F32),
        ]
        + pipeline(leaf_dev)
        + buffers
        + [pltpu.SemaphoreType.DMA(())],
        compiler_params=params(58),
        cost_estimate=pl.CostEstimate(flops=10**10, bytes_accessed=2**21, transcendentals=10**7),
        name="inside",
    )(near_list, near_count, halo, by_row, transfer[0], device_skel)
    left, right, inside, node = lax.optimization_barrier((left, right, inside, node))
    nodes = lax.all_to_all(node, axes, 0, 0)
    row = jnp.stack([left, halo, right])
    up = shifted(row, "leaf", 1)
    down = shifted(row, "leaf", -1)
    place = jnp.stack([lax.axis_index("leaf"), lax.axis_index("tm")]).astype(jnp.int32)

    near, far = pl.pallas_call(
        outside_body,
        in_specs=[SMEM] * 3 + [VMEM] * 3,
        out_specs=[VMEM] * 2,
        out_shape=[shape((leaf_dev, rhs, leaf_pts), F32), shape((leaf_dev, rhs, rank), F32)],
        scratch_shapes=pipeline(9 * leaf_dev)
        + [
            pltpu.VMEM((9 * leaf_dev, 16, rank), BF16),
            pltpu.VMEM((leaf_dev, 32, far_list.shape[1] * rank), BF16),
            pltpu.VMEM((leaf_dev, 16, far_list.shape[1] * rank), BF16),
        ]
        + buffers,
        compiler_params=params(14),
        cost_estimate=pl.CostEstimate(flops=3 * 10**10, bytes_accessed=2**21, transcendentals=3 * 10**7),
        name="outside",
    )(pairs, sizes, far_list, row, up, down)
    image, sums = pl.pallas_call(
        functools.partial(tail_body, lax.axis_size("tm")),
        in_specs=[SMEM] * 2 + [VMEM] * 10,
        out_specs=[VMEM] * 2,
        out_shape=[shape((rhs, points), F32), shape((devices, 128), F32)],
        scratch_shapes=[
            pltpu.VMEM((rhs, points), F32),
            pltpu.VMEM((32, devices * rank), BF16),
            pltpu.VMEM((16, devices * rank), BF16),
        ],
        compiler_params=params(10),
        name="tail",
    )(place, noise, inside, near, far, nodes, own, transfer[0], bases, inverse, direction, residual)
    all_sums = lax.all_to_all(sums, axes, 0, 0, tiled=True)
    return pl.pallas_call(
        update_body,
        in_specs=[VMEM] * 5,
        out_specs=[VMEM] * 2,
        out_shape=[shape((rhs, points), F32)] * 2,
        compiler_params=params(8),
        name="update",
    )(all_sums, iterate, direction, residual, image)


def solution(mesh):
    whole = P(None, ("leaf", "tm"))
    first = P(("leaf", "tm"))
    return jax.shard_map(
        shards,
        mesh=mesh,
        in_specs=(whole,) * 4 + (first,) * 7 + (P(), P()),
        out_specs=(whole, whole),
        check_vma=False,
    )
```
